256 devices in a mesh: dp: 128 (over y, z_lo, x, core), tensor: 2 (over z_hi).
Axes of the slice: x: 4, y: 4, z: 8 (z_hi: 2, z_lo: 4; z = z_hi * 4 + z_lo), core: 2. Of those that a mesh axis runs over, the one named last changes fastest.
Arguments:
- activations: bfloat16 [65536, 5120], P('dp'), may hold values from -60 to 60
- kv_cotangents: bfloat16 [65536, 8, 256], P('dp', 'tensor'), may hold values from -4 to 4
Outputs:
- combined_grad: float32 [5120, 8, 256], P('dp', 'tensor')
The draws below stay inside these ranges and needn't reach their ends.
All inputs are finite; a program needn't handle non-finite values.
Results may differ from the reference program's by a relative error of at most 0.0011.
Values may be sent and summed in bfloat16 or wider, within the bound.
A program may use at most 128 MiB of HBM per device.

```python
import math
import jax
import jax.numpy as jnp
from jax import lax

D = 5120
KV_HEADS = 8
HEAD = 128
TOK_DEV = 512
TOKENS = 65536
N_DP = 128


def shared_parts(key):
    key_acts, key_grads, key_feat, key_rowmix, key_headmix = jax.random.split(key, 5)
    base_acts = jax.random.truncated_normal(key_acts, -4.0, 4.0, (TOK_DEV, D), jnp.float32)
    base_grads = jax.random.truncated_normal(key_grads, -4.0, 4.0, (TOK_DEV, KV_HEADS, 2 * HEAD), jnp.float32)
    feature_scale = jnp.exp(jax.random.uniform(key_feat, (D,), jnp.float32, math.log(0.5), math.log(5.0)))
    block_mix = jax.random.uniform(key_rowmix, (D // 8,), jnp.float32, 0.05, 0.95)
    row_mix = jnp.repeat(block_mix, 8)
    pair_mix = jax.random.uniform(key_headmix, (KV_HEADS, 2, 1), jnp.float32, 0.05, 0.95)
    head_mix = jnp.broadcast_to(pair_mix, (KV_HEADS, 2, HEAD)).reshape(KV_HEADS, 2 * HEAD)
    return (base_acts, base_grads, feature_scale, row_mix, head_mix)


def rough_noise(key, shape):
    return jax.random.truncated_normal(key, -4.0, 4.0, shape, jnp.float32)


def draw_activations(key, part):
    base_acts, base_grads, feature_scale, row_mix, head_mix = shared_parts(key)
    key = jax.random.fold_in(key, 11)
    key_noise = jax.random.fold_in(key, 0)
    noise_part = rough_noise(key_noise, (N_DP, TOK_DEV, D))
    noise_mix = jnp.sqrt(1.0 - row_mix * row_mix)
    values = (row_mix * base_acts[None] + noise_mix * noise_part) * feature_scale
    return values.reshape(TOKENS, D).astype(jnp.bfloat16)


def draw_kv_cotangents(key, part):
    base_acts, base_grads, feature_scale, row_mix, head_mix = shared_parts(key)
    key = jax.random.fold_in(key, 23)
    key_noise = jax.random.fold_in(key, 0)
    noise_part = rough_noise(key_noise, (N_DP, TOK_DEV, KV_HEADS, 2 * HEAD))
    noise_mix = jnp.sqrt(1.0 - head_mix * head_mix)
    rising = 3.0 ** (jnp.arange(N_DP, dtype=jnp.float32) / max(N_DP - 1, 1))
    values = (head_mix * base_grads[None] + noise_mix * noise_part) * rising[:, None, None, None] * 0.0625
    return values.reshape(TOKENS, KV_HEADS, 2 * HEAD).astype(jnp.bfloat16)


def setup_inputs(seed: int = 0) -> dict:
    splits = jax.random.split(jax.random.key(seed), 3)
    return {
        "activations": draw_activations(jax.random.fold_in(splits[2], 71), 0),
        "kv_cotangents": draw_kv_cotangents(jax.random.fold_in(splits[2], 71), 0),
    }


epsilon = 1e-6


def replica_gradient(activations, kv_cotangents, replica):
    row_block = activations[replica * TOK_DEV:(replica + 1) * TOK_DEV].astype(jnp.float32)
    cot_block = kv_cotangents[replica * TOK_DEV:(replica + 1) * TOK_DEV].reshape(TOK_DEV, KV_HEADS * 2 * HEAD).astype(jnp.float32)
    gradient = lax.dot_general(row_block, cot_block, (((0,), (0,)), ((), ())), precision=lax.Precision.HIGHEST, preferred_element_type=jnp.float32)
    rounded = lax.optimization_barrier(gradient.astype(jnp.bfloat16))
    return rounded.astype(jnp.float32)


def adasum_pair(lower_vec, upper_vec):
    cross_sum = jnp.sum(lower_vec * upper_vec)
    lower_sq = jnp.sum(lower_vec * lower_vec)
    upper_sq = jnp.sum(upper_vec * upper_vec)
    lower_coef = 1.0 - cross_sum / (2.0 * lower_sq + epsilon)
    upper_coef = 1.0 - cross_sum / (2.0 * upper_sq + epsilon)
    return lower_coef * lower_vec + upper_coef * upper_vec


def adasum_range(activations, kv_cotangents, first, count):
    if count == 1:
        return replica_gradient(activations, kv_cotangents, first)
    half_count = count // 2
    lower_vec = adasum_range(activations, kv_cotangents, first, half_count)
    upper_vec = adasum_range(activations, kv_cotangents, first + half_count, half_count)
    return adasum_pair(lower_vec, upper_vec)


def reference(activations, kv_cotangents):
    combined = adasum_range(activations, kv_cotangents, 0, N_DP)
    return combined.reshape(D, KV_HEADS, 2 * HEAD)
```

```python
import functools

import jax
import jax.numpy as jnp
from jax import lax
from jax.experimental import pallas as pl
from jax.experimental.pallas import tpu as pltpu
from jax.sharding import PartitionSpec as P

MESH = pl.DeviceIdType.MESH
F32 = jnp.float32
BF16 = jnp.bfloat16
EPS = 1e-6
POWER = 9
TOP = 2.0**13
HALF = 2560
TILE = 640
BLOCK = 80
COLS = 1024


def coords(dp):
    return dp // 32, (dp // 8) % 4, (dp // 2) % 4, dp % 2


def rank(y, z, x, c):
    return ((y * 4 + z) * 4 + x) * 2 + c


def encode(v):
    v2 = v * v
    v4 = v2 * v2
    return (v4 * v4 * v).astype(BF16)


def decode(code):
    y = code.astype(F32)
    size = jnp.exp2(jnp.log2(jnp.abs(y)) * (1.0 / POWER))
    return jnp.where(y < 0, -size, size)


def iotas(rows):
    shape = (rows, 128)
    return (
        lax.broadcasted_iota(jnp.int32, shape, 0),
        lax.broadcasted_iota(jnp.int32, shape, 1),
    )


def partner_rows(gram, bit):
    rows = gram.shape[0]
    if bit == 8:
        return jnp.concatenate([gram[8:16], gram[0:8]], axis=0)
    parts = []
    for first in range(0, rows, 8):
        part = gram[first : first + 8]
        row = lax.broadcasted_iota(jnp.int32, part.shape, 0)
        parts.append(
            jnp.where((row & bit) == 0, pltpu.roll(part, 8 - bit, 0), pltpu.roll(part, bit, 0))
        )
    return parts[0] if len(parts) == 1 else jnp.concatenate(parts, axis=0)


def partner_lanes(gram, bit):
    lane = lax.broadcasted_iota(jnp.int32, gram.shape, 1)
    return jnp.where((lane & bit) == 0, pltpu.roll(gram, 128 - bit, 1), pltpu.roll(gram, bit, 1))


def solve(gram, count):
    rows = gram.shape[0]
    row, lane = iotas(rows)
    on_diag = row == lane
    first_diag = jnp.sum(jnp.where(on_diag, gram, 0.0), axis=1, keepdims=True)
    weight = jnp.ones((rows, 1), F32)
    bit = 1
    while bit < count:
        paired = (row ^ bit) == lane
        kept = jnp.where(on_diag, gram, 0.0)
        crossed = jnp.where(paired, gram, 0.0)
        col = 1.0 - jnp.sum(crossed, axis=1, keepdims=True) / (
            2.0 * jnp.sum(kept, axis=1, keepdims=True) + EPS
        )
        across = 1.0 - jnp.sum(crossed, axis=0, keepdims=True) / (
            2.0 * jnp.sum(kept, axis=0, keepdims=True) + EPS
        )
        weight = weight * col
        gram = gram * col * across
        if bit * 2 < count:
            gram = gram + partner_rows(gram, bit)
            gram = gram + partner_lanes(gram, bit)
        bit *= 2
    bound = float(count) * jnp.sum(weight * weight * first_diag, axis=0, keepdims=True) + 1e-36
    return weight, bound


def scalars(column, count):
    row = lax.broadcasted_iota(jnp.int32, column.shape, 0)
    return [jnp.sum(jnp.where(row == i, column, 0.0)) for i in range(count)]


def kernel(
    a_hbm, k_hbm, o_ref,
    a_own, a_oth, k_own, k_oth, a_t, grads, enc_x, recv_x, dec_x, enc_y, recv_y, recv_z, dec_z,
    rows_s, msg, slots0, slots1, slots2, slots3,
    load_sem, tok_send, tok_recv, x_send, x_recv, y_send, y_recv, z_send, z_recv, r_send, r_recv,
):
    me = lax.axis_index("dp")
    t = lax.axis_index("tensor")
    y, z, x, c = coords(me)
    row8, lane8 = iotas(8)

    def group16(k):
        return rank(y, z, (x + k // 4) % 4, (c + (k // 2) % 2) % 2), (t + k % 2) % 2

    def plane16(k):
        return rank((y + k // 4) % 4, (z + k % 4) % 4, x, c), t

    barrier = pltpu.get_barrier_semaphore()

    def greet_group(k, _):
        pl.semaphore_signal(barrier, inc=1, device_id=group16(k), device_id_type=MESH)
        return _

    def greet_plane(k, _):
        pl.semaphore_signal(barrier, inc=1, device_id=plane16(k), device_id_type=MESH)
        return _

    def greet_other(k, _):
        pl.semaphore_signal(
            barrier, inc=1, device_id=(rank((y + k) % 4, z, x, 1 - c), t), device_id_type=MESH
        )
        return _

    def a_cols(core, i):
        return pl.ds(pl.multiple_of(core * HALF + i * TILE, 128), TILE)

    load_k = pltpu.make_async_copy(k_hbm, k_own, load_sem.at[4])
    load_k.start()
    load_a = [
        pltpu.make_async_copy(a_hbm.at[:, a_cols(c, i)], a_own.at[i], load_sem.at[i])
        for i in range(4)
    ]
    for copy in load_a:
        copy.start()
    lax.fori_loop(1, 16, greet_group, 0)
    lax.fori_loop(1, 16, greet_plane, 0)
    lax.fori_loop(1, 4, greet_other, 0)

    def gradient_tile(a_ref, k_ref, which, i):
        a_t[...] = a_ref[i].T

        def columns(n, _):
            at = pl.ds(pl.multiple_of(n * 256, 256), 256)
            tile = jnp.dot(a_t[...], k_ref[:, at], preferred_element_type=F32)
            grads[which, pl.ds(i * 8, 8), :, at] = tile.astype(BF16).reshape(8, BLOCK, 256)
            return _

        lax.fori_loop(0, 4, columns, 0)

    load_k.wait()
    load_a[0].wait()
    gradient_tile(a_own, k_own, 0, 0)
    pl.semaphore_wait(barrier, 33)

    other = (rank(y, z, x, 1 - c), t)
    tok = [
        pltpu.make_async_remote_copy(
            k_hbm, k_oth, tok_send.at[4], tok_recv.at[4], device_id=other, device_id_type=MESH
        )
    ] + [
        pltpu.make_async_remote_copy(
            a_hbm.at[:, a_cols(1 - c, i)],
            a_oth.at[i],
            tok_send.at[i],
            tok_recv.at[i],
            device_id=other,
            device_id_type=MESH,
        )
        for i in range(4)
    ]
    for copy in tok:
        copy.start()
    for i in range(1, 4):
        load_a[i].wait()
        gradient_tile(a_own, k_own, 0, i)

    def pair_sums(block, sums):
        cross, own_sq, oth_sq = sums
        for r in range(0, BLOCK, 16):
            for l in range(0, COLS, 128):
                own = grads[0, block, r : r + 16, l : l + 128].astype(F32)
                oth = grads[1, block, r : r + 16, l : l + 128].astype(F32)
                p, q, s = own * oth, own * own, oth * oth
                cross = cross + (p[0:8] + p[8:16])
                own_sq = own_sq + (q[0:8] + q[8:16])
                oth_sq = oth_sq + (s[0:8] + s[8:16])
        return cross, own_sq, oth_sq

    zero = jnp.zeros((8, 128), F32)
    sums = (zero, zero, zero)
    tok[0].wait_recv()
    for i in range(4):
        tok[i + 1].wait_recv()
        gradient_tile(a_oth, k_oth, 1, i)
        sums = lax.fori_loop(8 * i, 8 * i + 8, pair_sums, sums)
    cross, own_sq, oth_sq = (jnp.sum(s) for s in sums)
    lower_sq = jnp.where(c == 0, own_sq, oth_sq)
    upper_sq = jnp.where(c == 0, oth_sq, own_sq)

    def entry(i, j):
        return (row8 == i) & (lane8 == j)

    def exchange(stage, slots, first, last, target):
        def go(k, _):
            pltpu.make_async_remote_copy(
                msg.at[stage],
                slots.at[k],
                r_send.at[stage, k],
                r_recv.at[stage, k],
                device_id=target(k),
                device_id_type=MESH,
            ).start()
            return _

        def arrive(k, total):
            pltpu.make_async_copy(slots.at[k], slots.at[k], r_recv.at[stage, k]).wait()
            return total + slots[k]

        lax.fori_loop(first, last, go, 0)
        return lax.fori_loop(first, last, arrive, msg[stage])

    def finish_exchange(stage, slots, first, last):
        def done(k, _):
            pltpu.make_async_copy(slots.at[k], slots.at[k], r_send.at[stage, k]).wait()
            return _

        lax.fori_loop(first, last, done, 0)

    msg[0] = (
        jnp.where(entry(0, 0), lower_sq, 0.0)
        + jnp.where(entry(1, 1), upper_sq, 0.0)
        + jnp.where(entry(0, 1) | entry(1, 0), cross, 0.0)
    )
    gram = exchange(0, slots0, 1, 4, group16)
    weight, bound = solve(gram, 2)
    scale = TOP * lax.rsqrt(bound)
    inverse1 = (1.0 / scale)
    w_low, w_up = scalars(weight * scale, 2)
    w_own = jnp.where(c == 0, w_low, w_up)
    w_oth = jnp.where(c == 0, w_up, w_low)

    def x_copy(d, b):
        return pltpu.make_async_remote_copy(
            enc_x.at[d - 1, b],
            recv_x.at[d - 1, b],
            x_send.at[d - 1, b],
            x_recv.at[d - 1, b],
            device_id=(rank(y, z, (x + d) % 4, c), t),
            device_id_type=MESH,
        )

    def x_send_block(b, _):
        for d in (2, 1, 3):
            block = b * 4 + (x + d) % 4
            for r in range(0, BLOCK, 16):
                for l in range(0, COLS, 256):
                    own = grads[0, block, r : r + 16, l : l + 256].astype(F32)
                    oth = grads[1, block, r : r + 16, l : l + 256].astype(F32)
                    enc_x[d - 1, b, r : r + 16, l : l + 256] = encode(w_own * own + w_oth * oth)
            x_copy(d, b).start()
        return _

    lax.fori_loop(0, 8, x_send_block, 0)

    def x_own_block(b, _):
        for r in range(0, BLOCK, 16):
            for l in range(0, COLS, 256):
                own = grads[0, b * 4 + x, r : r + 16, l : l + 256].astype(F32)
                oth = grads[1, b * 4 + x, r : r + 16, l : l + 256].astype(F32)
                dec_x[x, b, r : r + 16, l : l + 256] = w_own * own + w_oth * oth
        return _

    lax.fori_loop(0, 8, x_own_block, 0)
    pairs4 = [(i, j) for i in range(4) for j in range(i, 4)]

    def x_recv_block(b, sums):
        for d in (1, 3, 2):
            x_copy(d, b).wait_recv()
            source = (x + 4 - d) % 4
            for r in range(0, BLOCK, 16):
                for l in range(0, COLS, 256):
                    dec_x[source, b, r : r + 16, l : l + 256] = decode(
                        recv_x[d - 1, b, r : r + 16, l : l + 256]
                    )
        sums = list(sums)
        for r in range(0, BLOCK, 8):
            for l in range(0, COLS, 128):
                v = [dec_x[i, b, r : r + 8, l : l + 128] for i in range(4)]
                for n, (i, j) in enumerate(pairs4):
                    sums[n] = sums[n] + v[i] * v[j]
        return tuple(sums)

    sums = lax.fori_loop(0, 8, x_recv_block, (zero,) * 10)
    gram = jnp.where(entry(4, x), 0.25 * inverse1, 0.0)
    for (i, j), s in zip(pairs4, sums):
        gram = gram + jnp.where(entry(i, j) | entry(j, i), jnp.sum(s), 0.0)
    msg[1] = gram
    gram = exchange(1, slots1, 1, 16, group16)
    inv_row = jnp.where(lane8[0:1] < 4, gram[4:5], 0.0)
    inv_col = jnp.sum(jnp.where(row8 == lane8, inv_row, 0.0), axis=1, keepdims=True)
    gram = jnp.where((row8 < 4) & (lane8 < 4), gram, 0.0) * inv_row * inv_col
    weight, bound = solve(gram, 4)
    scale = TOP * lax.rsqrt(bound)
    inverse3 = (1.0 / scale)
    w_x = scalars(weight * inv_col * scale, 4)

    def y_stays(yy, half):
        py = 2 * c + yy
        return (py == y) & (half == c)

    def y_copy(yy, half, zt):
        return pltpu.make_async_remote_copy(
            enc_y.at[yy, half, zt],
            recv_y.at[y, zt],
            y_send.at[yy, half, zt],
            y_recv.at[y, zt],
            device_id=(rank(2 * c + yy, z, x, half), t),
            device_id_type=MESH,
        )

    def y_send_block(n, _):
        zt = (z + 1 + n // 2) % 4
        yy = n % 2
        b = yy * 4 + zt
        for half in range(2):
            for l in range(0, 512, 128):
                parts = []
                for first in (l, 512 + l):
                    v = [
                        dec_x[i, b, 40 * half : 40 * half + 40, first : first + 128] for i in range(4)
                    ]
                    parts.append((w_x[0] * v[0] + w_x[1] * v[1]) + (w_x[2] * v[2] + w_x[3] * v[3]))
                enc_y[yy, half, zt, :, l : l + 128] = encode(jnp.concatenate(parts, axis=0))
            here = y_stays(yy, half)

            @pl.when(here)
            def keep():
                pltpu.make_async_copy(
                    enc_y.at[yy, half, zt], recv_y.at[y, zt], y_recv.at[y, zt]
                ).start()

            @pl.when(jnp.logical_not(here))
            def push():
                y_copy(yy, half, zt).start()

        return _

    lax.fori_loop(0, 8, y_send_block, 0)

    def z_copy(d, sy):
        zt = (z + d) % 4
        return pltpu.make_async_remote_copy(
            recv_y.at[sy, zt],
            recv_z.at[z, sy],
            z_send.at[d - 1, sy],
            z_recv.at[z, sy],
            device_id=(rank(y, zt, x, c), t),
            device_id_type=MESH,
        )

    def y_arrival(sy, zt):
        pltpu.make_async_copy(recv_y.at[sy, zt], recv_y.at[sy, zt], y_recv.at[sy, zt]).wait()

    def z_relay(n, _):
        d = 1 + n // 4
        sy = n % 4
        y_arrival(sy, (z + d) % 4)
        z_copy(d, sy).start()
        return _

    lax.fori_loop(0, 12, z_relay, 0)

    def own_z(sy, _):
        y_arrival(sy, z)
        for r in range(0, BLOCK, 16):
            dec_z[sy * 4 + z, r : r + 16, :] = decode(recv_y[sy, z, r : r + 16, :])
        return _

    lax.fori_loop(0, 4, own_z, 0)

    def z_arrival(n, _):
        source = (z + 1 + n // 4) % 4
        sy = n % 4
        pltpu.make_async_copy(
            recv_z.at[source, sy], recv_z.at[source, sy], z_recv.at[source, sy]
        ).wait()
        for r in range(0, BLOCK, 16):
            dec_z[sy * 4 + source, r : r + 16, :] = decode(recv_z[source, sy, r : r + 16, :])
        return _

    lax.fori_loop(0, 12, z_arrival, 0)

    for bi in range(0, 16, 4):
        for bj in range(bi, 16, 4):
            pairs = [(i, j) for i in range(bi, bi + 4) for j in range(bj, bj + 4) if i <= j]

            def products(n, sums):
                r = pl.ds(pl.multiple_of(n * 8, 8), 8)
                sums = list(sums)
                for l in range(0, 512, 128):
                    v = {i: dec_z[i, r, l : l + 128] for i in {i for p in pairs for i in p}}
                    for m, (i, j) in enumerate(pairs):
                        sums[m] = sums[m] + v[i] * v[j]
                return tuple(sums)

            sums = lax.fori_loop(0, 10, products, (zero,) * len(pairs))
            for (i, j), s in zip(pairs, sums):
                line = jnp.sum(s, axis=0, keepdims=True)
                rows_s[i, j : j + 1, :] = line
                if i != j:
                    rows_s[j, i : i + 1, :] = line
    row16, lane16 = iotas(16)
    gram = jnp.zeros((16, 128), F32)
    for i in range(16):
        gram = gram + jnp.where(lane16 == i, jnp.sum(rows_s[i], axis=1, keepdims=True), 0.0)
    msg[2] = gram[0:8] + pltpu.roll(gram[8:16], 64, 1)
    partial = exchange(2, slots2, 1, 16, group16)
    msg[3] = partial + jnp.where(entry(0, 32 + 4 * y + z), inverse3, 0.0)
    total = exchange(3, slots3, 1, 16, plane16)
    inv_row = jnp.where(lane8[0:1] < 16, pltpu.roll(total, 96, 1)[0:1], 0.0)
    inv_col = jnp.sum(jnp.where(row16 == lane16, inv_row, 0.0), axis=1, keepdims=True)
    gram = jnp.concatenate([total, pltpu.roll(total, 64, 1)], axis=0)
    gram = jnp.where(lane16 < 16, gram, 0.0) * inv_row * inv_col
    weight, _ = solve(gram, 16)
    w_z = scalars(weight * inv_col, 16)
    for h in range(2):
        for r in range(0, 40, 8):
            for l in range(0, 512, 128):
                out = w_z[0] * dec_z[0, 40 * h + r : 40 * h + r + 8, l : l + 128]
                for i in range(1, 16):
                    out = out + w_z[i] * dec_z[i, 40 * h + r : 40 * h + r + 8, l : l + 128]
                o_ref[r : r + 8, 512 * h + l : 512 * h + l + 128] = out

    for copy in tok:
        copy.wait_send()

    def x_done(b, _):
        for d in (1, 2, 3):
            x_copy(d, b).wait_send()
        return _

    lax.fori_loop(0, 8, x_done, 0)

    def y_done(n, _):
        for half in range(2):

            @pl.when(jnp.logical_not(y_stays(n % 2, half)))
            def settle():
                y_copy(n % 2, half, n // 2).wait_send()

        return _

    lax.fori_loop(0, 8, y_done, 0)

    def z_done(n, _):
        z_copy(1 + n // 4, n % 4).wait_send()
        return _

    lax.fori_loop(0, 12, z_done, 0)
    finish_exchange(0, slots0, 1, 4)
    finish_exchange(1, slots1, 1, 16)
    finish_exchange(2, slots2, 1, 16)
    finish_exchange(3, slots3, 1, 16)


def body(activations, kv_cotangents):
    tokens = activations.shape[0]
    kv = kv_cotangents.reshape(tokens, COLS)
    dma = pltpu.SemaphoreType.DMA
    out = pl.pallas_call(
        kernel,
        out_shape=jax.ShapeDtypeStruct((40, COLS), F32),
        in_specs=[pl.BlockSpec(memory_space=pl.ANY)] * 2,
        out_specs=pl.BlockSpec(memory_space=pltpu.VMEM),
        scratch_shapes=[
            pltpu.VMEM((4, tokens, TILE), BF16),
            pltpu.VMEM((4, tokens, TILE), BF16),
            pltpu.VMEM((tokens, COLS), BF16),
            pltpu.VMEM((tokens, COLS), BF16),
            pltpu.VMEM((TILE, tokens), BF16),
            pltpu.VMEM((2, 32, BLOCK, COLS), BF16),
            pltpu.VMEM((3, 8, BLOCK, COLS), BF16),
            pltpu.VMEM((3, 8, BLOCK, COLS), BF16),
            pltpu.VMEM((4, 8, BLOCK, COLS), F32),
            pltpu.VMEM((2, 2, 4, BLOCK, 512), BF16),
            pltpu.VMEM((4, 4, BLOCK, 512), BF16),
            pltpu.VMEM((4, 4, BLOCK, 512), BF16),
            pltpu.VMEM((16, BLOCK, 512), F32),
            pltpu.VMEM((16, 16, 128), F32),
            pltpu.VMEM((4, 8, 128), F32),
            pltpu.VMEM((4, 8, 128), F32),
            pltpu.VMEM((16, 8, 128), F32),
            pltpu.VMEM((16, 8, 128), F32),
            pltpu.VMEM((16, 8, 128), F32),
            dma((5,)),
            dma((5,)),
            dma((5,)),
            dma((3, 8)),
            dma((3, 8)),
            dma((2, 2, 4)),
            dma((4, 4)),
            dma((3, 4)),
            dma((4, 4)),
            dma((4, 16)),
            dma((4, 16)),
        ],
        compiler_params=pltpu.CompilerParams(
            collective_id=0, has_side_effects=True, vmem_limit_bytes=58 * 2**20
        ),
    )(activations, kv)
    return out.reshape(40, kv_cotangents.shape[1], kv_cotangents.shape[2])


def solution(mesh):
    return jax.shard_map(
        body,
        mesh=mesh,
        in_specs=(P("dp", None), P("dp", "tensor", None)),
        out_specs=P("dp", "tensor", None),
        check_vma=False,
    )
```

```python
import functools

import jax
import jax.numpy as jnp
from jax import lax
from jax.experimental import pallas as pl
from jax.experimental.pallas import tpu as pltpu
from jax.sharding import PartitionSpec as P

MESH = pl.DeviceIdType.MESH
F32 = jnp.float32
BF16 = jnp.bfloat16
EPS = 1e-6
POWER = 9
TOP = 2.0**13
HALF = 2560
TILE = 640
BLOCK = 80
COLS = 1024


def coords(dp):
    return dp // 32, (dp // 8) % 4, (dp // 2) % 4, dp % 2


def rank(y, z, x, c):
    return ((y * 4 + z) * 4 + x) * 2 + c


def encode(v):
    v2 = v * v
    v4 = v2 * v2
    return (v4 * v4 * v).astype(BF16)


def decode(code):
    y = code.astype(F32)
    size = jnp.exp2(jnp.log2(jnp.abs(y)) * (1.0 / POWER))
    return jnp.where(y < 0, -size, size)


def iotas(rows):
    shape = (rows, 128)
    return (
        lax.broadcasted_iota(jnp.int32, shape, 0),
        lax.broadcasted_iota(jnp.int32, shape, 1),
    )


def partner_rows(gram, bit):
    rows = gram.shape[0]
    if bit == 8:
        return jnp.concatenate([gram[8:16], gram[0:8]], axis=0)
    parts = []
    for first in range(0, rows, 8):
        part = gram[first : first + 8]
        row = lax.broadcasted_iota(jnp.int32, part.shape, 0)
        parts.append(
            jnp.where((row & bit) == 0, pltpu.roll(part, 8 - bit, 0), pltpu.roll(part, bit, 0))
        )
    return parts[0] if len(parts) == 1 else jnp.concatenate(parts, axis=0)


def partner_lanes(gram, bit):
    lane = lax.broadcasted_iota(jnp.int32, gram.shape, 1)
    return jnp.where((lane & bit) == 0, pltpu.roll(gram, 128 - bit, 1), pltpu.roll(gram, bit, 1))


def solve(gram, count):
    rows = gram.shape[0]
    row, lane = iotas(rows)
    on_diag = row == lane
    weight = jnp.ones((rows, 1), F32)
    bit = 1
    while bit < count:
        paired = (row ^ bit) == lane
        kept = jnp.where(on_diag, gram, 0.0)
        crossed = jnp.where(paired, gram, 0.0)
        col = 1.0 - jnp.sum(crossed, axis=1, keepdims=True) / (
            2.0 * jnp.sum(kept, axis=1, keepdims=True) + EPS
        )
        across = 1.0 - jnp.sum(crossed, axis=0, keepdims=True) / (
            2.0 * jnp.sum(kept, axis=0, keepdims=True) + EPS
        )
        weight = weight * col
        gram = gram * col * across
        if bit * 2 < count:
            gram = gram + partner_rows(gram, bit)
            gram = gram + partner_lanes(gram, bit)
        bit *= 2
    return weight


def total(values):
    return jnp.sum(values, keepdims=True)


def wide(value, rows=16):
    return jnp.broadcast_to(value, (rows, 128))


def fold(values):
    rows, columns = values.shape
    parts = [
        values[r : r + 8, l : l + 128] for r in range(0, rows, 8) for l in range(0, columns, 128)
    ]
    while len(parts) > 1:
        odd = parts[len(parts) & ~1 :]
        parts = [p + q for p, q in zip(parts[0::2], parts[1::2])] + odd
    return parts[0]


def pair_weights(low_sq, up_sq, cross):
    return 1.0 - cross / (2.0 * low_sq + EPS), 1.0 - cross / (2.0 * up_sq + EPS)


def solve4(gram):
    c0, c1 = pair_weights(gram[0, 0], gram[1, 1], gram[0, 1])
    c2, c3 = pair_weights(gram[2, 2], gram[3, 3], gram[2, 3])
    low_sq = c0 * c0 * gram[0, 0] + 2.0 * c0 * c1 * gram[0, 1] + c1 * c1 * gram[1, 1]
    up_sq = c2 * c2 * gram[2, 2] + 2.0 * c2 * c3 * gram[2, 3] + c3 * c3 * gram[3, 3]
    cross = c0 * (c2 * gram[0, 2] + c3 * gram[0, 3]) + c1 * (c2 * gram[1, 2] + c3 * gram[1, 3])
    low, up = pair_weights(low_sq, up_sq, cross)
    weight = [c0 * low, c1 * low, c2 * up, c3 * up]
    bound = sum(weight[i] * weight[i] * gram[i, i] for i in range(4)) * 4.0 + 1e-36
    return weight, bound


def kernel(
    a_hbm, k_hbm, o_ref,
    a_own, a_oth, k_raw, k_own, k_oth, grads, enc_x, recv_x, dec_x, enc_y, recv_y, recv_z, dec_z,
    rows_s, msg, slots0, slots1, slots2, slots3,
    load_sem, tok_send, tok_recv, x_send, x_recv, y_send, y_recv, z_send, z_recv, r_send, r_recv,
):
    me = lax.axis_index("dp")
    t = lax.axis_index("tensor")
    y, z, x, c = coords(me)
    row8, lane8 = iotas(8)

    def group16(k):
        return rank(y, z, (x + k // 4) % 4, (c + (k // 2) % 2) % 2), (t + k % 2) % 2

    def plane16(k):
        return rank((y + k // 4) % 4, (z + k % 4) % 4, x, c), t

    barrier = pltpu.get_barrier_semaphore()

    def greet_group(k, _):
        pl.semaphore_signal(barrier, inc=1, device_id=group16(k), device_id_type=MESH)
        return _

    def greet_plane(k, _):
        pl.semaphore_signal(barrier, inc=1, device_id=plane16(k), device_id_type=MESH)
        return _

    def greet_other(k, _):
        pl.semaphore_signal(
            barrier, inc=1, device_id=(rank((y + k) % 4, z, x, 1 - c), t), device_id_type=MESH
        )
        return _

    def a_cols(core, i):
        return pl.ds(pl.multiple_of(core * HALF + i * TILE, 128), TILE)

    load_k = pltpu.make_async_copy(k_hbm, k_raw, load_sem.at[4])
    load_k.start()

    def load_a(i):
        return pltpu.make_async_copy(a_hbm.at[:, a_cols(c, i)], a_own.at[i], load_sem.at[i])

    def start_load(i, _):
        load_a(i).start()
        return _

    lax.fori_loop(0, 4, start_load, 0)
    lax.fori_loop(1, 16, greet_group, 0)
    lax.fori_loop(1, 16, greet_plane, 0)
    lax.fori_loop(1, 4, greet_other, 0)
    pl.semaphore_wait(barrier, 33)
    other = (rank(y, z, x, 1 - c), t)
    give_k = pltpu.make_async_remote_copy(
        k_own, k_oth, tok_send.at[4], tok_recv.at[4], device_id=other, device_id_type=MESH
    )

    def give_a(i):
        return pltpu.make_async_remote_copy(
            a_hbm.at[:, a_cols(1 - c, i)],
            a_oth.at[i],
            tok_send.at[i],
            tok_recv.at[i],
            device_id=other,
            device_id_type=MESH,
        )

    give_a(0).start()
    load_k.wait()

    def pack_k(n, _):
        r = pl.ds(pl.multiple_of(n * 32, 32), 32)
        k_own[r] = pltpu.einshape("thc->t(hc)", k_raw[r])
        return _

    lax.fori_loop(0, k_raw.shape[0] // 32, pack_k, 0)
    give_k.start()

    def start_give(i, _):
        give_a(i).start()
        return _

    lax.fori_loop(1, 4, start_give, 0)

    def gradient(a_ref, k_ref):
        return lax.dot_general(
            a_ref[...], k_ref[...], (((0,), (0,)), ((), ())), preferred_element_type=F32
        ).astype(BF16)

    def own_tile(i, own_sq):
        load_a(i).wait()
        tile = gradient(a_own.at[i], k_own)
        grads[0, pl.ds(i * 8, 8)] = tile.reshape(8, BLOCK, COLS)
        tile = tile.astype(F32)
        return own_sq + fold(tile * tile)

    zero = jnp.zeros((8, 128), F32)
    own_sq = lax.fori_loop(0, 4, own_tile, zero)
    give_k.wait_recv()

    def other_tile(i, sums):
        cross, oth_sq = sums
        give_a(i).wait_recv()
        tile = gradient(a_oth.at[i], k_oth)
        grads[1, pl.ds(i * 8, 8)] = tile.reshape(8, BLOCK, COLS)
        tile = tile.astype(F32)
        own = grads[0, pl.ds(i * 8, 8)].astype(F32).reshape(TILE, COLS)
        return cross + fold(own * tile), oth_sq + fold(tile * tile)

    cross, oth_sq = lax.fori_loop(0, 4, other_tile, (zero, zero))
    own_sq, oth_sq, cross = total(own_sq), total(oth_sq), total(cross)
    lower_sq = jnp.where(c == 0, own_sq, oth_sq)
    upper_sq = jnp.where(c == 0, oth_sq, own_sq)

    def entry(i, j):
        return (row8 == i) & (lane8 == j)

    def exchange(stage, slots, first, last, target):
        def go(k, _):
            pltpu.make_async_remote_copy(
                msg.at[stage],
                slots.at[k],
                r_send.at[stage, k],
                r_recv.at[stage, k],
                device_id=target(k),
                device_id_type=MESH,
            ).start()
            return _

        def arrive(k, table):
            pltpu.make_async_copy(slots.at[k], slots.at[k], r_recv.at[stage, k]).wait()
            return table + slots[k]

        lax.fori_loop(first, last, go, 0)
        return lax.fori_loop(first, last, arrive, msg[stage])

    def finish_exchange(stage, slots, first, last):
        def done(k, _):
            pltpu.make_async_copy(slots.at[k], slots.at[k], r_send.at[stage, k]).wait()
            return _

        lax.fori_loop(first, last, done, 0)

    msg[0] = (
        jnp.where(entry(0, 0), lower_sq, 0.0)
        + jnp.where(entry(1, 1), upper_sq, 0.0)
        + jnp.where(entry(0, 1) | entry(1, 0), cross, 0.0)
    )
    gram = exchange(0, slots0, 1, 4, group16)

    def pick(table, i, j):
        return total(jnp.where(entry(i, j), table, 0.0))

    lower_sq, upper_sq, cross = pick(gram, 0, 0), pick(gram, 1, 1), pick(gram, 0, 1)
    w_low, w_up = pair_weights(lower_sq, upper_sq, cross)
    bound = 2.0 * (w_low * w_low * lower_sq + w_up * w_up * upper_sq) + 1e-36
    scale = TOP * lax.rsqrt(bound)
    inverse1 = 1.0 / scale
    w_own = wide(scale * jnp.where(c == 0, w_low, w_up))
    w_oth = wide(scale * jnp.where(c == 0, w_up, w_low))

    def pair_of(block, r, l):
        own = grads[0, block, r : r + 16, l : l + 128].astype(F32)
        oth = grads[1, block, r : r + 16, l : l + 128].astype(F32)
        return w_own * own + w_oth * oth

    def x_copy(d, b):
        return pltpu.make_async_remote_copy(
            enc_x.at[d - 1, b],
            recv_x.at[d - 1, b],
            x_send.at[d - 1, b],
            x_recv.at[d - 1, b],
            device_id=(rank(y, z, (x + d) % 4, c), t),
            device_id_type=MESH,
        )

    def x_send_block(b, _):
        for d in (2, 1, 3):
            block = b * 4 + (x + d) % 4
            for r in range(0, BLOCK, 16):
                for l in range(0, COLS, 128):
                    enc_x[d - 1, b, r : r + 16, l : l + 128] = encode(pair_of(block, r, l))
            x_copy(d, b).start()
        return _

    lax.fori_loop(0, 8, x_send_block, 0)

    def x_own_block(b, _):
        for r in range(0, BLOCK, 16):
            for l in range(0, COLS, 128):
                dec_x[x, b, r : r + 16, l : l + 128] = pair_of(b * 4 + x, r, l)
        return _

    lax.fori_loop(0, 8, x_own_block, 0)
    pairs4 = [(i, j) for i in range(4) for j in range(i, 4)]

    def x_recv_block(b, sums):
        for d in (1, 3, 2):
            x_copy(d, b).wait_recv()
            source = (x + 4 - d) % 4
            for r in range(0, BLOCK, 16):
                for l in range(0, COLS, 256):
                    dec_x[source, b, r : r + 16, l : l + 256] = decode(
                        recv_x[d - 1, b, r : r + 16, l : l + 256]
                    )
        sums = list(sums)
        for r in range(0, BLOCK, 8):
            for l in range(0, COLS, 128):
                v = [dec_x[i, b, r : r + 8, l : l + 128] for i in range(4)]
                for n, (i, j) in enumerate(pairs4):
                    sums[n] = sums[n] + v[i] * v[j]
        return tuple(sums)

    sums = lax.fori_loop(0, 8, x_recv_block, (zero,) * 10)
    table = jnp.where(entry(4, x), 0.25 * inverse1, 0.0)
    for (i, j), s in zip(pairs4, sums):
        table = table + jnp.where(entry(i, j), total(s), 0.0)
    msg[1] = table
    table = exchange(1, slots1, 1, 16, group16)
    inv = [pick(table, 4, i) for i in range(4)]
    weight, bound = solve4({(i, j): pick(table, i, j) * inv[i] * inv[j] for i, j in pairs4})
    scale = TOP * lax.rsqrt(bound)
    inverse3 = 1.0 / scale
    w_x = [wide(weight[i] * inv[i] * scale, 40) for i in range(4)]

    def y_stays(yy, half):
        py = 2 * c + yy
        return (py == y) & (half == c)

    def y_copy(yy, half, zt):
        return pltpu.make_async_remote_copy(
            enc_y.at[yy, half, zt],
            recv_y.at[y, zt],
            y_send.at[yy, half, zt],
            y_recv.at[y, zt],
            device_id=(rank(2 * c + yy, z, x, half), t),
            device_id_type=MESH,
        )

    def y_send_block(n, _):
        zt = (z + 1 + n // 2) % 4
        yy = n % 2
        b = yy * 4 + zt
        for half in range(2):
            for l in range(0, 512, 128):
                parts = []
                for first in (l, 512 + l):
                    v = [
                        dec_x[i, b, 40 * half : 40 * half + 40, first : first + 128] for i in range(4)
                    ]
                    parts.append((w_x[0] * v[0] + w_x[1] * v[1]) + (w_x[2] * v[2] + w_x[3] * v[3]))
                enc_y[yy, half, zt, :, l : l + 128] = encode(jnp.concatenate(parts, axis=0))
            here = y_stays(yy, half)

            @pl.when(here)
            def keep():
                pltpu.make_async_copy(
                    enc_y.at[yy, half, zt], recv_y.at[y, zt], y_recv.at[y, zt]
                ).start()

            @pl.when(jnp.logical_not(here))
            def push():
                y_copy(yy, half, zt).start()

        return _

    lax.fori_loop(0, 8, y_send_block, 0)

    def z_copy(d, sy):
        zt = (z + d) % 4
        return pltpu.make_async_remote_copy(
            recv_y.at[sy, zt],
            recv_z.at[z, sy],
            z_send.at[d - 1, sy],
            z_recv.at[z, sy],
            device_id=(rank(y, zt, x, c), t),
            device_id_type=MESH,
        )

    def y_arrival(sy, zt):
        pltpu.make_async_copy(recv_y.at[sy, zt], recv_y.at[sy, zt], y_recv.at[sy, zt]).wait()

    def z_relay(n, _):
        d = 1 + n // 4
        sy = n % 4
        y_arrival(sy, (z + d) % 4)
        z_copy(d, sy).start()
        return _

    lax.fori_loop(0, 12, z_relay, 0)

    def own_z(sy, _):
        y_arrival(sy, z)
        for r in range(0, BLOCK, 16):
            dec_z[sy * 4 + z, r : r + 16, :] = decode(recv_y[sy, z, r : r + 16, :])
        return _

    lax.fori_loop(0, 4, own_z, 0)

    def z_arrival(n, _):
        source = (z + 1 + n // 4) % 4
        sy = n % 4
        pltpu.make_async_copy(
            recv_z.at[source, sy], recv_z.at[source, sy], z_recv.at[source, sy]
        ).wait()
        for r in range(0, BLOCK, 16):
            dec_z[sy * 4 + source, r : r + 16, :] = decode(recv_z[source, sy, r : r + 16, :])
        return _

    lax.fori_loop(0, 12, z_arrival, 0)

    for bi in range(0, 16, 4):
        for bj in range(bi, 16, 4):
            pairs = [(i, j) for i in range(bi, bi + 4) for j in range(bj, bj + 4) if i <= j]

            def products(n, sums):
                r = pl.ds(pl.multiple_of(n * 8, 8), 8)
                sums = list(sums)
                for l in range(0, 512, 128):
                    v = {i: dec_z[i, r, l : l + 128] for i in {i for p in pairs for i in p}}
                    for m, (i, j) in enumerate(pairs):
                        sums[m] = sums[m] + v[i] * v[j]
                return tuple(sums)

            sums = lax.fori_loop(0, 10, products, (zero,) * len(pairs))
            for (i, j), s in zip(pairs, sums):
                line = jnp.sum(s, axis=0, keepdims=True)
                rows_s[i, j : j + 1, :] = line
                if i != j:
                    rows_s[j, i : i + 1, :] = line
    row16, lane16 = iotas(16)
    gram = jnp.zeros((16, 128), F32)
    for i in range(16):
        gram = gram + jnp.where(lane16 == i, jnp.sum(rows_s[i], axis=1, keepdims=True), 0.0)
    msg[2] = gram[0:8] + pltpu.roll(gram[8:16], 64, 1)
    partial = exchange(2, slots2, 1, 16, group16)
    msg[3] = partial + jnp.where(entry(0, 32 + 4 * y + z), inverse3, 0.0)
    table = exchange(3, slots3, 1, 16, plane16)
    inv_row = jnp.where(lane8[0:1] < 16, pltpu.roll(table, 96, 1)[0:1], 0.0)
    inv_col = jnp.sum(jnp.where(row16 == lane16, inv_row, 0.0), axis=1, keepdims=True)
    gram = jnp.concatenate([table, pltpu.roll(table, 64, 1)], axis=0)
    gram = jnp.where(lane16 < 16, gram, 0.0) * inv_row * inv_col
    weight = solve(gram, 16) * inv_col
    w_z = [wide(weight[i : i + 1], 8) for i in range(16)]
    for h in range(2):
        for r in range(0, 40, 8):
            for l in range(0, 512, 128):
                out = w_z[0] * dec_z[0, 40 * h + r : 40 * h + r + 8, l : l + 128]
                for i in range(1, 16):
                    out = out + w_z[i] * dec_z[i, 40 * h + r : 40 * h + r + 8, l : l + 128]
                o_ref[r : r + 8, 512 * h + l : 512 * h + l + 128] = out

    give_k.wait_send()

    def given(i, _):
        give_a(i).wait_send()
        return _

    lax.fori_loop(0, 4, given, 0)

    def x_done(b, _):
        for d in (1, 2, 3):
            x_copy(d, b).wait_send()
        return _

    lax.fori_loop(0, 8, x_done, 0)

    def y_done(n, _):
        for half in range(2):

            @pl.when(jnp.logical_not(y_stays(n % 2, half)))
            def settle():
                y_copy(n % 2, half, n // 2).wait_send()

        return _

    lax.fori_loop(0, 8, y_done, 0)

    def z_done(n, _):
        z_copy(1 + n // 4, n % 4).wait_send()
        return _

    lax.fori_loop(0, 12, z_done, 0)
    finish_exchange(0, slots0, 1, 4)
    finish_exchange(1, slots1, 1, 16)
    finish_exchange(2, slots2, 1, 16)
    finish_exchange(3, slots3, 1, 16)


def body(activations, kv_cotangents):
    tokens = activations.shape[0]
    dma = pltpu.SemaphoreType.DMA
    out = pl.pallas_call(
        kernel,
        out_shape=jax.ShapeDtypeStruct((40, COLS), F32),
        in_specs=[pl.BlockSpec(memory_space=pl.ANY)] * 2,
        out_specs=pl.BlockSpec(memory_space=pltpu.VMEM),
        scratch_shapes=[
            pltpu.VMEM((4, tokens, TILE), BF16),
            pltpu.VMEM((4, tokens, TILE), BF16),
            pltpu.VMEM(kv_cotangents.shape, BF16),
            pltpu.VMEM((tokens, COLS), BF16),
            pltpu.VMEM((tokens, COLS), BF16),
            pltpu.VMEM((2, 32, BLOCK, COLS), BF16),
            pltpu.VMEM((3, 8, BLOCK, COLS), BF16),
            pltpu.VMEM((3, 8, BLOCK, COLS), BF16),
            pltpu.VMEM((4, 8, BLOCK, COLS), F32),
            pltpu.VMEM((2, 2, 4, BLOCK, 512), BF16),
            pltpu.VMEM((4, 4, BLOCK, 512), BF16),
            pltpu.VMEM((4, 4, BLOCK, 512), BF16),
            pltpu.VMEM((16, BLOCK, 512), F32),
            pltpu.VMEM((16, 16, 128), F32),
            pltpu.VMEM((4, 8, 128), F32),
            pltpu.VMEM((4, 8, 128), F32),
            pltpu.VMEM((16, 8, 128), F32),
            pltpu.VMEM((16, 8, 128), F32),
            pltpu.VMEM((16, 8, 128), F32),
            dma((5,)),
            dma((5,)),
            dma((5,)),
            dma((3, 8)),
            dma((3, 8)),
            dma((2, 2, 4)),
            dma((4, 4)),
            dma((3, 4)),
            dma((4, 4)),
            dma((4, 16)),
            dma((4, 16)),
        ],
        compiler_params=pltpu.CompilerParams(
            collective_id=0, has_side_effects=True, vmem_limit_bytes=58 * 2**20
        ),
    )(activations, kv_cotangents)
    return out.reshape(40, kv_cotangents.shape[1], kv_cotangents.shape[2])


def solution(mesh):
    return jax.shard_map(
        body,
        mesh=mesh,
        in_specs=(P("dp", None), P("dp", "tensor", None)),
        out_specs=P("dp", "tensor", None),
        check_vma=False,
    )
```

```python
import functools

import jax
import jax.numpy as jnp
from jax import lax
from jax.experimental import pallas as pl
from jax.experimental.pallas import tpu as pltpu
from jax.sharding import PartitionSpec as P

MESH = pl.DeviceIdType.MESH
F32 = jnp.float32
BF16 = jnp.bfloat16
EPS = 1e-6
POWER = 9
TOP = 2.0**13
HALF = 2560
TILE = 640
BLOCK = 80
COLS = 1024
PART = 512


def coords(dp):
    return dp // 32, (dp // 8) % 4, (dp // 2) % 4, dp % 2


def rank(y, z, x, c):
    return ((y * 4 + z) * 4 + x) * 2 + c


def encode(v):
    v2 = v * v
    v4 = v2 * v2
    return (v4 * v4 * v).astype(BF16)


def decode(code):
    y = code.astype(F32)
    size = jnp.exp2(jnp.log2(jnp.abs(y)) * (1.0 / POWER))
    return jnp.where(y < 0, -size, size)


def iotas(rows):
    shape = (rows, 128)
    return (
        lax.broadcasted_iota(jnp.int32, shape, 0),
        lax.broadcasted_iota(jnp.int32, shape, 1),
    )


def partner_rows(gram, bit):
    rows = gram.shape[0]
    if bit == 8:
        return jnp.concatenate([gram[8:16], gram[0:8]], axis=0)
    parts = []
    for first in range(0, rows, 8):
        part = gram[first : first + 8]
        row = lax.broadcasted_iota(jnp.int32, part.shape, 0)
        parts.append(
            jnp.where((row & bit) == 0, pltpu.roll(part, 8 - bit, 0), pltpu.roll(part, bit, 0))
        )
    return parts[0] if len(parts) == 1 else jnp.concatenate(parts, axis=0)


def partner_lanes(gram, bit):
    lane = lax.broadcasted_iota(jnp.int32, gram.shape, 1)
    return jnp.where((lane & bit) == 0, pltpu.roll(gram, 128 - bit, 1), pltpu.roll(gram, bit, 1))


def solve(gram, count):
    rows = gram.shape[0]
    row, lane = iotas(rows)
    on_diag = row == lane
    weight = jnp.ones((rows, 1), F32)
    bit = 1
    while bit < count:
        paired = (row ^ bit) == lane
        kept = jnp.where(on_diag, gram, 0.0)
        crossed = jnp.where(paired, gram, 0.0)
        col = 1.0 - jnp.sum(crossed, axis=1, keepdims=True) / (
            2.0 * jnp.sum(kept, axis=1, keepdims=True) + EPS
        )
        across = 1.0 - jnp.sum(crossed, axis=0, keepdims=True) / (
            2.0 * jnp.sum(kept, axis=0, keepdims=True) + EPS
        )
        weight = weight * col
        gram = gram * col * across
        if bit * 2 < count:
            gram = gram + partner_rows(gram, bit)
            gram = gram + partner_lanes(gram, bit)
        bit *= 2
    return weight


def total(values):
    return jnp.sum(values, keepdims=True)


def wide(value, rows=16):
    return jnp.broadcast_to(value, (rows, 128))


def fold(values):
    rows, columns = values.shape
    parts = [
        values[r : r + 8, l : l + 128] for r in range(0, rows, 8) for l in range(0, columns, 128)
    ]
    while len(parts) > 1:
        odd = parts[len(parts) & ~1 :]
        parts = [p + q for p, q in zip(parts[0::2], parts[1::2])] + odd
    return parts[0]


def pair_weights(low_sq, up_sq, cross):
    return 1.0 - cross / (2.0 * low_sq + EPS), 1.0 - cross / (2.0 * up_sq + EPS)


def solve4(gram):
    c0, c1 = pair_weights(gram[0, 0], gram[1, 1], gram[0, 1])
    c2, c3 = pair_weights(gram[2, 2], gram[3, 3], gram[2, 3])
    low_sq = c0 * c0 * gram[0, 0] + 2.0 * c0 * c1 * gram[0, 1] + c1 * c1 * gram[1, 1]
    up_sq = c2 * c2 * gram[2, 2] + 2.0 * c2 * c3 * gram[2, 3] + c3 * c3 * gram[3, 3]
    cross = c0 * (c2 * gram[0, 2] + c3 * gram[0, 3]) + c1 * (c2 * gram[1, 2] + c3 * gram[1, 3])
    low, up = pair_weights(low_sq, up_sq, cross)
    weight = [c0 * low, c1 * low, c2 * up, c3 * up]
    bound = sum(weight[i] * weight[i] * gram[i, i] for i in range(4)) * 4.0 + 1e-36
    return weight, bound


def kernel(
    a_hbm, k_hbm, o_ref,
    a_own, a_oth, k_raw, k_own, k_oth, grads, enc_x, recv_x, dec_x, enc_q, recv_q, recv_r, dec_q, sums_q,
    enc_y, recv_y, recv_z, enc_yq, recv_yq, dec_z,
    rows_s, msg, msg_q, slots0, slots1, slots2, slots3, slots_q, slots_w,
    load_sem, tok_send, tok_recv, x_send, x_recv, zq_send, zq_recv, xr_send, xr_recv,
    yq_send, yq_recv, y_send, y_recv, z_send, z_recv, r_send, r_recv, q_sems,
):
    me = lax.axis_index("dp")
    t = lax.axis_index("tensor")
    y, z, x, c = coords(me)
    row8, lane8 = iotas(8)

    def group16(k):
        return rank(y, z, (x + k // 4) % 4, (c + (k // 2) % 2) % 2), (t + k % 2) % 2

    def plane16(k):
        return rank((y + k // 4) % 4, (z + k % 4) % 4, x, c), t

    barrier = pltpu.get_barrier_semaphore()

    def greet_group(k, _):
        pl.semaphore_signal(barrier, inc=1, device_id=group16(k), device_id_type=MESH)
        return _

    def greet_plane(k, _):
        pl.semaphore_signal(barrier, inc=1, device_id=plane16(k), device_id_type=MESH)
        return _

    def greet_other(k, _):
        pl.semaphore_signal(
            barrier, inc=1, device_id=(rank((y + k) % 4, z, x, 1 - c), t), device_id_type=MESH
        )
        return _

    def a_cols(core, i):
        return pl.ds(pl.multiple_of(core * HALF + i * TILE, 128), TILE)

    load_k = pltpu.make_async_copy(k_hbm, k_raw, load_sem.at[4])
    load_k.start()

    def load_a(i):
        return pltpu.make_async_copy(a_hbm.at[:, a_cols(c, i)], a_own.at[i], load_sem.at[i])

    def start_load(i, _):
        load_a(i).start()
        return _

    lax.fori_loop(0, 4, start_load, 0)
    lax.fori_loop(1, 16, greet_group, 0)
    lax.fori_loop(1, 16, greet_plane, 0)
    lax.fori_loop(1, 4, greet_other, 0)
    pl.semaphore_wait(barrier, 33)
    other = (rank(y, z, x, 1 - c), t)
    give_k = pltpu.make_async_remote_copy(
        k_own, k_oth, tok_send.at[4], tok_recv.at[4], device_id=other, device_id_type=MESH
    )

    def give_a(i):
        return pltpu.make_async_remote_copy(
            a_hbm.at[:, a_cols(1 - c, i)],
            a_oth.at[i],
            tok_send.at[i],
            tok_recv.at[i],
            device_id=other,
            device_id_type=MESH,
        )

    give_a(0).start()
    load_k.wait()

    def pack_k(n, _):
        r = pl.ds(pl.multiple_of(n * 32, 32), 32)
        k_own[r] = pltpu.einshape("thc->t(hc)", k_raw[r])
        return _

    lax.fori_loop(0, k_raw.shape[0] // 32, pack_k, 0)
    give_k.start()

    def start_give(i, _):
        give_a(i).start()
        return _

    lax.fori_loop(1, 4, start_give, 0)

    def gradient(a_ref, k_ref):
        return lax.dot_general(
            a_ref[...], k_ref[...], (((0,), (0,)), ((), ())), preferred_element_type=F32
        ).astype(BF16)

    def own_tile(i, own_sq):
        load_a(i).wait()
        tile = gradient(a_own.at[i], k_own)
        grads[0, pl.ds(i * 8, 8)] = tile.reshape(8, BLOCK, COLS)
        tile = tile.astype(F32)
        return own_sq + fold(tile * tile)

    zero = jnp.zeros((8, 128), F32)
    own_sq = lax.fori_loop(0, 4, own_tile, zero)
    give_k.wait_recv()

    def other_tile(i, sums):
        cross, oth_sq = sums
        give_a(i).wait_recv()
        tile = gradient(a_oth.at[i], k_oth)
        grads[1, pl.ds(i * 8, 8)] = tile.reshape(8, BLOCK, COLS)
        tile = tile.astype(F32)
        own = grads[0, pl.ds(i * 8, 8)].astype(F32).reshape(TILE, COLS)
        return cross + fold(own * tile), oth_sq + fold(tile * tile)

    cross, oth_sq = lax.fori_loop(0, 4, other_tile, (zero, zero))
    own_sq, oth_sq, cross = total(own_sq), total(oth_sq), total(cross)
    lower_sq = jnp.where(c == 0, own_sq, oth_sq)
    upper_sq = jnp.where(c == 0, oth_sq, own_sq)

    def entry(i, j):
        return (row8 == i) & (lane8 == j)

    def exchange(stage, slots, first, last, target):
        def go(k, _):
            pltpu.make_async_remote_copy(
                msg.at[stage],
                slots.at[k],
                r_send.at[stage, k],
                r_recv.at[stage, k],
                device_id=target(k),
                device_id_type=MESH,
            ).start()
            return _

        def arrive(k, table):
            pltpu.make_async_copy(slots.at[k], slots.at[k], r_recv.at[stage, k]).wait()
            return table + slots[k]

        lax.fori_loop(first, last, go, 0)
        return lax.fori_loop(first, last, arrive, msg[stage])

    def finish_exchange(stage, slots, first, last):
        def done(k, _):
            pltpu.make_async_copy(slots.at[k], slots.at[k], r_send.at[stage, k]).wait()
            return _

        lax.fori_loop(first, last, done, 0)

    msg[0] = (
        jnp.where(entry(0, 0), lower_sq, 0.0)
        + jnp.where(entry(1, 1), upper_sq, 0.0)
        + jnp.where(entry(0, 1) | entry(1, 0), cross, 0.0)
    )
    gram = exchange(0, slots0, 1, 4, group16)

    def pick(table, i, j):
        return total(jnp.where(entry(i, j), table, 0.0))

    lower_sq, upper_sq, cross = pick(gram, 0, 0), pick(gram, 1, 1), pick(gram, 0, 1)
    w_low, w_up = pair_weights(lower_sq, upper_sq, cross)
    bound = 2.0 * (w_low * w_low * lower_sq + w_up * w_up * upper_sq) + 1e-36
    scale = TOP * lax.rsqrt(bound)
    inverse1 = 1.0 / scale
    w_own = wide(scale * jnp.where(c == 0, w_low, w_up))
    w_oth = wide(scale * jnp.where(c == 0, w_up, w_low))

    def pair_of(block, r, l):
        own = grads[0, block, r : r + 16, l : l + 128].astype(F32)
        oth = grads[1, block, r : r + 16, l : l + 128].astype(F32)
        return w_own * own + w_oth * oth

    def along_x(d):
        return rank(y, z, (x + d) % 4, c), t

    def along_z(d):
        return rank(y, (z + d) % 4, x, c), t

    def x_copy(d, b):
        return pltpu.make_async_remote_copy(
            enc_x.at[d - 1, b],
            recv_x.at[d - 1, b],
            x_send.at[d - 1, b],
            x_recv.at[d - 1, b],
            device_id=along_x(d),
            device_id_type=MESH,
        )

    def zq_copy(dz, yy, dx):
        return pltpu.make_async_remote_copy(
            enc_q.at[dz - 1, yy, dx],
            recv_q.at[dz, yy, dx],
            zq_send.at[dz - 1, yy * 4 + dx],
            zq_recv.at[dz - 1, yy * 4 + dx],
            device_id=along_z(dz),
            device_id_type=MESH,
        )

    def xr_copy(dx, dz, yy):
        return pltpu.make_async_remote_copy(
            recv_q.at[dz, yy, dx],
            recv_r.at[dx - 1, dz, yy],
            xr_send.at[dx - 1, dz * 2 + yy],
            xr_recv.at[dx - 1, dz * 2 + yy],
            device_id=along_x(dx),
            device_id_type=MESH,
        )

    def x_send_block(b):
        for d in (2, 1, 3):
            block = b * 4 + (x + d) % 4
            for r in range(0, BLOCK, 16):
                for l in range(0, PART, 128):
                    enc_x[d - 1, b, r : r + 16, l : l + 128] = encode(pair_of(block, r, l))
            x_copy(d, b).start()

    def q_send_block(yy, dx):
        for dz in (2, 1, 3, 0):
            block = yy * 16 + ((z + dz) % 4) * 4 + (x + dx) % 4
            for r in range(0, BLOCK, 16):
                for l in range(0, COLS - PART, 128):
                    code = encode(pair_of(block, r, PART + l))
                    if dz:
                        enc_q[dz - 1, yy, dx, r : r + 16, l : l + 128] = code
                    else:
                        recv_q[0, yy, dx, r : r + 16, l : l + 128] = code
            if dz:
                zq_copy(dz, yy, dx).start()

    def send_far(m, _):
        x_send_block(m)
        q_send_block(m, 2)
        return _

    def send_near(k, _):
        x_send_block(2 + k)
        q_send_block(k // 2, 1 + 2 * (k % 2))
        return _

    def send_own(m, _):
        x_send_block(6 + m)
        q_send_block(m, 0)
        return _

    lax.fori_loop(0, 2, send_far, 0)
    lax.fori_loop(0, 4, send_near, 0)
    lax.fori_loop(0, 2, send_own, 0)

    def x_own_block(b, _):
        for r in range(0, BLOCK, 16):
            for l in range(0, PART, 128):
                dec_x[x, b, r : r + 16, l : l + 128] = pair_of(b * 4 + x, r, l)
        return _

    lax.fori_loop(0, 8, x_own_block, 0)
    pairs4 = [(i, j) for i in range(4) for j in range(i, 4)]

    def x_recv_block(b, sums):
        for d in (1, 3, 2):
            x_copy(d, b).wait_recv()
            source = (x + 4 - d) % 4
            for r in range(0, BLOCK, 16):
                for l in range(0, PART, 256):
                    dec_x[source, b, r : r + 16, l : l + 256] = decode(
                        recv_x[d - 1, b, r : r + 16, l : l + 256]
                    )
        sums = list(sums)
        for r in range(0, BLOCK, 8):
            for l in range(0, PART, 128):
                v = [dec_x[i, b, r : r + 8, l : l + 128] for i in range(4)]
                for n, (i, j) in enumerate(pairs4):
                    sums[n] = sums[n] + v[i] * v[j]
        return tuple(sums)

    def relay(yy, dx):
        for dz in (0, 1, 3, 2):
            if dz:
                zq_copy(dz, yy, dx).wait_recv()
            xr_copy(dx, dz, yy).start()

    def relay_far(m, _):
        relay(m, 2)
        return _

    def relay_near(k, _):
        relay(k // 2, 1 + 2 * (k % 2))
        return _

    sums = lax.fori_loop(0, 4, x_recv_block, (zero,) * 10)
    lax.fori_loop(0, 2, relay_far, 0)
    sums = lax.fori_loop(4, 8, x_recv_block, sums)
    lax.fori_loop(0, 4, relay_near, 0)

    def q_decode(dx, yy):
        def one(dz, _):
            if dx:
                xr_copy(dx, dz, yy).wait_recv()
                source = recv_r.at[dx - 1, dz, yy]
            else:
                source = recv_q.at[dz, yy, 0]
            for r in range(0, BLOCK, 16):
                for l in range(0, COLS - PART, 256):
                    dec_q[dz, (x + 4 - dx) % 4, yy, r : r + 16, l : l + 256] = decode(
                        source[r : r + 16, l : l + 256]
                    )
            return _

        lax.fori_loop(0, 4, one, 0)

    def q_own(yy):
        for dz in (1, 2, 3):
            zq_copy(dz, yy, 0).wait_recv()
        q_decode(0, yy)

    def q_gram(yy):
        def one(dz, _):
            sums = [zero if yy == 0 else sums_q[dz, n] for n in range(10)]
            for r in range(0, BLOCK, 8):
                for l in range(0, COLS - PART, 128):
                    v = [dec_q[dz, i, yy, r : r + 8, l : l + 128] for i in range(4)]
                    for n, (i, j) in enumerate(pairs4):
                        sums[n] = sums[n] + v[i] * v[j]
            for n in range(10):
                sums_q[dz, n] = sums[n]
            return _

        lax.fori_loop(0, 4, one, 0)

    q_decode(2, 0)
    q_decode(2, 1)
    q_decode(1, 0)
    q_decode(3, 0)
    q_own(0)
    q_gram(0)
    q_decode(1, 1)
    q_decode(3, 1)
    q_own(1)
    q_gram(1)

    def q_copy(dz):
        return pltpu.make_async_remote_copy(
            msg_q.at[dz],
            slots_q.at[dz],
            q_sems.at[0, dz],
            q_sems.at[1, dz],
            device_id=along_z(4 - dz),
            device_id_type=MESH,
        )

    def tile_of(sums):
        table = jnp.zeros((8, 128), F32)
        for (i, j), s in zip(pairs4, sums):
            table = table + jnp.where(entry(i, j), total(s), 0.0)
        return table

    for dz in (2, 1, 3):
        msg_q[dz] = tile_of([sums_q[dz, n] for n in range(10)])
        q_copy(dz).start()
    table = jnp.where(entry(4, x), 0.25 * inverse1, 0.0)
    table = table + tile_of([s + sums_q[0, n] for n, s in enumerate(sums)])
    for dz in (1, 3, 2):
        q_copy(dz).wait_recv()
        table = table + slots_q[dz]
    msg[1] = table
    table = exchange(1, slots1, 1, 16, group16)
    inv = [pick(table, 4, i) for i in range(4)]
    weight, bound = solve4({(i, j): pick(table, i, j) * inv[i] * inv[j] for i, j in pairs4})
    scale = TOP * lax.rsqrt(bound)
    inverse3 = 1.0 / scale
    w_own_z = [weight[i] * inv[i] * scale for i in range(4)]

    def w_copy(dz):
        return pltpu.make_async_remote_copy(
            msg_q.at[0],
            slots_w.at[dz],
            q_sems.at[2, dz],
            q_sems.at[3, dz],
            device_id=along_z(dz),
            device_id_type=MESH,
        )

    table = jnp.zeros((8, 128), F32)
    for i in range(4):
        table = table + jnp.where(entry(0, i), w_own_z[i], 0.0)
    msg_q[0] = table
    for dz in (2, 1, 3):
        w_copy(dz).start()
    w_x = [wide(w_own_z[i], 40) for i in range(4)]

    def y_stays(yy, half):
        py = 2 * c + yy
        return (py == y) & (half == c)

    def y_copy(yy, half, zt):
        return pltpu.make_async_remote_copy(
            enc_y.at[yy, half, zt],
            recv_y.at[y, zt],
            y_send.at[yy, half, zt],
            y_recv.at[y, zt],
            device_id=(rank(2 * c + yy, z, x, half), t),
            device_id_type=MESH,
        )

    def combined(weights, block, half, l, width):
        parts = []
        for first in (l, width + l):
            rows, at = slice(40 * half, 40 * half + 40), slice(first, first + 128)
            v = [block(i, rows, at) for i in range(4)]
            parts.append(
                (weights[0] * v[0] + weights[1] * v[1]) + (weights[2] * v[2] + weights[3] * v[3])
            )
        return encode(jnp.concatenate(parts, axis=0))

    def y_send_block(n, _):
        zt = (z + 1 + n // 2) % 4
        yy = n % 2
        b = yy * 4 + zt
        for half in range(2):
            for l in range(0, PART // 2, 128):
                enc_y[yy, half, zt, :, l : l + 128] = combined(
                    w_x, lambda i, r, at: dec_x[i, b, r, at], half, l, PART // 2
                )
            here = y_stays(yy, half)

            @pl.when(here)
            def keep():
                pltpu.make_async_copy(
                    enc_y.at[yy, half, zt], recv_y.at[y, zt], y_recv.at[y, zt]
                ).start()

            @pl.when(jnp.logical_not(here))
            def push():
                y_copy(yy, half, zt).start()

        return _

    lax.fori_loop(0, 8, y_send_block, 0)

    def z_copy(d, sy):
        zt = (z + d) % 4
        return pltpu.make_async_remote_copy(
            recv_y.at[sy, zt],
            recv_z.at[z, sy],
            z_send.at[d - 1, sy],
            z_recv.at[z, sy],
            device_id=(rank(y, zt, x, c), t),
            device_id_type=MESH,
        )

    def y_arrival(sy, zt):
        pltpu.make_async_copy(recv_y.at[sy, zt], recv_y.at[sy, zt], y_recv.at[sy, zt]).wait()

    def z_relay(n, _):
        d = 1 + n // 4
        sy = n % 4
        y_arrival(sy, (z + d) % 4)
        z_copy(d, sy).start()
        return _

    lax.fori_loop(0, 12, z_relay, 0)

    def yq_copy(yy, half):
        return pltpu.make_async_remote_copy(
            enc_yq.at[yy, half],
            recv_yq.at[y],
            yq_send.at[yy, half],
            yq_recv.at[y],
            device_id=(rank(2 * c + yy, z, x, half), t),
            device_id_type=MESH,
        )

    w_by_z = []
    for dz in range(4):
        if dz:
            w_copy(dz).wait_recv()
            w_by_z.append([wide(pick(slots_w[dz], 0, i), 40) for i in range(4)])
        else:
            w_by_z.append(w_x)

    def yq_send_block(yy, _):
        for half in range(2):
            for dz in range(4):
                for l in range(0, (COLS - PART) // 2, 128):
                    enc_yq[yy, half, (z + 4 - dz) % 4, :, l : l + 128] = combined(
                        w_by_z[dz],
                        lambda i, r, at: dec_q[dz, i, yy, r, at],
                        half,
                        l,
                        (COLS - PART) // 2,
                    )
            here = y_stays(yy, half)

            @pl.when(here)
            def keep():
                pltpu.make_async_copy(enc_yq.at[yy, half], recv_yq.at[y], yq_recv.at[y]).start()

            @pl.when(jnp.logical_not(here))
            def push():
                yq_copy(yy, half).start()

        return _

    lax.fori_loop(0, 2, yq_send_block, 0)

    def own_z(sy, _):
        y_arrival(sy, z)
        for r in range(0, BLOCK, 16):
            dec_z[sy * 4 + z, r : r + 16, 0 : PART // 2] = decode(recv_y[sy, z, r : r + 16, :])
        return _

    lax.fori_loop(0, 4, own_z, 0)

    def yq_arrival(n, _):
        sy = (y + n) % 4
        pltpu.make_async_copy(recv_yq.at[sy], recv_yq.at[sy], yq_recv.at[sy]).wait()
        for sz in range(4):
            for r in range(0, BLOCK, 16):
                dec_z[sy * 4 + sz, r : r + 16, PART // 2 :] = decode(recv_yq[sy, sz, r : r + 16, :])
        return _

    lax.fori_loop(0, 4, yq_arrival, 0)

    def z_arrival(n, _):
        source = (z + 1 + n // 4) % 4
        sy = n % 4
        pltpu.make_async_copy(
            recv_z.at[source, sy], recv_z.at[source, sy], z_recv.at[source, sy]
        ).wait()
        for r in range(0, BLOCK, 16):
            dec_z[sy * 4 + source, r : r + 16, 0 : PART // 2] = decode(
                recv_z[source, sy, r : r + 16, :]
            )
        return _

    lax.fori_loop(0, 12, z_arrival, 0)

    for bi in range(0, 16, 4):
        for bj in range(bi, 16, 4):
            pairs = [(i, j) for i in range(bi, bi + 4) for j in range(bj, bj + 4) if i <= j]

            def products(n, sums):
                r = pl.ds(pl.multiple_of(n * 8, 8), 8)
                sums = list(sums)
                for l in range(0, 512, 128):
                    v = {i: dec_z[i, r, l : l + 128] for i in {i for p in pairs for i in p}}
                    for m, (i, j) in enumerate(pairs):
                        sums[m] = sums[m] + v[i] * v[j]
                return tuple(sums)

            sums = lax.fori_loop(0, 10, products, (zero,) * len(pairs))
            for (i, j), s in zip(pairs, sums):
                line = jnp.sum(s, axis=0, keepdims=True)
                rows_s[i, j : j + 1, :] = line
                if i != j:
                    rows_s[j, i : i + 1, :] = line
    row16, lane16 = iotas(16)
    gram = jnp.zeros((16, 128), F32)
    for i in range(16):
        gram = gram + jnp.where(lane16 == i, jnp.sum(rows_s[i], axis=1, keepdims=True), 0.0)
    msg[2] = gram[0:8] + pltpu.roll(gram[8:16], 64, 1)
    partial = exchange(2, slots2, 1, 16, group16)
    msg[3] = partial + jnp.where(entry(0, 32 + 4 * y + z), inverse3, 0.0)
    table = exchange(3, slots3, 1, 16, plane16)
    inv_row = jnp.where(lane8[0:1] < 16, pltpu.roll(table, 96, 1)[0:1], 0.0)
    inv_col = jnp.sum(jnp.where(row16 == lane16, inv_row, 0.0), axis=1, keepdims=True)
    gram = jnp.concatenate([table, pltpu.roll(table, 64, 1)], axis=0)
    gram = jnp.where(lane16 < 16, gram, 0.0) * inv_row * inv_col
    weight = solve(gram, 16) * inv_col
    w_z = [wide(weight[i : i + 1], 8) for i in range(16)]
    for first, width, at in ((0, PART // 2, 0), (PART, (COLS - PART) // 2, PART // 2)):
        for h in range(2):
            for r in range(0, 40, 8):
                for l in range(0, width, 128):
                    rows, lanes = slice(40 * h + r, 40 * h + r + 8), slice(at + l, at + l + 128)
                    terms = [w_z[i] * dec_z[i, rows, lanes] for i in range(16)]
                    while len(terms) > 1:
                        terms = [p + q for p, q in zip(terms[0::2], terms[1::2])]
                    column = first + h * width + l
                    o_ref[r : r + 8, column : column + 128] = terms[0]

    give_k.wait_send()

    def given(i, _):
        give_a(i).wait_send()
        return _

    lax.fori_loop(0, 4, given, 0)

    def x_done(b, _):
        for d in (1, 2, 3):
            x_copy(d, b).wait_send()
        return _

    lax.fori_loop(0, 8, x_done, 0)

    def zq_done(n, _):
        for dz in (1, 2, 3):
            zq_copy(dz, n // 4, n % 4).wait_send()
        return _

    lax.fori_loop(0, 8, zq_done, 0)

    def xr_done(n, _):
        for dx in (1, 2, 3):
            xr_copy(dx, n // 2, n % 2).wait_send()
        return _

    lax.fori_loop(0, 8, xr_done, 0)
    for dz in (1, 2, 3):
        q_copy(dz).wait_send()
        w_copy(dz).wait_send()

    def yq_done(yy, _):
        for half in range(2):

            @pl.when(jnp.logical_not(y_stays(yy, half)))
            def settle_q():
                yq_copy(yy, half).wait_send()

        return _

    lax.fori_loop(0, 2, yq_done, 0)

    def y_done(n, _):
        for half in range(2):

            @pl.when(jnp.logical_not(y_stays(n % 2, half)))
            def settle():
                y_copy(n % 2, half, n // 2).wait_send()

        return _

    lax.fori_loop(0, 8, y_done, 0)

    def z_done(n, _):
        z_copy(1 + n // 4, n % 4).wait_send()
        return _

    lax.fori_loop(0, 12, z_done, 0)
    finish_exchange(0, slots0, 1, 4)
    finish_exchange(1, slots1, 1, 16)
    finish_exchange(2, slots2, 1, 16)
    finish_exchange(3, slots3, 1, 16)


def body(activations, kv_cotangents):
    tokens = activations.shape[0]
    dma = pltpu.SemaphoreType.DMA
    rest = COLS - PART
    out = pl.pallas_call(
        kernel,
        out_shape=jax.ShapeDtypeStruct((40, COLS), F32),
        in_specs=[pl.BlockSpec(memory_space=pl.ANY)] * 2,
        out_specs=pl.BlockSpec(memory_space=pltpu.VMEM),
        scratch_shapes=[
            pltpu.VMEM((4, tokens, TILE), BF16),
            pltpu.VMEM((4, tokens, TILE), BF16),
            pltpu.VMEM(kv_cotangents.shape, BF16),
            pltpu.VMEM((tokens, COLS), BF16),
            pltpu.VMEM((tokens, COLS), BF16),
            pltpu.VMEM((2, 32, BLOCK, COLS), BF16),
            pltpu.VMEM((3, 8, BLOCK, PART), BF16),
            pltpu.VMEM((3, 8, BLOCK, PART), BF16),
            pltpu.VMEM((4, 8, BLOCK, PART), F32),
            pltpu.VMEM((3, 2, 4, BLOCK, rest), BF16),
            pltpu.VMEM((4, 2, 4, BLOCK, rest), BF16),
            pltpu.VMEM((3, 4, 2, BLOCK, rest), BF16),
            pltpu.VMEM((4, 4, 2, BLOCK, rest), F32),
            pltpu.VMEM((4, 10, 8, 128), F32),
            pltpu.VMEM((2, 2, 4, BLOCK, PART // 2), BF16),
            pltpu.VMEM((4, 4, BLOCK, PART // 2), BF16),
            pltpu.VMEM((4, 4, BLOCK, PART // 2), BF16),
            pltpu.VMEM((2, 2, 4, BLOCK, rest // 2), BF16),
            pltpu.VMEM((4, 4, BLOCK, rest // 2), BF16),
            pltpu.VMEM((16, BLOCK, COLS // 2), F32),
            pltpu.VMEM((16, 16, 128), F32),
            pltpu.VMEM((4, 8, 128), F32),
            pltpu.VMEM((4, 8, 128), F32),
            pltpu.VMEM((4, 8, 128), F32),
            pltpu.VMEM((16, 8, 128), F32),
            pltpu.VMEM((16, 8, 128), F32),
            pltpu.VMEM((16, 8, 128), F32),
            pltpu.VMEM((4, 8, 128), F32),
            pltpu.VMEM((4, 8, 128), F32),
            dma((5,)),
            dma((5,)),
            dma((5,)),
            dma((3, 8)),
            dma((3, 8)),
            dma((3, 8)),
            dma((3, 8)),
            dma((3, 8)),
            dma((3, 8)),
            dma((2, 2)),
            dma((4,)),
            dma((2, 2, 4)),
            dma((4, 4)),
            dma((3, 4)),
            dma((4, 4)),
            dma((4, 16)),
            dma((4, 16)),
            dma((4, 4)),
        ],
        compiler_params=pltpu.CompilerParams(
            collective_id=0, has_side_effects=True, vmem_limit_bytes=58 * 2**20
        ),
    )(activations, kv_cotangents)
    return out.reshape(40, kv_cotangents.shape[1], kv_cotangents.shape[2])


def solution(mesh):
    return jax.shard_map(
        body,
        mesh=mesh,
        in_specs=(P("dp", None), P("dp", "tensor", None)),
        out_specs=P("dp", "tensor", None),
        check_vma=False,
    )
```

```python
import functools

import jax
import jax.numpy as jnp
from jax import lax
from jax.experimental import pallas as pl
from jax.experimental.pallas import tpu as pltpu
from jax.sharding import PartitionSpec as P

MESH = pl.DeviceIdType.MESH
F32 = jnp.float32
BF16 = jnp.bfloat16
EPS = 1e-6
POWER = 9
TOP = 2.0**13
HALF = 2560
TILE = 640
BLOCK = 80
COLS = 1024
PART = 512


def coords(dp):
    return dp // 32, (dp // 8) % 4, (dp // 2) % 4, dp % 2


def rank(y, z, x, c):
    return ((y * 4 + z) * 4 + x) * 2 + c


def encode(v):
    v2 = v * v
    v4 = v2 * v2
    return (v4 * v4 * v).astype(BF16)


def decode(code):
    y = code.astype(F32)
    size = jnp.exp2(jnp.log2(jnp.abs(y)) * (1.0 / POWER))
    return jnp.where(y < 0, -size, size)


def iotas(rows):
    shape = (rows, 128)
    return (
        lax.broadcasted_iota(jnp.int32, shape, 0),
        lax.broadcasted_iota(jnp.int32, shape, 1),
    )


def partner_rows(gram, bit):
    rows = gram.shape[0]
    if bit == 8:
        return jnp.concatenate([gram[8:16], gram[0:8]], axis=0)
    parts = []
    for first in range(0, rows, 8):
        part = gram[first : first + 8]
        row = lax.broadcasted_iota(jnp.int32, part.shape, 0)
        parts.append(
            jnp.where((row & bit) == 0, pltpu.roll(part, 8 - bit, 0), pltpu.roll(part, bit, 0))
        )
    return parts[0] if len(parts) == 1 else jnp.concatenate(parts, axis=0)


def partner_lanes(gram, bit):
    lane = lax.broadcasted_iota(jnp.int32, gram.shape, 1)
    return jnp.where((lane & bit) == 0, pltpu.roll(gram, 128 - bit, 1), pltpu.roll(gram, bit, 1))


def solve(gram, count):
    rows = gram.shape[0]
    row, lane = iotas(rows)
    on_diag = row == lane
    weight = jnp.ones((rows, 1), F32)
    bit = 1
    while bit < count:
        paired = (row ^ bit) == lane
        kept = jnp.where(on_diag, gram, 0.0)
        crossed = jnp.where(paired, gram, 0.0)
        col = 1.0 - jnp.sum(crossed, axis=1, keepdims=True) / (
            2.0 * jnp.sum(kept, axis=1, keepdims=True) + EPS
        )
        across = 1.0 - jnp.sum(crossed, axis=0, keepdims=True) / (
            2.0 * jnp.sum(kept, axis=0, keepdims=True) + EPS
        )
        weight = weight * col
        gram = gram * col * across
        if bit * 2 < count:
            gram = gram + partner_rows(gram, bit)
            gram = gram + partner_lanes(gram, bit)
        bit *= 2
    return weight


def total(values):
    return jnp.sum(values, keepdims=True)


def wide(value, rows=16):
    return jnp.broadcast_to(value, (rows, 128))


def fold(values):
    rows, columns = values.shape
    parts = [
        values[r : r + 8, l : l + 128] for r in range(0, rows, 8) for l in range(0, columns, 128)
    ]
    while len(parts) > 1:
        odd = parts[len(parts) & ~1 :]
        parts = [p + q for p, q in zip(parts[0::2], parts[1::2])] + odd
    return parts[0]


def pair_weights(low_sq, up_sq, cross):
    return 1.0 - cross / (2.0 * low_sq + EPS), 1.0 - cross / (2.0 * up_sq + EPS)


def solve4(gram):
    c0, c1 = pair_weights(gram[0, 0], gram[1, 1], gram[0, 1])
    c2, c3 = pair_weights(gram[2, 2], gram[3, 3], gram[2, 3])
    low_sq = c0 * c0 * gram[0, 0] + 2.0 * c0 * c1 * gram[0, 1] + c1 * c1 * gram[1, 1]
    up_sq = c2 * c2 * gram[2, 2] + 2.0 * c2 * c3 * gram[2, 3] + c3 * c3 * gram[3, 3]
    cross = c0 * (c2 * gram[0, 2] + c3 * gram[0, 3]) + c1 * (c2 * gram[1, 2] + c3 * gram[1, 3])
    low, up = pair_weights(low_sq, up_sq, cross)
    weight = [c0 * low, c1 * low, c2 * up, c3 * up]
    bound = sum(weight[i] * weight[i] * gram[i, i] for i in range(4)) * 4.0 + 1e-36
    return weight, bound


def kernel(
    a_hbm, k_hbm, o_ref,
    a_own, a_oth, k_raw, k_own, k_oth, grads, enc_x, recv_x, dec_x, enc_q, recv_q, recv_r, dec_q, sums_q,
    enc_y, recv_y, recv_z, enc_yq, recv_yq, dec_z,
    rows_s, sums_z, msg, msg_q, slots0, slots1, slots2, slots3, slots_q, slots_w,
    load_sem, tok_send, tok_recv, x_send, x_recv, zq_send, zq_recv, xr_send, xr_recv,
    yq_send, yq_recv, y_send, y_recv, z_send, z_recv, r_send, r_recv, q_sems, ready,
):
    me = lax.axis_index("dp")
    t = lax.axis_index("tensor")
    y, z, x, c = coords(me)
    row8, lane8 = iotas(8)

    def group16(k):
        return rank(y, z, (x + k // 4) % 4, (c + (k // 2) % 2) % 2), (t + k % 2) % 2

    def plane16(k):
        return rank((y + k // 4) % 4, (z + k % 4) % 4, x, c), t

    def a_cols(core, i):
        return pl.ds(pl.multiple_of(core * HALF + i * TILE, 128), TILE)

    load_k = pltpu.make_async_copy(k_hbm, k_raw, load_sem.at[4])
    load_k.start()

    def load_a(i):
        return pltpu.make_async_copy(a_hbm.at[:, a_cols(c, i)], a_own.at[i], load_sem.at[i])

    def start_load(i, _):
        load_a(i).start()
        return _

    lax.fori_loop(0, 4, start_load, 0)

    barrier = pltpu.get_barrier_semaphore()
    other = (rank(y, z, x, 1 - c), t)

    def greet_group(k, _):
        pl.semaphore_signal(
            barrier,
            inc=1,
            device_id=(rank(y, z, (x + k // 2) % 4, 0), (t + k % 2) % 2),
            device_id_type=MESH,
        )
        return _

    def greet_plane(k, _):
        pl.semaphore_signal(
            barrier,
            inc=1,
            device_id=(rank((y + k // 4) % 4, (z + k % 4) % 4, x, 0), t),
            device_id_type=MESH,
        )
        return _

    @pl.when(c == 0)
    def open_pair():
        pl.semaphore_signal(barrier, inc=1, device_id=other, device_id_type=MESH)

    @pl.when(c == 1)
    def answer_pair():
        pl.semaphore_wait(barrier, 1)
        pl.semaphore_signal(ready, inc=1, device_id=other, device_id_type=MESH)

    @pl.when(c == 0)
    def greet_chips():
        pl.semaphore_wait(ready, 1)

    give_k = pltpu.make_async_remote_copy(
        k_own, k_oth, tok_send.at[4], tok_recv.at[4], device_id=other, device_id_type=MESH
    )

    def give_a(i):
        return pltpu.make_async_remote_copy(
            a_hbm.at[:, a_cols(1 - c, i)],
            a_oth.at[i],
            tok_send.at[i],
            tok_recv.at[i],
            device_id=other,
            device_id_type=MESH,
        )

    give_a(0).start()

    @pl.when(c == 0)
    def greet_all():
        lax.fori_loop(1, 8, greet_group, 0)
        lax.fori_loop(1, 16, greet_plane, 0)

    load_k.wait()

    def pack_k(n, _):
        r = pl.ds(pl.multiple_of(n * 32, 32), 32)
        k_own[r] = pltpu.einshape("thc->t(hc)", k_raw[r])
        return _

    lax.fori_loop(0, k_raw.shape[0] // 32, pack_k, 0)
    give_k.start()

    def start_give(i, _):
        give_a(i).start()
        return _

    lax.fori_loop(1, 4, start_give, 0)

    def gradient(a_ref, k_ref):
        return lax.dot_general(
            a_ref[...], k_ref[...], (((0,), (0,)), ((), ())), preferred_element_type=F32
        ).astype(BF16)

    def own_tile(i, own_sq):
        load_a(i).wait()
        tile = gradient(a_own.at[i], k_own)
        grads[0, pl.ds(i * 8, 8)] = tile.reshape(8, BLOCK, COLS)
        tile = tile.astype(F32)
        return own_sq + fold(tile * tile)

    zero = jnp.zeros((8, 128), F32)
    own_sq = lax.fori_loop(0, 4, own_tile, zero)

    @pl.when(c == 0)
    def all_greeted():
        pl.semaphore_wait(barrier, 22)
        pl.semaphore_signal(ready, inc=1, device_id=other, device_id_type=MESH)

    give_k.wait_recv()

    def other_tile(i, sums):
        cross, oth_sq = sums
        give_a(i).wait_recv()
        tile = gradient(a_oth.at[i], k_oth)
        grads[1, pl.ds(i * 8, 8)] = tile.reshape(8, BLOCK, COLS)
        tile = tile.astype(F32)
        own = grads[0, pl.ds(i * 8, 8)].astype(F32).reshape(TILE, COLS)
        return cross + fold(own * tile), oth_sq + fold(tile * tile)

    cross, oth_sq = lax.fori_loop(0, 4, other_tile, (zero, zero))

    @pl.when(c == 1)
    def told():
        pl.semaphore_wait(ready, 1)

    own_sq, oth_sq, cross = total(own_sq), total(oth_sq), total(cross)
    lower_sq = jnp.where(c == 0, own_sq, oth_sq)
    upper_sq = jnp.where(c == 0, oth_sq, own_sq)

    def entry(i, j):
        return (row8 == i) & (lane8 == j)

    def exchange(stage, slots, first, last, target):
        def go(k, _):
            pltpu.make_async_remote_copy(
                msg.at[stage],
                slots.at[k],
                r_send.at[stage, k],
                r_recv.at[stage, k],
                device_id=target(k),
                device_id_type=MESH,
            ).start()
            return _

        def arrive(k, table):
            pltpu.make_async_copy(slots.at[k], slots.at[k], r_recv.at[stage, k]).wait()
            return table + slots[k]

        lax.fori_loop(first, last, go, 0)
        return lax.fori_loop(first, last, arrive, msg[stage])

    def finish_exchange(stage, slots, first, last):
        def done(k, _):
            pltpu.make_async_copy(slots.at[k], slots.at[k], r_send.at[stage, k]).wait()
            return _

        lax.fori_loop(first, last, done, 0)

    msg[0] = (
        jnp.where(entry(0, 0), lower_sq, 0.0)
        + jnp.where(entry(1, 1), upper_sq, 0.0)
        + jnp.where(entry(0, 1) | entry(1, 0), cross, 0.0)
    )
    gram = exchange(0, slots0, 1, 4, group16)

    def pick(table, i, j):
        return total(jnp.where(entry(i, j), table, 0.0))

    lower_sq, upper_sq, cross = pick(gram, 0, 0), pick(gram, 1, 1), pick(gram, 0, 1)
    w_low, w_up = pair_weights(lower_sq, upper_sq, cross)
    bound = 2.0 * (w_low * w_low * lower_sq + w_up * w_up * upper_sq) + 1e-36
    scale = TOP * lax.rsqrt(bound)
    inverse1 = 1.0 / scale
    w_own = wide(scale * jnp.where(c == 0, w_low, w_up))
    w_oth = wide(scale * jnp.where(c == 0, w_up, w_low))

    def pair_of(block, r, l):
        own = grads[0, block, r : r + 16, l : l + 128].astype(F32)
        oth = grads[1, block, r : r + 16, l : l + 128].astype(F32)
        return w_own * own + w_oth * oth

    def along_x(d):
        return rank(y, z, (x + d) % 4, c), t

    def along_z(d):
        return rank(y, (z + d) % 4, x, c), t

    def x_copy(d, b):
        return pltpu.make_async_remote_copy(
            enc_x.at[d - 1, b],
            recv_x.at[d - 1, b],
            x_send.at[d - 1, b],
            x_recv.at[d - 1, b],
            device_id=along_x(d),
            device_id_type=MESH,
        )

    def zq_copy(dz, yy, dx):
        return pltpu.make_async_remote_copy(
            enc_q.at[dz - 1, yy, dx],
            recv_q.at[dz, yy, dx],
            zq_send.at[dz - 1, yy * 4 + dx],
            zq_recv.at[dz - 1, yy * 4 + dx],
            device_id=along_z(dz),
            device_id_type=MESH,
        )

    def xr_copy(dx, dz, yy):
        return pltpu.make_async_remote_copy(
            recv_q.at[dz, yy, dx],
            recv_r.at[dx - 1, dz, yy],
            xr_send.at[dx - 1, dz * 2 + yy],
            xr_recv.at[dx - 1, dz * 2 + yy],
            device_id=along_x(dx),
            device_id_type=MESH,
        )

    def x_send_block(b):
        for d in (2, 1, 3):
            block = b * 4 + (x + d) % 4
            for r in range(0, BLOCK, 16):
                for l in range(0, PART, 128):
                    enc_x[d - 1, b, r : r + 16, l : l + 128] = encode(pair_of(block, r, l))
            x_copy(d, b).start()

    def q_send_block(yy, dx):
        for dz in (2, 1, 3, 0):
            block = yy * 16 + ((z + dz) % 4) * 4 + (x + dx) % 4
            for r in range(0, BLOCK, 16):
                for l in range(0, COLS - PART, 128):
                    code = encode(pair_of(block, r, PART + l))
                    if dz:
                        enc_q[dz - 1, yy, dx, r : r + 16, l : l + 128] = code
                    else:
                        recv_q[0, yy, dx, r : r + 16, l : l + 128] = code
            if dz:
                zq_copy(dz, yy, dx).start()

    def send_far(m, _):
        x_send_block(m)
        q_send_block(m, 2)
        return _

    def send_near(k, _):
        x_send_block(2 + k)
        q_send_block(k // 2, 1 + 2 * (k % 2))
        return _

    def send_own(m, _):
        x_send_block(6 + m)
        q_send_block(m, 0)
        return _

    lax.fori_loop(0, 2, send_far, 0)
    lax.fori_loop(0, 4, send_near, 0)
    lax.fori_loop(0, 2, send_own, 0)

    def x_own_block(b, _):
        for r in range(0, BLOCK, 16):
            for l in range(0, PART, 128):
                dec_x[x, b, r : r + 16, l : l + 128] = pair_of(b * 4 + x, r, l)
        return _

    lax.fori_loop(0, 8, x_own_block, 0)
    pairs4 = [(i, j) for i in range(4) for j in range(i, 4)]

    def x_recv_block(b, sums):
        for d in (1, 3, 2):
            x_copy(d, b).wait_recv()
            source = (x + 4 - d) % 4
            for r in range(0, BLOCK, 16):
                for l in range(0, PART, 256):
                    dec_x[source, b, r : r + 16, l : l + 256] = decode(
                        recv_x[d - 1, b, r : r + 16, l : l + 256]
                    )
        sums = list(sums)
        for r in range(0, BLOCK, 8):
            for l in range(0, PART, 128):
                v = [dec_x[i, b, r : r + 8, l : l + 128] for i in range(4)]
                for n, (i, j) in enumerate(pairs4):
                    sums[n] = sums[n] + v[i] * v[j]
        return tuple(sums)

    def relay(yy, dx):
        for dz in (0, 1, 3, 2):
            if dz:
                zq_copy(dz, yy, dx).wait_recv()
            xr_copy(dx, dz, yy).start()

    def relay_far(m, _):
        relay(m, 2)
        return _

    def relay_near(k, _):
        relay(k // 2, 1 + 2 * (k % 2))
        return _

    sums = lax.fori_loop(0, 4, x_recv_block, (zero,) * 10)
    lax.fori_loop(0, 2, relay_far, 0)
    sums = lax.fori_loop(4, 8, x_recv_block, sums)
    lax.fori_loop(0, 4, relay_near, 0)

    def q_decode(dx, yy):
        def one(dz, _):
            if dx:
                xr_copy(dx, dz, yy).wait_recv()
                source = recv_r.at[dx - 1, dz, yy]
            else:
                source = recv_q.at[dz, yy, 0]
            for r in range(0, BLOCK, 16):
                for l in range(0, COLS - PART, 256):
                    dec_q[dz, (x + 4 - dx) % 4, yy, r : r + 16, l : l + 256] = decode(
                        source[r : r + 16, l : l + 256]
                    )
            return _

        lax.fori_loop(0, 4, one, 0)

    def q_own(yy):
        for dz in (1, 2, 3):
            zq_copy(dz, yy, 0).wait_recv()
        q_decode(0, yy)

    def q_gram(yy):
        def one(dz, _):
            sums = [zero if yy == 0 else sums_q[dz, n] for n in range(10)]
            for r in range(0, BLOCK, 8):
                for l in range(0, COLS - PART, 128):
                    v = [dec_q[dz, i, yy, r : r + 8, l : l + 128] for i in range(4)]
                    for n, (i, j) in enumerate(pairs4):
                        sums[n] = sums[n] + v[i] * v[j]
            for n in range(10):
                sums_q[dz, n] = sums[n]
            return _

        lax.fori_loop(0, 4, one, 0)

    q_decode(2, 0)
    q_decode(2, 1)
    q_decode(1, 0)
    q_decode(3, 0)
    q_own(0)
    q_gram(0)
    q_decode(1, 1)
    q_decode(3, 1)
    q_own(1)
    q_gram(1)

    def q_copy(dz):
        return pltpu.make_async_remote_copy(
            msg_q.at[dz],
            slots_q.at[dz],
            q_sems.at[0, dz],
            q_sems.at[1, dz],
            device_id=along_z(4 - dz),
            device_id_type=MESH,
        )

    def tile_of(sums):
        table = jnp.zeros((8, 128), F32)
        for (i, j), s in zip(pairs4, sums):
            table = table + jnp.where(entry(i, j), total(s), 0.0)
        return table

    for dz in (2, 1, 3):
        msg_q[dz] = tile_of([sums_q[dz, n] for n in range(10)])
        q_copy(dz).start()
    table = jnp.where(entry(4, x), 0.25 * inverse1, 0.0)
    table = table + tile_of([s + sums_q[0, n] for n, s in enumerate(sums)])
    for dz in (1, 3, 2):
        q_copy(dz).wait_recv()
        table = table + slots_q[dz]
    msg[1] = table
    table = exchange(1, slots1, 1, 16, group16)
    inv = [pick(table, 4, i) for i in range(4)]
    weight, bound = solve4({(i, j): pick(table, i, j) * inv[i] * inv[j] for i, j in pairs4})
    scale = TOP * lax.rsqrt(bound)
    inverse3 = 1.0 / scale
    w_own_z = [weight[i] * inv[i] * scale for i in range(4)]

    def w_copy(dz):
        return pltpu.make_async_remote_copy(
            msg_q.at[0],
            slots_w.at[dz],
            q_sems.at[2, dz],
            q_sems.at[3, dz],
            device_id=along_z(dz),
            device_id_type=MESH,
        )

    table = jnp.zeros((8, 128), F32)
    for i in range(4):
        table = table + jnp.where(entry(0, i), w_own_z[i], 0.0)
    msg_q[0] = table
    for dz in (2, 1, 3):
        w_copy(dz).start()
    w_x = [wide(w_own_z[i], 40) for i in range(4)]

    def y_stays(yy, half):
        py = 2 * c + yy
        return (py == y) & (half == c)

    def y_copy(yy, half, zt):
        return pltpu.make_async_remote_copy(
            enc_y.at[yy, half, zt],
            recv_y.at[y, zt],
            y_send.at[yy, half, zt],
            y_recv.at[y, zt],
            device_id=(rank(2 * c + yy, z, x, half), t),
            device_id_type=MESH,
        )

    def combined(weights, block, half, l, width):
        parts = []
        for first in (l, width + l):
            rows, at = slice(40 * half, 40 * half + 40), slice(first, first + 128)
            v = [block(i, rows, at) for i in range(4)]
            parts.append(
                (weights[0] * v[0] + weights[1] * v[1]) + (weights[2] * v[2] + weights[3] * v[3])
            )
        return encode(jnp.concatenate(parts, axis=0))

    def y_send_block(n, _):
        zt = (z + 1 + n // 2) % 4
        yy = n % 2
        b = yy * 4 + zt
        for half in range(2):
            for l in range(0, PART // 2, 128):
                enc_y[yy, half, zt, :, l : l + 128] = combined(
                    w_x, lambda i, r, at: dec_x[i, b, r, at], half, l, PART // 2
                )
            here = y_stays(yy, half)

            @pl.when(here)
            def keep():
                pltpu.make_async_copy(
                    enc_y.at[yy, half, zt], recv_y.at[y, zt], y_recv.at[y, zt]
                ).start()

            @pl.when(jnp.logical_not(here))
            def push():
                y_copy(yy, half, zt).start()

        return _

    lax.fori_loop(0, 8, y_send_block, 0)

    def z_copy(d, sy):
        zt = (z + d) % 4
        return pltpu.make_async_remote_copy(
            recv_y.at[sy, zt],
            recv_z.at[z, sy],
            z_send.at[d - 1, sy],
            z_recv.at[z, sy],
            device_id=(rank(y, zt, x, c), t),
            device_id_type=MESH,
        )

    def y_arrival(sy, zt):
        pltpu.make_async_copy(recv_y.at[sy, zt], recv_y.at[sy, zt], y_recv.at[sy, zt]).wait()

    def z_relay(n, _):
        d = 1 + n // 4
        sy = n % 4
        y_arrival(sy, (z + d) % 4)
        z_copy(d, sy).start()
        return _

    lax.fori_loop(0, 12, z_relay, 0)

    def yq_copy(yy, half):
        return pltpu.make_async_remote_copy(
            enc_yq.at[yy, half],
            recv_yq.at[y],
            yq_send.at[yy, half],
            yq_recv.at[y],
            device_id=(rank(2 * c + yy, z, x, half), t),
            device_id_type=MESH,
        )

    w_by_z = []
    for dz in range(4):
        if dz:
            w_copy(dz).wait_recv()
            w_by_z.append([wide(pick(slots_w[dz], 0, i), 40) for i in range(4)])
        else:
            w_by_z.append(w_x)

    def yq_send_block(yy, _):
        for half in range(2):
            for dz in range(4):
                for l in range(0, (COLS - PART) // 2, 128):
                    enc_yq[yy, half, (z + 4 - dz) % 4, :, l : l + 128] = combined(
                        w_by_z[dz],
                        lambda i, r, at: dec_q[dz, i, yy, r, at],
                        half,
                        l,
                        (COLS - PART) // 2,
                    )
            here = y_stays(yy, half)

            @pl.when(here)
            def keep():
                pltpu.make_async_copy(enc_yq.at[yy, half], recv_yq.at[y], yq_recv.at[y]).start()

            @pl.when(jnp.logical_not(here))
            def push():
                yq_copy(yy, half).start()

        return _

    lax.fori_loop(0, 2, yq_send_block, 0)

    def own_z(sy, _):
        y_arrival(sy, z)
        for r in range(0, BLOCK, 16):
            dec_z[sy * 4 + z, r : r + 16, 0 : PART // 2] = decode(recv_y[sy, z, r : r + 16, :])
        return _

    lax.fori_loop(0, 4, own_z, 0)

    def yq_arrival(n, _):
        sy = (y + n) % 4
        pltpu.make_async_copy(recv_yq.at[sy], recv_yq.at[sy], yq_recv.at[sy]).wait()
        for sz in range(4):
            for r in range(0, BLOCK, 16):
                dec_z[sy * 4 + sz, r : r + 16, PART // 2 :] = decode(recv_yq[sy, sz, r : r + 16, :])
        return _

    lax.fori_loop(0, 4, yq_arrival, 0)

    def group_pairs(a, b):
        return [(i, j) for i in range(4) for j in range(4) if a != b or i <= j]

    def products(a, b, first, last, sums):
        def one(n, sums):
            r = pl.ds(pl.multiple_of(n * 8, 8), 8)
            sums = list(sums)
            for l in range(first, last, 128):
                v = [dec_z[i * 4 + (z + 4 - a) % 4, r, l : l + 128] for i in range(4)]
                w = v if a == b else [dec_z[i * 4 + (z + 4 - b) % 4, r, l : l + 128] for i in range(4)]
                for m, (i, j) in enumerate(group_pairs(a, b)):
                    sums[m] = sums[m] + v[i] * w[j]
            return tuple(sums)

        return lax.fori_loop(0, 10, one, tuple(sums))

    def finish_rows(a, b, sums):
        for (i, j), total_ij in zip(group_pairs(a, b), sums):
            line = jnp.sum(total_ij, axis=0, keepdims=True)
            first, second = i * 4 + (z + 4 - a) % 4, j * 4 + (z + 4 - b) % 4
            rows_s[first, pl.ds(second, 1), :] = line
            rows_s[second, pl.ds(first, 1), :] = line

    blocks = [(a, b) for a in range(4) for b in range(a + 1)]
    for n, (a, b) in enumerate(blocks):
        sums = products(a, b, PART // 2, COLS // 2, [zero] * len(group_pairs(a, b)))
        for m, value in enumerate(sums):
            sums_z[n, m] = value

    def z_arrival(source, sy):
        pltpu.make_async_copy(
            recv_z.at[source, sy], recv_z.at[source, sy], z_recv.at[source, sy]
        ).wait()
        for r in range(0, BLOCK, 16):
            dec_z[sy * 4 + source, r : r + 16, 0 : PART // 2] = decode(
                recv_z[source, sy, r : r + 16, :]
            )

    for a in range(4):
        if a:

            def arrive_z(sy, _):
                z_arrival((z + 4 - a) % 4, sy)
                return _

            lax.fori_loop(0, 4, arrive_z, 0)
        for b in range(a + 1):
            n = blocks.index((a, b))
            before = [sums_z[n, m] for m in range(len(group_pairs(a, b)))]
            finish_rows(a, b, products(a, b, 0, PART // 2, before))
    row16, lane16 = iotas(16)
    gram = jnp.zeros((16, 128), F32)
    for i in range(16):
        gram = gram + jnp.where(lane16 == i, jnp.sum(rows_s[i], axis=1, keepdims=True), 0.0)
    msg[2] = gram[0:8] + pltpu.roll(gram[8:16], 64, 1)
    partial = exchange(2, slots2, 1, 16, group16)
    msg[3] = partial + jnp.where(entry(0, 32 + 4 * y + z), inverse3, 0.0)
    table = exchange(3, slots3, 1, 16, plane16)
    inv_row = jnp.where(lane8[0:1] < 16, pltpu.roll(table, 96, 1)[0:1], 0.0)
    inv_col = jnp.sum(jnp.where(row16 == lane16, inv_row, 0.0), axis=1, keepdims=True)
    gram = jnp.concatenate([table, pltpu.roll(table, 64, 1)], axis=0)
    gram = jnp.where(lane16 < 16, gram, 0.0) * inv_row * inv_col
    weight = solve(gram, 16) * inv_col
    w_z = [wide(weight[i : i + 1], 8) for i in range(16)]
    for first, width, at in ((0, PART // 2, 0), (PART, (COLS - PART) // 2, PART // 2)):
        for h in range(2):
            for r in range(0, 40, 8):
                for l in range(0, width, 128):
                    rows, lanes = slice(40 * h + r, 40 * h + r + 8), slice(at + l, at + l + 128)
                    terms = [w_z[i] * dec_z[i, rows, lanes] for i in range(16)]
                    while len(terms) > 1:
                        terms = [p + q for p, q in zip(terms[0::2], terms[1::2])]
                    column = first + h * width + l
                    o_ref[r : r + 8, column : column + 128] = terms[0]

    give_k.wait_send()

    def given(i, _):
        give_a(i).wait_send()
        return _

    lax.fori_loop(0, 4, given, 0)

    def x_done(b, _):
        for d in (1, 2, 3):
            x_copy(d, b).wait_send()
        return _

    lax.fori_loop(0, 8, x_done, 0)

    def zq_done(n, _):
        for dz in (1, 2, 3):
            zq_copy(dz, n // 4, n % 4).wait_send()
        return _

    lax.fori_loop(0, 8, zq_done, 0)

    def xr_done(n, _):
        for dx in (1, 2, 3):
            xr_copy(dx, n // 2, n % 2).wait_send()
        return _

    lax.fori_loop(0, 8, xr_done, 0)
    for dz in (1, 2, 3):
        q_copy(dz).wait_send()
        w_copy(dz).wait_send()

    def yq_done(yy, _):
        for half in range(2):

            @pl.when(jnp.logical_not(y_stays(yy, half)))
            def settle_q():
                yq_copy(yy, half).wait_send()

        return _

    lax.fori_loop(0, 2, yq_done, 0)

    def y_done(n, _):
        for half in range(2):

            @pl.when(jnp.logical_not(y_stays(n % 2, half)))
            def settle():
                y_copy(n % 2, half, n // 2).wait_send()

        return _

    lax.fori_loop(0, 8, y_done, 0)

    def z_done(n, _):
        z_copy(1 + n // 4, n % 4).wait_send()
        return _

    lax.fori_loop(0, 12, z_done, 0)
    finish_exchange(0, slots0, 1, 4)
    finish_exchange(1, slots1, 1, 16)
    finish_exchange(2, slots2, 1, 16)
    finish_exchange(3, slots3, 1, 16)


def body(activations, kv_cotangents):
    tokens = activations.shape[0]
    dma = pltpu.SemaphoreType.DMA
    rest = COLS - PART
    out = pl.pallas_call(
        kernel,
        out_shape=jax.ShapeDtypeStruct((40, COLS), F32),
        in_specs=[pl.BlockSpec(memory_space=pl.ANY)] * 2,
        out_specs=pl.BlockSpec(memory_space=pltpu.VMEM),
        scratch_shapes=[
            pltpu.VMEM((4, tokens, TILE), BF16),
            pltpu.VMEM((4, tokens, TILE), BF16),
            pltpu.VMEM(kv_cotangents.shape, BF16),
            pltpu.VMEM((tokens, COLS), BF16),
            pltpu.VMEM((tokens, COLS), BF16),
            pltpu.VMEM((2, 32, BLOCK, COLS), BF16),
            pltpu.VMEM((3, 8, BLOCK, PART), BF16),
            pltpu.VMEM((3, 8, BLOCK, PART), BF16),
            pltpu.VMEM((4, 8, BLOCK, PART), F32),
            pltpu.VMEM((3, 2, 4, BLOCK, rest), BF16),
            pltpu.VMEM((4, 2, 4, BLOCK, rest), BF16),
            pltpu.VMEM((3, 4, 2, BLOCK, rest), BF16),
            pltpu.VMEM((4, 4, 2, BLOCK, rest), F32),
            pltpu.VMEM((4, 10, 8, 128), F32),
            pltpu.VMEM((2, 2, 4, BLOCK, PART // 2), BF16),
            pltpu.VMEM((4, 4, BLOCK, PART // 2), BF16),
            pltpu.VMEM((4, 4, BLOCK, PART // 2), BF16),
            pltpu.VMEM((2, 2, 4, BLOCK, rest // 2), BF16),
            pltpu.VMEM((4, 4, BLOCK, rest // 2), BF16),
            pltpu.VMEM((16, BLOCK, COLS // 2), F32),
            pltpu.VMEM((16, 16, 128), F32),
            pltpu.VMEM((10, 16, 8, 128), F32),
            pltpu.VMEM((4, 8, 128), F32),
            pltpu.VMEM((4, 8, 128), F32),
            pltpu.VMEM((4, 8, 128), F32),
            pltpu.VMEM((16, 8, 128), F32),
            pltpu.VMEM((16, 8, 128), F32),
            pltpu.VMEM((16, 8, 128), F32),
            pltpu.VMEM((4, 8, 128), F32),
            pltpu.VMEM((4, 8, 128), F32),
            dma((5,)),
            dma((5,)),
            dma((5,)),
            dma((3, 8)),
            dma((3, 8)),
            dma((3, 8)),
            dma((3, 8)),
            dma((3, 8)),
            dma((3, 8)),
            dma((2, 2)),
            dma((4,)),
            dma((2, 2, 4)),
            dma((4, 4)),
            dma((3, 4)),
            dma((4, 4)),
            dma((4, 16)),
            dma((4, 16)),
            dma((4, 4)),
            pltpu.SemaphoreType.REGULAR,
        ],
        compiler_params=pltpu.CompilerParams(
            collective_id=0, has_side_effects=True, vmem_limit_bytes=58 * 2**20
        ),
    )(activations, kv_cotangents)
    return out.reshape(40, kv_cotangents.shape[1], kv_cotangents.shape[2])


def solution(mesh):
    return jax.shard_map(
        body,
        mesh=mesh,
        in_specs=(P("dp", None), P("dp", "tensor", None)),
        out_specs=P("dp", "tensor", None),
        check_vma=False,
    )
```

```python
import functools

import jax
import jax.numpy as jnp
from jax import lax
from jax.experimental import pallas as pl
from jax.experimental.pallas import tpu as pltpu
from jax.sharding import PartitionSpec as P

MESH = pl.DeviceIdType.MESH
F32 = jnp.float32
BF16 = jnp.bfloat16
EPS = 1e-6
POWER = 9
TOP = 2.0**13
HALF = 2560
TILE = 640
BLOCK = 80
COLS = 1024
PART = 512


def coords(dp):
    return dp // 32, (dp // 8) % 4, (dp // 2) % 4, dp % 2


def rank(y, z, x, c):
    return ((y * 4 + z) * 4 + x) * 2 + c


def encode(v):
    v2 = v * v
    v4 = v2 * v2
    return (v4 * v4 * v).astype(BF16)


def decode(code):
    y = code.astype(F32)
    size = jnp.exp2(jnp.log2(jnp.abs(y)) * (1.0 / POWER))
    return jnp.where(y < 0, -size, size)


def iotas(rows):
    shape = (rows, 128)
    return (
        lax.broadcasted_iota(jnp.int32, shape, 0),
        lax.broadcasted_iota(jnp.int32, shape, 1),
    )


def partner_rows(gram, bit):
    rows = gram.shape[0]
    if bit == 8:
        return jnp.concatenate([gram[8:16], gram[0:8]], axis=0)
    parts = []
    for first in range(0, rows, 8):
        part = gram[first : first + 8]
        row = lax.broadcasted_iota(jnp.int32, part.shape, 0)
        parts.append(
            jnp.where((row & bit) == 0, pltpu.roll(part, 8 - bit, 0), pltpu.roll(part, bit, 0))
        )
    return parts[0] if len(parts) == 1 else jnp.concatenate(parts, axis=0)


def partner_lanes(gram, bit):
    lane = lax.broadcasted_iota(jnp.int32, gram.shape, 1)
    return jnp.where((lane & bit) == 0, pltpu.roll(gram, 128 - bit, 1), pltpu.roll(gram, bit, 1))


def solve(gram, count):
    rows = gram.shape[0]
    row, lane = iotas(rows)
    on_diag = row == lane
    weight = jnp.ones((rows, 1), F32)
    bit = 1
    while bit < count:
        paired = (row ^ bit) == lane
        kept = jnp.where(on_diag, gram, 0.0)
        crossed = jnp.where(paired, gram, 0.0)
        col = 1.0 - jnp.sum(crossed, axis=1, keepdims=True) / (
            2.0 * jnp.sum(kept, axis=1, keepdims=True) + EPS
        )
        across = 1.0 - jnp.sum(crossed, axis=0, keepdims=True) / (
            2.0 * jnp.sum(kept, axis=0, keepdims=True) + EPS
        )
        weight = weight * col
        gram = gram * col * across
        if bit * 2 < count:
            gram = gram + partner_rows(gram, bit)
            gram = gram + partner_lanes(gram, bit)
        bit *= 2
    return weight


def total(values):
    return jnp.sum(values, keepdims=True)


def wide(value, rows=16):
    return jnp.broadcast_to(value, (rows, 128))


def fold(values):
    rows, columns = values.shape
    parts = [
        values[r : r + 8, l : l + 128] for r in range(0, rows, 8) for l in range(0, columns, 128)
    ]
    while len(parts) > 1:
        odd = parts[len(parts) & ~1 :]
        parts = [p + q for p, q in zip(parts[0::2], parts[1::2])] + odd
    return parts[0]


def pair_weights(low_sq, up_sq, cross):
    return 1.0 - cross / (2.0 * low_sq + EPS), 1.0 - cross / (2.0 * up_sq + EPS)


def solve4(gram):
    c0, c1 = pair_weights(gram[0, 0], gram[1, 1], gram[0, 1])
    c2, c3 = pair_weights(gram[2, 2], gram[3, 3], gram[2, 3])
    low_sq = c0 * c0 * gram[0, 0] + 2.0 * c0 * c1 * gram[0, 1] + c1 * c1 * gram[1, 1]
    up_sq = c2 * c2 * gram[2, 2] + 2.0 * c2 * c3 * gram[2, 3] + c3 * c3 * gram[3, 3]
    cross = c0 * (c2 * gram[0, 2] + c3 * gram[0, 3]) + c1 * (c2 * gram[1, 2] + c3 * gram[1, 3])
    low, up = pair_weights(low_sq, up_sq, cross)
    weight = [c0 * low, c1 * low, c2 * up, c3 * up]
    bound = sum(weight[i] * weight[i] * gram[i, i] for i in range(4)) * 4.0 + 1e-36
    return weight, bound


def kernel(
    a_hbm, k_hbm, o_ref,
    a_own, a_oth, k_raw, k_own, k_oth, grads, recv_g, msg_g, slots_g, enc_x, recv_x, dec_x, enc_q, recv_q, recv_r, dec_q, sums_q,
    enc_y, recv_y, recv_z, enc_yq, recv_yq, dec_z,
    rows_s, sums_z, msg0, msg1, msg2, msg3, msg_q, slots0, slots1, slots2, slots3, slots_q, slots_w,
    load_sem, tok_send, tok_recv, x_send, x_recv, zq_send, zq_recv, xr_send, xr_recv,
    yq_send, yq_recv, y_send, y_recv, z_send, z_recv, r_send, r_recv, q_sems, g_sems, ready,
):
    me = lax.axis_index("dp")
    t = lax.axis_index("tensor")
    y, z, x, c = coords(me)
    lane1 = lax.broadcasted_iota(jnp.int32, (1, 128), 1)

    def group16(k):
        return rank(y, z, (x + k // 4) % 4, (c + (k // 2) % 2) % 2), (t + k % 2) % 2

    def plane16(k):
        return rank((y + k // 4) % 4, (z + k % 4) % 4, x, c), t

    def a_cols(core, i):
        return pl.ds(pl.multiple_of(core * HALF + i * TILE, 128), TILE)

    load_k = pltpu.make_async_copy(k_hbm, k_raw, load_sem.at[4])
    load_k.start()

    def load_a(i):
        return pltpu.make_async_copy(a_hbm.at[:, a_cols(c, i)], a_own.at[i], load_sem.at[i])

    def start_load(i, _):
        load_a(i).start()
        return _

    lax.fori_loop(0, 4, start_load, 0)

    barrier = pltpu.get_barrier_semaphore()
    other = (rank(y, z, x, 1 - c), t)

    def greet_group(k, _):
        pl.semaphore_signal(
            barrier,
            inc=1,
            device_id=(rank(y, z, (x + k // 2) % 4, 0), (t + k % 2) % 2),
            device_id_type=MESH,
        )
        return _

    def greet_plane(k, _):
        pl.semaphore_signal(
            barrier,
            inc=1,
            device_id=(rank((y + k // 4) % 4, (z + k % 4) % 4, x, 0), t),
            device_id_type=MESH,
        )
        return _

    @pl.when(c == 0)
    def open_pair():
        pl.semaphore_signal(barrier, inc=1, device_id=other, device_id_type=MESH)

    @pl.when(c == 1)
    def answer_pair():
        pl.semaphore_wait(barrier, 1)
        pl.semaphore_signal(ready, inc=1, device_id=other, device_id_type=MESH)

    @pl.when(c == 0)
    def greet_chips():
        pl.semaphore_wait(ready, 1)

    give_k = pltpu.make_async_remote_copy(
        k_own, k_oth, tok_send.at[4], tok_recv.at[4], device_id=other, device_id_type=MESH
    )

    def give_a(i):
        return pltpu.make_async_remote_copy(
            a_hbm.at[:, a_cols(1 - c, i)],
            a_oth.at[i],
            tok_send.at[i],
            tok_recv.at[i],
            device_id=other,
            device_id_type=MESH,
        )

    give_a(0).start()

    @pl.when(c == 0)
    def greet_all():
        lax.fori_loop(1, 8, greet_group, 0)
        lax.fori_loop(1, 16, greet_plane, 0)

    load_k.wait()

    def pack_k(n, _):
        r = pl.ds(pl.multiple_of(n * 32, 32), 32)
        k_own[r] = pltpu.einshape("thc->t(hc)", k_raw[r])
        return _

    lax.fori_loop(0, k_raw.shape[0] // 32, pack_k, 0)
    give_k.start()

    def start_give(i, _):
        give_a(i).start()
        return _

    lax.fori_loop(1, 4, start_give, 0)

    def gradient(a_ref, k_ref):
        return lax.dot_general(
            a_ref[...], k_ref[...], (((0,), (0,)), ((), ())), preferred_element_type=F32
        ).astype(BF16)

    def own_tile(i, own_sq):
        load_a(i).wait()
        tile = gradient(a_own.at[i], k_own)
        grads[0, pl.ds(i * 8, 8)] = tile.reshape(8, BLOCK, COLS)
        tile = tile.astype(F32)
        return own_sq + fold(tile * tile)

    zero = jnp.zeros((8, 128), F32)
    own_sq = lax.fori_loop(0, 4, own_tile, zero)

    @pl.when(c == 0)
    def all_greeted():
        pl.semaphore_wait(barrier, 22)
        pl.semaphore_signal(ready, inc=1, device_id=other, device_id_type=MESH)

    @pl.when(c == 1)
    def told():
        pl.semaphore_wait(ready, 1)

    def along_x(d):
        return rank(y, z, (x + d) % 4, c), t

    def raw_copy(which, d):
        return pltpu.make_async_remote_copy(
            grads.at[which, (x + d) % 4, :, pl.ds(0, PART)],
            recv_g.at[which, d - 1],
            g_sems.at[0, which * 3 + d - 1],
            g_sems.at[1, which * 3 + d - 1],
            device_id=along_x(d),
            device_id_type=MESH,
        )

    for d in (2, 1, 3):
        raw_copy(0, d).start()
    give_k.wait_recv()

    def other_tile(i, sums):
        cross, oth_sq = sums
        give_a(i).wait_recv()
        tile = gradient(a_oth.at[i], k_oth)
        grads[1, pl.ds(i * 8, 8)] = tile.reshape(8, BLOCK, COLS)
        tile = tile.astype(F32)
        own = grads[0, pl.ds(i * 8, 8)].astype(F32).reshape(TILE, COLS)
        return cross + fold(own * tile), oth_sq + fold(tile * tile)

    sums = other_tile(0, (zero, zero))
    for d in (2, 1, 3):
        raw_copy(1, d).start()
    cross, oth_sq = lax.fori_loop(1, 4, other_tile, sums)

    own_sq, oth_sq, cross = total(own_sq), total(oth_sq), total(cross)
    lower_sq = jnp.where(c == 0, own_sq, oth_sq)
    upper_sq = jnp.where(c == 0, oth_sq, own_sq)

    def spot(lane, value):
        return jnp.where(lane1 == lane, value, 0.0)

    def pick(table, lane):
        return total(jnp.where(lane1 == lane, table, 0.0))

    def exchange(stage, msg, slots, first, last, target):
        def go(k, _):
            pltpu.make_async_remote_copy(
                msg,
                slots.at[k],
                r_send.at[stage, k],
                r_recv.at[stage, k],
                device_id=target(k),
                device_id_type=MESH,
            ).start()
            return _

        def arrive(k, table):
            pltpu.make_async_copy(slots.at[k], slots.at[k], r_recv.at[stage, k]).wait()
            return table + slots[k]

        lax.fori_loop(first, last, go, 0)
        return lax.fori_loop(first, last, arrive, msg[...])

    def finish_exchange(stage, slots, first, last):
        def done(k, _):
            pltpu.make_async_copy(slots.at[k], slots.at[k], r_send.at[stage, k]).wait()
            return _

        lax.fori_loop(first, last, done, 0)

    msg0[...] = spot(0, lower_sq) + spot(1, upper_sq) + spot(2, cross)
    table = exchange(0, msg0, slots0, 1, 4, group16)
    lower_sq, upper_sq, cross = pick(table, 0), pick(table, 1), pick(table, 2)
    w_low, w_up = pair_weights(lower_sq, upper_sq, cross)
    bound = 2.0 * (w_low * w_low * lower_sq + w_up * w_up * upper_sq) + 1e-36
    scale = TOP * lax.rsqrt(bound)
    inverse1 = 1.0 / scale
    w_own = scale * jnp.where(c == 0, w_low, w_up)
    w_oth = scale * jnp.where(c == 0, w_up, w_low)
    msg_g[...] = spot(0, w_own) + spot(1, w_oth)

    def pair_copy(d):
        return pltpu.make_async_remote_copy(
            msg_g,
            slots_g.at[d],
            g_sems.at[0, 5 + d],
            g_sems.at[1, 5 + d],
            device_id=along_x(d),
            device_id_type=MESH,
        )

    for d in (2, 1, 3):
        pair_copy(d).start()
    w_own, w_oth = wide(w_own), wide(w_oth)

    def pair_of(block, r, l):
        own = grads[0, block, r : r + 16, l : l + 128].astype(F32)
        oth = grads[1, block, r : r + 16, l : l + 128].astype(F32)
        return w_own * own + w_oth * oth

    def along_z(d):
        return rank(y, (z + d) % 4, x, c), t

    def x_copy(d, b):
        return pltpu.make_async_remote_copy(
            enc_x.at[d - 1, b],
            recv_x.at[d - 1, b],
            x_send.at[d - 1, b],
            x_recv.at[d - 1, b],
            device_id=along_x(d),
            device_id_type=MESH,
        )

    def zq_copy(dz, yy, dx):
        return pltpu.make_async_remote_copy(
            enc_q.at[dz - 1, yy, dx],
            recv_q.at[dz, yy, dx],
            zq_send.at[dz - 1, yy * 4 + dx],
            zq_recv.at[dz - 1, yy * 4 + dx],
            device_id=along_z(dz),
            device_id_type=MESH,
        )

    def xr_copy(dx, dz, yy):
        return pltpu.make_async_remote_copy(
            recv_q.at[dz, yy, dx],
            recv_r.at[dx - 1, dz, yy],
            xr_send.at[dx - 1, dz * 2 + yy],
            xr_recv.at[dx - 1, dz * 2 + yy],
            device_id=along_x(dx),
            device_id_type=MESH,
        )

    def x_send_block(b):
        for d in (2, 1, 3):
            block = b * 4 + (x + d) % 4
            for r in range(0, BLOCK, 16):
                for l in range(0, PART, 128):
                    enc_x[d - 1, b, r : r + 16, l : l + 128] = encode(pair_of(block, r, l))
            x_copy(d, b).start()

    def q_send_block(yy, dx):
        for dz in (2, 1, 3, 0):
            block = yy * 16 + ((z + dz) % 4) * 4 + (x + dx) % 4
            for r in range(0, BLOCK, 16):
                for l in range(0, COLS - PART, 128):
                    code = encode(pair_of(block, r, PART + l))
                    if dz:
                        enc_q[dz - 1, yy, dx, r : r + 16, l : l + 128] = code
                    else:
                        recv_q[0, yy, dx, r : r + 16, l : l + 128] = code
            if dz:
                zq_copy(dz, yy, dx).start()

    def send_far(m, _):
        x_send_block(1 + m)
        q_send_block(m, 2)
        return _

    def send_near(k, _):
        x_send_block(3 + k)
        q_send_block(k // 2, 1 + 2 * (k % 2))
        return _

    def send_own(m, _):
        q_send_block(m, 0)
        return _

    lax.fori_loop(0, 2, send_far, 0)
    lax.fori_loop(0, 4, send_near, 0)
    x_send_block(7)
    lax.fori_loop(0, 2, send_own, 0)

    def x_own_block(b, _):
        for r in range(0, BLOCK, 16):
            for l in range(0, PART, 128):
                dec_x[x, b, r : r + 16, l : l + 128] = pair_of(b * 4 + x, r, l)
        return _

    lax.fori_loop(0, 8, x_own_block, 0)
    pairs4 = [(i, j) for i in range(4) for j in range(i, 4)]

    def x_products(b, sums):
        sums = list(sums)
        for r in range(0, BLOCK, 8):
            for l in range(0, PART, 128):
                v = [dec_x[i, b, r : r + 8, l : l + 128] for i in range(4)]
                for n, (i, j) in enumerate(pairs4):
                    sums[n] = sums[n] + v[i] * v[j]
        return tuple(sums)

    def x_recv_raw(sums):
        for d in (1, 3, 2):
            raw_copy(0, d).wait_recv()
            raw_copy(1, d).wait_recv()
            pair_copy(d).wait_recv()
            w_first, w_second = wide(pick(slots_g[d], 0)), wide(pick(slots_g[d], 1))
            for r in range(0, BLOCK, 16):
                for l in range(0, PART, 128):
                    first = recv_g[0, d - 1, r : r + 16, l : l + 128].astype(F32)
                    second = recv_g[1, d - 1, r : r + 16, l : l + 128].astype(F32)
                    dec_x[(x + 4 - d) % 4, 0, r : r + 16, l : l + 128] = (
                        w_first * first + w_second * second
                    )
        return x_products(0, sums)

    def x_recv_block(b, sums):
        for d in (1, 3, 2):
            x_copy(d, b).wait_recv()
            source = (x + 4 - d) % 4
            for r in range(0, BLOCK, 16):
                for l in range(0, PART, 256):
                    dec_x[source, b, r : r + 16, l : l + 256] = decode(
                        recv_x[d - 1, b, r : r + 16, l : l + 256]
                    )
        return x_products(b, sums)

    def relay(yy, dx):
        for dz in (0, 1, 3, 2):
            if dz:
                zq_copy(dz, yy, dx).wait_recv()
            xr_copy(dx, dz, yy).start()

    def relay_far(m, _):
        relay(m, 2)
        return _

    def relay_near(k, _):
        relay(k // 2, 1 + 2 * (k % 2))
        return _

    sums = lax.fori_loop(1, 4, x_recv_block, x_recv_raw((zero,) * 10))
    lax.fori_loop(0, 2, relay_far, 0)
    sums = lax.fori_loop(4, 8, x_recv_block, sums)
    lax.fori_loop(0, 4, relay_near, 0)

    def q_decode(dx, yy):
        def one(dz, _):
            if dx:
                xr_copy(dx, dz, yy).wait_recv()
                source = recv_r.at[dx - 1, dz, yy]
            else:
                source = recv_q.at[dz, yy, 0]
            for r in range(0, BLOCK, 16):
                for l in range(0, COLS - PART, 256):
                    dec_q[dz, (x + 4 - dx) % 4, yy, r : r + 16, l : l + 256] = decode(
                        source[r : r + 16, l : l + 256]
                    )
            return _

        lax.fori_loop(0, 4, one, 0)

    def q_own(yy):
        for dz in (1, 2, 3):
            zq_copy(dz, yy, 0).wait_recv()
        q_decode(0, yy)

    def q_gram(yy):
        def one(dz, _):
            sums = [zero if yy == 0 else sums_q[dz, n] for n in range(10)]
            for r in range(0, BLOCK, 8):
                for l in range(0, COLS - PART, 128):
                    v = [dec_q[dz, i, yy, r : r + 8, l : l + 128] for i in range(4)]
                    for n, (i, j) in enumerate(pairs4):
                        sums[n] = sums[n] + v[i] * v[j]
            for n in range(10):
                sums_q[dz, n] = sums[n]
            return _

        lax.fori_loop(0, 4, one, 0)

    q_decode(2, 0)
    q_decode(2, 1)
    q_decode(1, 0)
    q_decode(3, 0)
    q_own(0)
    q_gram(0)
    q_decode(1, 1)
    q_decode(3, 1)
    q_own(1)
    q_gram(1)

    def q_copy(dz):
        return pltpu.make_async_remote_copy(
            msg_q.at[dz],
            slots_q.at[dz],
            q_sems.at[0, dz],
            q_sems.at[1, dz],
            device_id=along_z(4 - dz),
            device_id_type=MESH,
        )

    def tile_of(sums):
        return sum((spot(n, total(s)) for n, s in enumerate(sums[1:], 1)), spot(0, total(sums[0])))

    for dz in (2, 1, 3):
        msg_q[dz] = tile_of([sums_q[dz, n] for n in range(10)])
        q_copy(dz).start()
    table = spot(16 + x, 0.25 * inverse1)
    table = table + tile_of([s + sums_q[0, n] for n, s in enumerate(sums)])
    for dz in (1, 3, 2):
        q_copy(dz).wait_recv()
        table = table + slots_q[dz]
    msg1[...] = table
    table = exchange(1, msg1, slots1, 1, 16, group16)
    inv = [pick(table, 16 + i) for i in range(4)]
    weight, bound = solve4(
        {(i, j): pick(table, n) * inv[i] * inv[j] for n, (i, j) in enumerate(pairs4)}
    )
    scale = TOP * lax.rsqrt(bound)
    inverse3 = 1.0 / scale
    w_own_z = [weight[i] * inv[i] * scale for i in range(4)]

    def w_copy(dz):
        return pltpu.make_async_remote_copy(
            msg_q.at[0],
            slots_w.at[dz],
            q_sems.at[2, dz],
            q_sems.at[3, dz],
            device_id=along_z(dz),
            device_id_type=MESH,
        )

    msg_q[0] = (spot(0, w_own_z[0]) + spot(1, w_own_z[1])) + (
        spot(2, w_own_z[2]) + spot(3, w_own_z[3])
    )
    for dz in (2, 1, 3):
        w_copy(dz).start()
    w_x = [wide(w_own_z[i], 40) for i in range(4)]

    def y_stays(yy, half):
        py = 2 * c + yy
        return (py == y) & (half == c)

    def y_copy(yy, half, zt):
        return pltpu.make_async_remote_copy(
            enc_y.at[yy, half, zt],
            recv_y.at[y, zt],
            y_send.at[yy, half, zt],
            y_recv.at[y, zt],
            device_id=(rank(2 * c + yy, z, x, half), t),
            device_id_type=MESH,
        )

    def combined(weights, block, half, l, width):
        parts = []
        for first in (l, width + l):
            rows, at = slice(40 * half, 40 * half + 40), slice(first, first + 128)
            v = [block(i, rows, at) for i in range(4)]
            parts.append(
                (weights[0] * v[0] + weights[1] * v[1]) + (weights[2] * v[2] + weights[3] * v[3])
            )
        return encode(jnp.concatenate(parts, axis=0))

    def y_send_block(n, _):
        zt = (z + 1 + n // 2) % 4
        yy = n % 2
        b = yy * 4 + zt
        for half in range(2):
            for l in range(0, PART // 2, 128):
                enc_y[yy, half, zt, :, l : l + 128] = combined(
                    w_x, lambda i, r, at: dec_x[i, b, r, at], half, l, PART // 2
                )
            here = y_stays(yy, half)

            @pl.when(here)
            def keep():
                pltpu.make_async_copy(
                    enc_y.at[yy, half, zt], recv_y.at[y, zt], y_recv.at[y, zt]
                ).start()

            @pl.when(jnp.logical_not(here))
            def push():
                y_copy(yy, half, zt).start()

        return _

    lax.fori_loop(0, 8, y_send_block, 0)

    def z_copy(d, sy):
        zt = (z + d) % 4
        return pltpu.make_async_remote_copy(
            recv_y.at[sy, zt],
            recv_z.at[z, sy],
            z_send.at[d - 1, sy],
            z_recv.at[z, sy],
            device_id=(rank(y, zt, x, c), t),
            device_id_type=MESH,
        )

    def y_arrival(sy, zt):
        pltpu.make_async_copy(recv_y.at[sy, zt], recv_y.at[sy, zt], y_recv.at[sy, zt]).wait()

    def z_relay(n, _):
        d = 1 + n // 4
        sy = n % 4
        y_arrival(sy, (z + d) % 4)
        z_copy(d, sy).start()
        return _

    lax.fori_loop(0, 12, z_relay, 0)

    def yq_copy(yy, half):
        return pltpu.make_async_remote_copy(
            enc_yq.at[yy, half],
            recv_yq.at[y],
            yq_send.at[yy, half],
            yq_recv.at[y],
            device_id=(rank(2 * c + yy, z, x, half), t),
            device_id_type=MESH,
        )

    w_by_z = []
    for dz in range(4):
        if dz:
            w_copy(dz).wait_recv()
            w_by_z.append([wide(pick(slots_w[dz], i), 40) for i in range(4)])
        else:
            w_by_z.append(w_x)

    def yq_send_block(yy, _):
        for half in range(2):
            for dz in range(4):
                for l in range(0, (COLS - PART) // 2, 128):
                    enc_yq[yy, half, (z + 4 - dz) % 4, :, l : l + 128] = combined(
                        w_by_z[dz],
                        lambda i, r, at: dec_q[dz, i, yy, r, at],
                        half,
                        l,
                        (COLS - PART) // 2,
                    )
            here = y_stays(yy, half)

            @pl.when(here)
            def keep():
                pltpu.make_async_copy(enc_yq.at[yy, half], recv_yq.at[y], yq_recv.at[y]).start()

            @pl.when(jnp.logical_not(here))
            def push():
                yq_copy(yy, half).start()

        return _

    lax.fori_loop(0, 2, yq_send_block, 0)

    def own_z(sy, _):
        y_arrival(sy, z)
        for r in range(0, BLOCK, 16):
            dec_z[sy * 4 + z, r : r + 16, 0 : PART // 2] = decode(recv_y[sy, z, r : r + 16, :])
        return _

    lax.fori_loop(0, 4, own_z, 0)

    def yq_arrival(n, _):
        sy = (y + n) % 4
        pltpu.make_async_copy(recv_yq.at[sy], recv_yq.at[sy], yq_recv.at[sy]).wait()
        for sz in range(4):
            for r in range(0, BLOCK, 16):
                dec_z[sy * 4 + sz, r : r + 16, PART // 2 :] = decode(recv_yq[sy, sz, r : r + 16, :])
        return _

    lax.fori_loop(0, 4, yq_arrival, 0)

    def group_pairs(a, b):
        return [(i, j) for i in range(4) for j in range(4) if a != b or i <= j]

    def products(a, b, first, last, sums):
        def one(n, sums):
            r = pl.ds(pl.multiple_of(n * 8, 8), 8)
            sums = list(sums)
            for l in range(first, last, 128):
                v = [dec_z[i * 4 + (z + 4 - a) % 4, r, l : l + 128] for i in range(4)]
                w = v if a == b else [dec_z[i * 4 + (z + 4 - b) % 4, r, l : l + 128] for i in range(4)]
                for m, (i, j) in enumerate(group_pairs(a, b)):
                    sums[m] = sums[m] + v[i] * w[j]
            return tuple(sums)

        return lax.fori_loop(0, 10, one, tuple(sums), unroll=5)

    def finish_rows(a, b, sums):
        for (i, j), total_ij in zip(group_pairs(a, b), sums):
            line = jnp.sum(total_ij, axis=0, keepdims=True)
            first, second = i * 4 + (z + 4 - a) % 4, j * 4 + (z + 4 - b) % 4
            rows_s[first, pl.ds(second, 1), :] = line
            rows_s[second, pl.ds(first, 1), :] = line

    blocks = [(a, b) for a in range(4) for b in range(a + 1)]
    for n, (a, b) in enumerate(blocks):
        sums = products(a, b, PART // 2, COLS // 2, [zero] * len(group_pairs(a, b)))
        for m, value in enumerate(sums):
            sums_z[n, m] = value

    def z_arrival(source, sy):
        pltpu.make_async_copy(
            recv_z.at[source, sy], recv_z.at[source, sy], z_recv.at[source, sy]
        ).wait()
        for r in range(0, BLOCK, 16):
            dec_z[sy * 4 + source, r : r + 16, 0 : PART // 2] = decode(
                recv_z[source, sy, r : r + 16, :]
            )

    for a in range(4):
        if a:

            def arrive_z(sy, _):
                z_arrival((z + 4 - a) % 4, sy)
                return _

            lax.fori_loop(0, 4, arrive_z, 0)
        for b in range(a + 1):
            n = blocks.index((a, b))
            before = [sums_z[n, m] for m in range(len(group_pairs(a, b)))]
            finish_rows(a, b, products(a, b, 0, PART // 2, before))
    row16, lane16 = iotas(16)
    gram = jnp.zeros((16, 128), F32)
    for i in range(16):
        gram = gram + jnp.where(lane16 == i, jnp.sum(rows_s[i], axis=1, keepdims=True), 0.0)

    def flat(part):
        line = jnp.where(row16[0:8] == 0, part, 0.0)
        for i in range(1, 8):
            line = line + jnp.where(row16[0:8] == i, pltpu.roll(part, 16 * i, 1), 0.0)
        return jnp.sum(line, axis=0, keepdims=True)

    def square(line):
        full = wide(line, 8)
        part = jnp.where(row16[0:8] == 0, full, 0.0)
        for i in range(1, 8):
            part = part + jnp.where(row16[0:8] == i, pltpu.roll(full, 128 - 16 * i, 1), 0.0)
        return part

    msg2[0:1] = flat(gram[0:8])
    msg2[1:2] = flat(gram[8:16])
    partial = exchange(2, msg2, slots2, 1, 16, group16)
    msg3[0:2] = partial
    msg3[2:4] = wide(spot(4 * y + z, inverse3), 2)
    table = exchange(3, msg3, slots3, 1, 16, plane16)
    inv_row = table[2:3]
    inv_col = jnp.sum(jnp.where(row16 == lane16, inv_row, 0.0), axis=1, keepdims=True)
    gram = jnp.concatenate([square(table[0:1]), square(table[1:2])], axis=0)
    gram = jnp.where(lane16 < 16, gram, 0.0) * inv_row * inv_col
    weight = solve(gram, 16) * inv_col
    w_z = [wide(weight[i : i + 1], 8) for i in range(16)]
    for first, width, at in ((0, PART // 2, 0), (PART, (COLS - PART) // 2, PART // 2)):
        for h in range(2):
            for r in range(0, 40, 8):
                for l in range(0, width, 128):
                    rows, lanes = slice(40 * h + r, 40 * h + r + 8), slice(at + l, at + l + 128)
                    terms = [w_z[i] * dec_z[i, rows, lanes] for i in range(16)]
                    while len(terms) > 1:
                        terms = [p + q for p, q in zip(terms[0::2], terms[1::2])]
                    column = first + h * width + l
                    o_ref[r : r + 8, column : column + 128] = terms[0]

    give_k.wait_send()

    def given(i, _):
        give_a(i).wait_send()
        return _

    lax.fori_loop(0, 4, given, 0)

    def x_done(b, _):
        for d in (1, 2, 3):
            x_copy(d, b).wait_send()
        return _

    lax.fori_loop(1, 8, x_done, 0)
    for d in (1, 2, 3):
        raw_copy(0, d).wait_send()
        raw_copy(1, d).wait_send()
        pair_copy(d).wait_send()

    def zq_done(n, _):
        for dz in (1, 2, 3):
            zq_copy(dz, n // 4, n % 4).wait_send()
        return _

    lax.fori_loop(0, 8, zq_done, 0)

    def xr_done(n, _):
        for dx in (1, 2, 3):
            xr_copy(dx, n // 2, n % 2).wait_send()
        return _

    lax.fori_loop(0, 8, xr_done, 0)
    for dz in (1, 2, 3):
        q_copy(dz).wait_send()
        w_copy(dz).wait_send()

    def yq_done(yy, _):
        for half in range(2):

            @pl.when(jnp.logical_not(y_stays(yy, half)))
            def settle_q():
                yq_copy(yy, half).wait_send()

        return _

    lax.fori_loop(0, 2, yq_done, 0)

    def y_done(n, _):
        for half in range(2):

            @pl.when(jnp.logical_not(y_stays(n % 2, half)))
            def settle():
                y_copy(n % 2, half, n // 2).wait_send()

        return _

    lax.fori_loop(0, 8, y_done, 0)

    def z_done(n, _):
        z_copy(1 + n // 4, n % 4).wait_send()
        return _

    lax.fori_loop(0, 12, z_done, 0)
    finish_exchange(0, slots0, 1, 4)
    finish_exchange(1, slots1, 1, 16)
    finish_exchange(2, slots2, 1, 16)
    finish_exchange(3, slots3, 1, 16)


def body(activations, kv_cotangents):
    tokens = activations.shape[0]
    dma = pltpu.SemaphoreType.DMA
    rest = COLS - PART
    out = pl.pallas_call(
        kernel,
        out_shape=jax.ShapeDtypeStruct((40, COLS), F32),
        in_specs=[pl.BlockSpec(memory_space=pl.ANY)] * 2,
        out_specs=pl.BlockSpec(memory_space=pltpu.VMEM),
        scratch_shapes=[
            pltpu.VMEM((4, tokens, TILE), BF16),
            pltpu.VMEM((4, tokens, TILE), BF16),
            pltpu.VMEM(kv_cotangents.shape, BF16),
            pltpu.VMEM((tokens, COLS), BF16),
            pltpu.VMEM((tokens, COLS), BF16),
            pltpu.VMEM((2, 32, BLOCK, COLS), BF16),
            pltpu.VMEM((2, 3, BLOCK, PART), BF16),
            pltpu.VMEM((1, 128), F32),
            pltpu.VMEM((4, 1, 128), F32),
            pltpu.VMEM((3, 8, BLOCK, PART), BF16),
            pltpu.VMEM((3, 8, BLOCK, PART), BF16),
            pltpu.VMEM((4, 8, BLOCK, PART), F32),
            pltpu.VMEM((3, 2, 4, BLOCK, rest), BF16),
            pltpu.VMEM((4, 2, 4, BLOCK, rest), BF16),
            pltpu.VMEM((3, 4, 2, BLOCK, rest), BF16),
            pltpu.VMEM((4, 4, 2, BLOCK, rest), F32),
            pltpu.VMEM((4, 10, 8, 128), F32),
            pltpu.VMEM((2, 2, 4, BLOCK, PART // 2), BF16),
            pltpu.VMEM((4, 4, BLOCK, PART // 2), BF16),
            pltpu.VMEM((4, 4, BLOCK, PART // 2), BF16),
            pltpu.VMEM((2, 2, 4, BLOCK, rest // 2), BF16),
            pltpu.VMEM((4, 4, BLOCK, rest // 2), BF16),
            pltpu.VMEM((16, BLOCK, COLS // 2), F32),
            pltpu.VMEM((16, 16, 128), F32),
            pltpu.VMEM((10, 16, 8, 128), F32),
            pltpu.VMEM((1, 128), F32),
            pltpu.VMEM((1, 128), F32),
            pltpu.VMEM((2, 128), F32),
            pltpu.VMEM((4, 128), F32),
            pltpu.VMEM((4, 1, 128), F32),
            pltpu.VMEM((4, 1, 128), F32),
            pltpu.VMEM((16, 1, 128), F32),
            pltpu.VMEM((16, 2, 128), F32),
            pltpu.VMEM((16, 4, 128), F32),
            pltpu.VMEM((4, 1, 128), F32),
            pltpu.VMEM((4, 1, 128), F32),
            dma((5,)),
            dma((5,)),
            dma((5,)),
            dma((3, 8)),
            dma((3, 8)),
            dma((3, 8)),
            dma((3, 8)),
            dma((3, 8)),
            dma((3, 8)),
            dma((2, 2)),
            dma((4,)),
            dma((2, 2, 4)),
            dma((4, 4)),
            dma((3, 4)),
            dma((4, 4)),
            dma((4, 16)),
            dma((4, 16)),
            dma((4, 4)),
            dma((2, 9)),
            pltpu.SemaphoreType.REGULAR,
        ],
        compiler_params=pltpu.CompilerParams(
            collective_id=0, has_side_effects=True, vmem_limit_bytes=58 * 2**20
        ),
    )(activations, kv_cotangents)
    return out.reshape(40, kv_cotangents.shape[1], kv_cotangents.shape[2])


def solution(mesh):
    return jax.shard_map(
        body,
        mesh=mesh,
        in_specs=(P("dp", None), P("dp", "tensor", None)),
        out_specs=P("dp", "tensor", None),
        check_vma=False,
    )
```

```python
import functools

import jax
import jax.numpy as jnp
from jax import lax
from jax.experimental import pallas as pl
from jax.experimental.pallas import tpu as pltpu
from jax.sharding import PartitionSpec as P

MESH = pl.DeviceIdType.MESH
F32 = jnp.float32
BF16 = jnp.bfloat16
EPS = 1e-6
POWER = 9
TOP = 2.0**13
HALF = 2560
TILE = 640
BLOCK = 80
COLS = 1024
PART = 512


def coords(dp):
    return dp // 32, (dp // 8) % 4, (dp // 2) % 4, dp % 2


def rank(y, z, x, c):
    return ((y * 4 + z) * 4 + x) * 2 + c


def encode(v):
    v2 = v * v
    v4 = v2 * v2
    return (v4 * v4 * v).astype(BF16)


def decode(code):
    y = code.astype(F32)
    size = jnp.exp2(jnp.log2(jnp.abs(y)) * (1.0 / POWER))
    return jnp.where(y < 0, -size, size)


def iotas(rows):
    shape = (rows, 128)
    return (
        lax.broadcasted_iota(jnp.int32, shape, 0),
        lax.broadcasted_iota(jnp.int32, shape, 1),
    )


def partner_rows(gram, bit):
    rows = gram.shape[0]
    if bit == 8:
        return jnp.concatenate([gram[8:16], gram[0:8]], axis=0)
    parts = []
    for first in range(0, rows, 8):
        part = gram[first : first + 8]
        row = lax.broadcasted_iota(jnp.int32, part.shape, 0)
        parts.append(
            jnp.where((row & bit) == 0, pltpu.roll(part, 8 - bit, 0), pltpu.roll(part, bit, 0))
        )
    return parts[0] if len(parts) == 1 else jnp.concatenate(parts, axis=0)


def partner_lanes(gram, bit):
    lane = lax.broadcasted_iota(jnp.int32, gram.shape, 1)
    return jnp.where((lane & bit) == 0, pltpu.roll(gram, 128 - bit, 1), pltpu.roll(gram, bit, 1))


def solve(gram, count):
    rows = gram.shape[0]
    row, lane = iotas(rows)
    on_diag = row == lane
    weight = jnp.ones((rows, 1), F32)
    bit = 1
    while bit < count:
        paired = (row ^ bit) == lane
        kept = jnp.where(on_diag, gram, 0.0)
        crossed = jnp.where(paired, gram, 0.0)
        col = 1.0 - jnp.sum(crossed, axis=1, keepdims=True) / (
            2.0 * jnp.sum(kept, axis=1, keepdims=True) + EPS
        )
        across = 1.0 - jnp.sum(crossed, axis=0, keepdims=True) / (
            2.0 * jnp.sum(kept, axis=0, keepdims=True) + EPS
        )
        weight = weight * col
        gram = gram * col * across
        if bit * 2 < count:
            gram = gram + partner_rows(gram, bit)
            gram = gram + partner_lanes(gram, bit)
        bit *= 2
    return weight


def total(values):
    return jnp.sum(values, keepdims=True)


def wide(value, rows=16):
    return jnp.broadcast_to(value, (rows, 128))


def fold(values):
    rows, columns = values.shape
    parts = [
        values[r : r + 8, l : l + 128] for r in range(0, rows, 8) for l in range(0, columns, 128)
    ]
    while len(parts) > 1:
        odd = parts[len(parts) & ~1 :]
        parts = [p + q for p, q in zip(parts[0::2], parts[1::2])] + odd
    return parts[0]


def pair_weights(low_sq, up_sq, cross):
    return 1.0 - cross / (2.0 * low_sq + EPS), 1.0 - cross / (2.0 * up_sq + EPS)


def solve4(gram):
    c0, c1 = pair_weights(gram[0, 0], gram[1, 1], gram[0, 1])
    c2, c3 = pair_weights(gram[2, 2], gram[3, 3], gram[2, 3])
    low_sq = c0 * c0 * gram[0, 0] + 2.0 * c0 * c1 * gram[0, 1] + c1 * c1 * gram[1, 1]
    up_sq = c2 * c2 * gram[2, 2] + 2.0 * c2 * c3 * gram[2, 3] + c3 * c3 * gram[3, 3]
    cross = c0 * (c2 * gram[0, 2] + c3 * gram[0, 3]) + c1 * (c2 * gram[1, 2] + c3 * gram[1, 3])
    low, up = pair_weights(low_sq, up_sq, cross)
    weight = [c0 * low, c1 * low, c2 * up, c3 * up]
    bound = sum(weight[i] * weight[i] * gram[i, i] for i in range(4)) * 4.0 + 1e-36
    return weight, bound


def kernel(
    a_hbm, k_hbm, o_ref,
    a_own, a_oth, k_raw, k_own, k_oth, grads, recv_g, msg_g, slots_g, enc_x, recv_x, dec_x, enc_q, recv_q, recv_r, dec_q, sums_q,
    enc_y, recv_y, recv_z, enc_yq, recv_yq, dec_z,
    rows_s, sums_z, msg0, msg1, msg2, msg3, msg_q, slots0, slots1, slots2, slots3, slots_q, slots_w,
    load_sem, tok_send, tok_recv, x_send, x_recv, zq_send, zq_recv, xr_send, xr_recv,
    yq_send, yq_recv, y_send, y_recv, z_send, z_recv, r_send, r_recv, q_sems, g_sems, ready,
):
    me = lax.axis_index("dp")
    t = lax.axis_index("tensor")
    y, z, x, c = coords(me)
    lane1 = lax.broadcasted_iota(jnp.int32, (1, 128), 1)

    def group16(k):
        return rank(y, z, (x + k // 4) % 4, (c + (k // 2) % 2) % 2), (t + k % 2) % 2

    def plane16(k):
        return rank((y + k // 4) % 4, (z + k % 4) % 4, x, c), t

    def a_cols(core, i):
        return pl.ds(pl.multiple_of(core * HALF + i * TILE, 128), TILE)

    load_k = pltpu.make_async_copy(k_hbm, k_raw, load_sem.at[4])
    load_k.start()

    def load_a(i):
        return pltpu.make_async_copy(a_hbm.at[:, a_cols(c, i)], a_own.at[i], load_sem.at[i])

    def start_load(i, _):
        load_a(i).start()
        return _

    lax.fori_loop(0, 4, start_load, 0)

    barrier = pltpu.get_barrier_semaphore()
    other = (rank(y, z, x, 1 - c), t)

    def greet_group(k, _):
        pl.semaphore_signal(
            barrier,
            inc=1,
            device_id=(rank(y, z, (x + k // 2) % 4, 0), (t + k % 2) % 2),
            device_id_type=MESH,
        )
        return _

    def greet_plane(k, _):
        pl.semaphore_signal(
            barrier,
            inc=1,
            device_id=(rank((y + k // 4) % 4, (z + k % 4) % 4, x, 0), t),
            device_id_type=MESH,
        )
        return _

    @pl.when(c == 0)
    def open_pair():
        pl.semaphore_signal(barrier, inc=1, device_id=other, device_id_type=MESH)

    @pl.when(c == 1)
    def answer_pair():
        pl.semaphore_wait(barrier, 1)
        pl.semaphore_signal(ready, inc=1, device_id=other, device_id_type=MESH)

    @pl.when(c == 0)
    def greet_chips():
        pl.semaphore_wait(ready, 1)

    give_k = pltpu.make_async_remote_copy(
        k_own, k_oth, tok_send.at[4], tok_recv.at[4], device_id=other, device_id_type=MESH
    )

    def give_a(i):
        return pltpu.make_async_remote_copy(
            a_hbm.at[:, a_cols(1 - c, i)],
            a_oth.at[i],
            tok_send.at[i],
            tok_recv.at[i],
            device_id=other,
            device_id_type=MESH,
        )

    give_a(0).start()

    @pl.when(c == 0)
    def greet_all():
        lax.fori_loop(1, 8, greet_group, 0)
        lax.fori_loop(1, 16, greet_plane, 0)

    load_k.wait()

    def pack_k(n, _):
        r = pl.ds(pl.multiple_of(n * 32, 32), 32)
        k_own[r] = pltpu.einshape("thc->t(hc)", k_raw[r])
        return _

    lax.fori_loop(0, k_raw.shape[0] // 32, pack_k, 0)
    give_k.start()

    def start_give(i, _):
        give_a(i).start()
        return _

    lax.fori_loop(1, 4, start_give, 0)

    def gradient(a_ref, k_ref):
        return lax.dot_general(
            a_ref[...], k_ref[...], (((0,), (0,)), ((), ())), preferred_element_type=F32
        ).astype(BF16)

    def own_tile(i, own_sq):
        load_a(i).wait()
        tile = gradient(a_own.at[i], k_own)
        grads[0, pl.ds(i * 8, 8)] = tile.reshape(8, BLOCK, COLS)
        tile = tile.astype(F32)
        return own_sq + fold(tile * tile)

    zero = jnp.zeros((8, 128), F32)
    own_sq = lax.fori_loop(0, 4, own_tile, zero)

    @pl.when(c == 0)
    def all_greeted():
        pl.semaphore_wait(barrier, 22)
        pl.semaphore_signal(ready, inc=1, device_id=other, device_id_type=MESH)

    @pl.when(c == 1)
    def told():
        pl.semaphore_wait(ready, 1)

    def along_x(d):
        return rank(y, z, (x + d) % 4, c), t

    def raw_copy(which, d):
        return pltpu.make_async_remote_copy(
            grads.at[which, (x + d) % 4, :, pl.ds(0, PART)],
            recv_g.at[which, d - 1],
            g_sems.at[0, which * 3 + d - 1],
            g_sems.at[1, which * 3 + d - 1],
            device_id=along_x(d),
            device_id_type=MESH,
        )

    for d in (2, 1, 3):
        raw_copy(0, d).start()
    give_k.wait_recv()

    def other_tile(i, sums):
        cross, oth_sq = sums
        give_a(i).wait_recv()
        tile = gradient(a_oth.at[i], k_oth)
        grads[1, pl.ds(i * 8, 8)] = tile.reshape(8, BLOCK, COLS)
        tile = tile.astype(F32)
        own = grads[0, pl.ds(i * 8, 8)].astype(F32).reshape(TILE, COLS)
        return cross + fold(own * tile), oth_sq + fold(tile * tile)

    sums = other_tile(0, (zero, zero))
    for d in (2, 1, 3):
        raw_copy(1, d).start()
    cross, oth_sq = lax.fori_loop(1, 4, other_tile, sums)

    own_sq, oth_sq, cross = total(own_sq), total(oth_sq), total(cross)
    lower_sq = jnp.where(c == 0, own_sq, oth_sq)
    upper_sq = jnp.where(c == 0, oth_sq, own_sq)

    def spot(lane, value):
        return jnp.where(lane1 == lane, value, 0.0)

    def pick(table, lane):
        return total(jnp.where(lane1 == lane, table, 0.0))

    def exchange(stage, msg, slots, first, last, target):
        def go(k, _):
            pltpu.make_async_remote_copy(
                msg,
                slots.at[k],
                r_send.at[stage, k],
                r_recv.at[stage, k],
                device_id=target(k),
                device_id_type=MESH,
            ).start()
            return _

        def arrive(k, table):
            pltpu.make_async_copy(slots.at[k], slots.at[k], r_recv.at[stage, k]).wait()
            return table + slots[k]

        lax.fori_loop(first, last, go, 0)
        return lax.fori_loop(first, last, arrive, msg[...])

    def finish_exchange(stage, slots, first, last):
        def done(k, _):
            pltpu.make_async_copy(slots.at[k], slots.at[k], r_send.at[stage, k]).wait()
            return _

        lax.fori_loop(first, last, done, 0)

    msg0[...] = spot(0, lower_sq) + spot(1, upper_sq) + spot(2, cross)
    table = exchange(0, msg0, slots0, 1, 4, group16)
    lower_sq, upper_sq, cross = pick(table, 0), pick(table, 1), pick(table, 2)
    w_low, w_up = pair_weights(lower_sq, upper_sq, cross)
    bound = 2.0 * (w_low * w_low * lower_sq + w_up * w_up * upper_sq) + 1e-36
    scale = TOP * lax.rsqrt(bound)
    inverse1 = 1.0 / scale
    w_own = scale * jnp.where(c == 0, w_low, w_up)
    w_oth = scale * jnp.where(c == 0, w_up, w_low)
    msg_g[...] = spot(0, w_own) + spot(1, w_oth)

    def pair_copy(d):
        return pltpu.make_async_remote_copy(
            msg_g,
            slots_g.at[d],
            g_sems.at[0, 5 + d],
            g_sems.at[1, 5 + d],
            device_id=along_x(d),
            device_id_type=MESH,
        )

    for d in (2, 1, 3):
        pair_copy(d).start()
    w_own, w_oth = wide(w_own), wide(w_oth)

    def pair_of(block, r, l):
        own = grads[0, block, r : r + 16, l : l + 128].astype(F32)
        oth = grads[1, block, r : r + 16, l : l + 128].astype(F32)
        return w_own * own + w_oth * oth

    def along_z(d):
        return rank(y, (z + d) % 4, x, c), t

    def x_copy(d, b):
        return pltpu.make_async_remote_copy(
            enc_x.at[d - 1, b],
            recv_x.at[d - 1, b],
            x_send.at[d - 1, b],
            x_recv.at[d - 1, b],
            device_id=along_x(d),
            device_id_type=MESH,
        )

    def zq_copy(dz, yy, dx):
        return pltpu.make_async_remote_copy(
            enc_q.at[dz - 1, yy, dx],
            recv_q.at[dz, yy, dx],
            zq_send.at[dz - 1, yy * 4 + dx],
            zq_recv.at[dz - 1, yy * 4 + dx],
            device_id=along_z(dz),
            device_id_type=MESH,
        )

    def xr_copy(dx, dz, yy):
        return pltpu.make_async_remote_copy(
            recv_q.at[dz, yy, dx],
            recv_r.at[dx - 1, dz, yy],
            xr_send.at[dx - 1, dz * 2 + yy],
            xr_recv.at[dx - 1, dz * 2 + yy],
            device_id=along_x(dx),
            device_id_type=MESH,
        )

    def x_send_block(b):
        for d in (2, 1, 3):
            block = b * 4 + (x + d) % 4
            for r in range(0, BLOCK, 16):
                for l in range(0, PART, 128):
                    enc_x[d - 1, b, r : r + 16, l : l + 128] = encode(pair_of(block, r, l))
            x_copy(d, b).start()

    def q_send_block(yy, dx):
        for dz in (2, 1, 3, 0):
            block = yy * 16 + ((z + dz) % 4) * 4 + (x + dx) % 4
            for r in range(0, BLOCK, 16):
                for l in range(0, COLS - PART, 128):
                    code = encode(pair_of(block, r, PART + l))
                    if dz:
                        enc_q[dz - 1, yy, dx, r : r + 16, l : l + 128] = code
                    else:
                        recv_q[0, yy, dx, r : r + 16, l : l + 128] = code
            if dz:
                zq_copy(dz, yy, dx).start()

    def send_far(m, _):
        q_send_block(m, 2)
        x_send_block(1 + m)
        return _

    def send_near(k, _):
        q_send_block(k // 2, 1 + 2 * (k % 2))
        x_send_block(3 + k)
        return _

    def send_own(m, _):
        q_send_block(m, 0)
        return _

    lax.fori_loop(0, 2, send_far, 0)
    lax.fori_loop(0, 4, send_near, 0)
    x_send_block(7)
    lax.fori_loop(0, 2, send_own, 0)

    def x_own_block(b, _):
        for r in range(0, BLOCK, 16):
            for l in range(0, PART, 128):
                dec_x[x, b, r : r + 16, l : l + 128] = pair_of(b * 4 + x, r, l)
        return _

    lax.fori_loop(0, 8, x_own_block, 0)
    pairs4 = [(i, j) for i in range(4) for j in range(i, 4)]

    def x_products(b, sums):
        sums = list(sums)
        for r in range(0, BLOCK, 8):
            for l in range(0, PART, 128):
                v = [dec_x[i, b, r : r + 8, l : l + 128] for i in range(4)]
                for n, (i, j) in enumerate(pairs4):
                    sums[n] = sums[n] + v[i] * v[j]
        return tuple(sums)

    def x_recv_raw(sums):
        for d in (1, 3, 2):
            raw_copy(0, d).wait_recv()
            raw_copy(1, d).wait_recv()
            pair_copy(d).wait_recv()
            w_first, w_second = wide(pick(slots_g[d], 0)), wide(pick(slots_g[d], 1))
            for r in range(0, BLOCK, 16):
                for l in range(0, PART, 128):
                    first = recv_g[0, d - 1, r : r + 16, l : l + 128].astype(F32)
                    second = recv_g[1, d - 1, r : r + 16, l : l + 128].astype(F32)
                    dec_x[(x + 4 - d) % 4, 0, r : r + 16, l : l + 128] = (
                        w_first * first + w_second * second
                    )
        return x_products(0, sums)

    def x_recv_block(b, sums):
        for d in (1, 3, 2):
            x_copy(d, b).wait_recv()
            source = (x + 4 - d) % 4
            for r in range(0, BLOCK, 16):
                for l in range(0, PART, 256):
                    dec_x[source, b, r : r + 16, l : l + 256] = decode(
                        recv_x[d - 1, b, r : r + 16, l : l + 256]
                    )
        return x_products(b, sums)

    def relay(yy, dx):
        for dz in (0, 1, 3, 2):
            if dz:
                zq_copy(dz, yy, dx).wait_recv()
            xr_copy(dx, dz, yy).start()

    def relay_far(m, _):
        relay(m, 2)
        return _

    def relay_near(k, _):
        relay(k // 2, 1 + 2 * (k % 2))
        return _

    sums = lax.fori_loop(1, 4, x_recv_block, x_recv_raw((zero,) * 10))
    lax.fori_loop(0, 2, relay_far, 0)
    sums = lax.fori_loop(4, 8, x_recv_block, sums)
    lax.fori_loop(0, 4, relay_near, 0)

    def q_decode(dx, yy):
        def one(dz, _):
            if dx:
                xr_copy(dx, dz, yy).wait_recv()
                source = recv_r.at[dx - 1, dz, yy]
            else:
                source = recv_q.at[dz, yy, 0]
            for r in range(0, BLOCK, 16):
                for l in range(0, COLS - PART, 256):
                    dec_q[dz, (x + 4 - dx) % 4, yy, r : r + 16, l : l + 256] = decode(
                        source[r : r + 16, l : l + 256]
                    )
            return _

        lax.fori_loop(0, 4, one, 0)

    def q_own(yy):
        for dz in (1, 2, 3):
            zq_copy(dz, yy, 0).wait_recv()
        q_decode(0, yy)

    def q_gram(yy):
        def one(dz, _):
            sums = [zero if yy == 0 else sums_q[dz, n] for n in range(10)]
            for r in range(0, BLOCK, 8):
                for l in range(0, COLS - PART, 128):
                    v = [dec_q[dz, i, yy, r : r + 8, l : l + 128] for i in range(4)]
                    for n, (i, j) in enumerate(pairs4):
                        sums[n] = sums[n] + v[i] * v[j]
            for n in range(10):
                sums_q[dz, n] = sums[n]
            return _

        lax.fori_loop(0, 4, one, 0)

    q_decode(2, 0)
    q_decode(2, 1)
    q_decode(1, 0)
    q_decode(3, 0)
    q_own(0)
    q_gram(0)
    q_decode(1, 1)
    q_decode(3, 1)
    q_own(1)
    q_gram(1)

    def q_copy(dz):
        return pltpu.make_async_remote_copy(
            msg_q.at[dz],
            slots_q.at[dz],
            q_sems.at[0, dz],
            q_sems.at[1, dz],
            device_id=along_z(4 - dz),
            device_id_type=MESH,
        )

    def tile_of(sums):
        return sum((spot(n, total(s)) for n, s in enumerate(sums[1:], 1)), spot(0, total(sums[0])))

    for dz in (2, 1, 3):
        msg_q[dz] = tile_of([sums_q[dz, n] for n in range(10)])
        q_copy(dz).start()
    table = spot(16 + x, 0.25 * inverse1)
    table = table + tile_of([s + sums_q[0, n] for n, s in enumerate(sums)])
    for dz in (1, 3, 2):
        q_copy(dz).wait_recv()
        table = table + slots_q[dz]
    msg1[...] = table
    table = exchange(1, msg1, slots1, 1, 16, group16)
    inv = [pick(table, 16 + i) for i in range(4)]
    weight, bound = solve4(
        {(i, j): pick(table, n) * inv[i] * inv[j] for n, (i, j) in enumerate(pairs4)}
    )
    scale = TOP * lax.rsqrt(bound)
    inverse3 = 1.0 / scale
    w_own_z = [weight[i] * inv[i] * scale for i in range(4)]

    def w_copy(dz):
        return pltpu.make_async_remote_copy(
            msg_q.at[0],
            slots_w.at[dz],
            q_sems.at[2, dz],
            q_sems.at[3, dz],
            device_id=along_z(dz),
            device_id_type=MESH,
        )

    msg_q[0] = (spot(0, w_own_z[0]) + spot(1, w_own_z[1])) + (
        spot(2, w_own_z[2]) + spot(3, w_own_z[3])
    )
    for dz in (2, 1, 3):
        w_copy(dz).start()
    w_x = [wide(w_own_z[i], 40) for i in range(4)]

    def y_stays(yy, half):
        py = 2 * c + yy
        return (py == y) & (half == c)

    def y_copy(yy, half, zt):
        return pltpu.make_async_remote_copy(
            enc_y.at[yy, half, zt],
            recv_y.at[y, zt],
            y_send.at[yy, half, zt],
            y_recv.at[y, zt],
            device_id=(rank(2 * c + yy, z, x, half), t),
            device_id_type=MESH,
        )

    def combined(weights, block, half, l, width):
        parts = []
        for first in (l, width + l):
            rows, at = slice(40 * half, 40 * half + 40), slice(first, first + 128)
            v = [block(i, rows, at) for i in range(4)]
            parts.append(
                (weights[0] * v[0] + weights[1] * v[1]) + (weights[2] * v[2] + weights[3] * v[3])
            )
        return encode(jnp.concatenate(parts, axis=0))

    def y_send_block(n, _):
        zt = (z + 1 + n // 2) % 4
        yy = n % 2
        b = yy * 4 + zt
        for half in range(2):
            for l in range(0, PART // 2, 128):
                enc_y[yy, half, zt, :, l : l + 128] = combined(
                    w_x, lambda i, r, at: dec_x[i, b, r, at], half, l, PART // 2
                )
            here = y_stays(yy, half)

            @pl.when(here)
            def keep():
                pltpu.make_async_copy(
                    enc_y.at[yy, half, zt], recv_y.at[y, zt], y_recv.at[y, zt]
                ).start()

            @pl.when(jnp.logical_not(here))
            def push():
                y_copy(yy, half, zt).start()

        return _

    lax.fori_loop(0, 8, y_send_block, 0)

    def z_copy(d, sy):
        zt = (z + d) % 4
        return pltpu.make_async_remote_copy(
            recv_y.at[sy, zt],
            recv_z.at[z, sy],
            z_send.at[d - 1, sy],
            z_recv.at[z, sy],
            device_id=(rank(y, zt, x, c), t),
            device_id_type=MESH,
        )

    def y_arrival(sy, zt):
        pltpu.make_async_copy(recv_y.at[sy, zt], recv_y.at[sy, zt], y_recv.at[sy, zt]).wait()

    def z_relay(n, _):
        d = 1 + n % 3
        sy = (y + n // 3) % 4
        y_arrival(sy, (z + d) % 4)
        z_copy(d, sy).start()
        return _

    lax.fori_loop(0, 12, z_relay, 0)

    def yq_copy(yy, half):
        return pltpu.make_async_remote_copy(
            enc_yq.at[yy, half],
            recv_yq.at[y],
            yq_send.at[yy, half],
            yq_recv.at[y],
            device_id=(rank(2 * c + yy, z, x, half), t),
            device_id_type=MESH,
        )

    w_by_z = []
    for dz in range(4):
        if dz:
            w_copy(dz).wait_recv()
            w_by_z.append([wide(pick(slots_w[dz], i), 40) for i in range(4)])
        else:
            w_by_z.append(w_x)

    def yq_send_block(yy, _):
        for half in range(2):
            for dz in range(4):
                for l in range(0, (COLS - PART) // 2, 128):
                    enc_yq[yy, half, (z + 4 - dz) % 4, :, l : l + 128] = combined(
                        w_by_z[dz],
                        lambda i, r, at: dec_q[dz, i, yy, r, at],
                        half,
                        l,
                        (COLS - PART) // 2,
                    )
            here = y_stays(yy, half)

            @pl.when(here)
            def keep():
                pltpu.make_async_copy(enc_yq.at[yy, half], recv_yq.at[y], yq_recv.at[y]).start()

            @pl.when(jnp.logical_not(here))
            def push():
                yq_copy(yy, half).start()

        return _

    lax.fori_loop(0, 2, yq_send_block, 0)

    def own_z(sy, _):
        y_arrival(sy, z)
        for r in range(0, BLOCK, 16):
            dec_z[sy * 4 + z, r : r + 16, 0 : PART // 2] = decode(recv_y[sy, z, r : r + 16, :])
        return _

    lax.fori_loop(0, 4, own_z, 0)

    def yq_arrival(n, _):
        sy = (y + n) % 4
        pltpu.make_async_copy(recv_yq.at[sy], recv_yq.at[sy], yq_recv.at[sy]).wait()
        for sz in range(4):
            for r in range(0, BLOCK, 16):
                dec_z[sy * 4 + sz, r : r + 16, PART // 2 :] = decode(recv_yq[sy, sz, r : r + 16, :])
        return _

    lax.fori_loop(0, 4, yq_arrival, 0)

    def group_pairs(a, b):
        return [(i, j) for i in range(4) for j in range(4) if a != b or i <= j]

    def products(a, b, first, last, sums):
        def one(n, sums):
            r = pl.ds(pl.multiple_of(n * 8, 8), 8)
            sums = list(sums)
            for l in range(first, last, 128):
                v = [dec_z[i * 4 + (z + 4 - a) % 4, r, l : l + 128] for i in range(4)]
                w = v if a == b else [dec_z[i * 4 + (z + 4 - b) % 4, r, l : l + 128] for i in range(4)]
                for m, (i, j) in enumerate(group_pairs(a, b)):
                    sums[m] = sums[m] + v[i] * w[j]
            return tuple(sums)

        return lax.fori_loop(0, 10, one, tuple(sums), unroll=5)

    def finish_rows(a, b, sums):
        for (i, j), total_ij in zip(group_pairs(a, b), sums):
            line = jnp.sum(total_ij, axis=0, keepdims=True)
            first, second = i * 4 + (z + 4 - a) % 4, j * 4 + (z + 4 - b) % 4
            rows_s[first, pl.ds(second, 1), :] = line
            rows_s[second, pl.ds(first, 1), :] = line

    blocks = [(a, b) for a in range(4) for b in range(a + 1)]
    for n, (a, b) in enumerate(blocks):
        sums = products(a, b, PART // 2, COLS // 2, [zero] * len(group_pairs(a, b)))
        for m, value in enumerate(sums):
            sums_z[n, m] = value

    def z_arrival(source, sy):
        pltpu.make_async_copy(
            recv_z.at[source, sy], recv_z.at[source, sy], z_recv.at[source, sy]
        ).wait()
        for r in range(0, BLOCK, 16):
            dec_z[sy * 4 + source, r : r + 16, 0 : PART // 2] = decode(
                recv_z[source, sy, r : r + 16, :]
            )

    for a in range(4):
        if a:

            def arrive_z(sy, _):
                z_arrival((z + 4 - a) % 4, sy)
                return _

            lax.fori_loop(0, 4, arrive_z, 0)
        for b in range(a + 1):
            n = blocks.index((a, b))
            before = [sums_z[n, m] for m in range(len(group_pairs(a, b)))]
            finish_rows(a, b, products(a, b, 0, PART // 2, before))
    row16, lane16 = iotas(16)
    gram = jnp.zeros((16, 128), F32)
    for i in range(16):
        gram = gram + jnp.where(lane16 == i, jnp.sum(rows_s[i], axis=1, keepdims=True), 0.0)

    def flat(part):
        line = jnp.where(row16[0:8] == 0, part, 0.0)
        for i in range(1, 8):
            line = line + jnp.where(row16[0:8] == i, pltpu.roll(part, 16 * i, 1), 0.0)
        return jnp.sum(line, axis=0, keepdims=True)

    def square(line):
        full = wide(line, 8)
        part = jnp.where(row16[0:8] == 0, full, 0.0)
        for i in range(1, 8):
            part = part + jnp.where(row16[0:8] == i, pltpu.roll(full, 128 - 16 * i, 1), 0.0)
        return part

    msg2[0:1] = flat(gram[0:8])
    msg2[1:2] = flat(gram[8:16])
    partial = exchange(2, msg2, slots2, 1, 16, group16)
    msg3[0:2] = partial
    msg3[2:4] = wide(spot(4 * y + z, inverse3), 2)
    table = exchange(3, msg3, slots3, 1, 16, plane16)
    inv_row = table[2:3]
    inv_col = jnp.sum(jnp.where(row16 == lane16, inv_row, 0.0), axis=1, keepdims=True)
    gram = jnp.concatenate([square(table[0:1]), square(table[1:2])], axis=0)
    gram = jnp.where(lane16 < 16, gram, 0.0) * inv_row * inv_col
    weight = solve(gram, 16) * inv_col
    w_z = [wide(weight[i : i + 1], 8) for i in range(16)]
    for first, width, at in ((0, PART // 2, 0), (PART, (COLS - PART) // 2, PART // 2)):
        for h in range(2):
            for r in range(0, 40, 8):
                for l in range(0, width, 128):
                    rows, lanes = slice(40 * h + r, 40 * h + r + 8), slice(at + l, at + l + 128)
                    terms = [w_z[i] * dec_z[i, rows, lanes] for i in range(16)]
                    while len(terms) > 1:
                        terms = [p + q for p, q in zip(terms[0::2], terms[1::2])]
                    column = first + h * width + l
                    o_ref[r : r + 8, column : column + 128] = terms[0]

    give_k.wait_send()

    def given(i, _):
        give_a(i).wait_send()
        return _

    lax.fori_loop(0, 4, given, 0)

    def x_done(b, _):
        for d in (1, 2, 3):
            x_copy(d, b).wait_send()
        return _

    lax.fori_loop(1, 8, x_done, 0)
    for d in (1, 2, 3):
        raw_copy(0, d).wait_send()
        raw_copy(1, d).wait_send()
        pair_copy(d).wait_send()

    def zq_done(n, _):
        for dz in (1, 2, 3):
            zq_copy(dz, n // 4, n % 4).wait_send()
        return _

    lax.fori_loop(0, 8, zq_done, 0)

    def xr_done(n, _):
        for dx in (1, 2, 3):
            xr_copy(dx, n // 2, n % 2).wait_send()
        return _

    lax.fori_loop(0, 8, xr_done, 0)
    for dz in (1, 2, 3):
        q_copy(dz).wait_send()
        w_copy(dz).wait_send()

    def yq_done(yy, _):
        for half in range(2):

            @pl.when(jnp.logical_not(y_stays(yy, half)))
            def settle_q():
                yq_copy(yy, half).wait_send()

        return _

    lax.fori_loop(0, 2, yq_done, 0)

    def y_done(n, _):
        for half in range(2):

            @pl.when(jnp.logical_not(y_stays(n % 2, half)))
            def settle():
                y_copy(n % 2, half, n // 2).wait_send()

        return _

    lax.fori_loop(0, 8, y_done, 0)

    def z_done(n, _):
        z_copy(1 + n // 4, n % 4).wait_send()
        return _

    lax.fori_loop(0, 12, z_done, 0)
    finish_exchange(0, slots0, 1, 4)
    finish_exchange(1, slots1, 1, 16)
    finish_exchange(2, slots2, 1, 16)
    finish_exchange(3, slots3, 1, 16)


def body(activations, kv_cotangents):
    tokens = activations.shape[0]
    dma = pltpu.SemaphoreType.DMA
    rest = COLS - PART
    out = pl.pallas_call(
        kernel,
        out_shape=jax.ShapeDtypeStruct((40, COLS), F32),
        in_specs=[pl.BlockSpec(memory_space=pl.ANY)] * 2,
        out_specs=pl.BlockSpec(memory_space=pltpu.VMEM),
        scratch_shapes=[
            pltpu.VMEM((4, tokens, TILE), BF16),
            pltpu.VMEM((4, tokens, TILE), BF16),
            pltpu.VMEM(kv_cotangents.shape, BF16),
            pltpu.VMEM((tokens, COLS), BF16),
            pltpu.VMEM((tokens, COLS), BF16),
            pltpu.VMEM((2, 32, BLOCK, COLS), BF16),
            pltpu.VMEM((2, 3, BLOCK, PART), BF16),
            pltpu.VMEM((1, 128), F32),
            pltpu.VMEM((4, 1, 128), F32),
            pltpu.VMEM((3, 8, BLOCK, PART), BF16),
            pltpu.VMEM((3, 8, BLOCK, PART), BF16),
            pltpu.VMEM((4, 8, BLOCK, PART), F32),
            pltpu.VMEM((3, 2, 4, BLOCK, rest), BF16),
            pltpu.VMEM((4, 2, 4, BLOCK, rest), BF16),
            pltpu.VMEM((3, 4, 2, BLOCK, rest), BF16),
            pltpu.VMEM((4, 4, 2, BLOCK, rest), F32),
            pltpu.VMEM((4, 10, 8, 128), F32),
            pltpu.VMEM((2, 2, 4, BLOCK, PART // 2), BF16),
            pltpu.VMEM((4, 4, BLOCK, PART // 2), BF16),
            pltpu.VMEM((4, 4, BLOCK, PART // 2), BF16),
            pltpu.VMEM((2, 2, 4, BLOCK, rest // 2), BF16),
            pltpu.VMEM((4, 4, BLOCK, rest // 2), BF16),
            pltpu.VMEM((16, BLOCK, COLS // 2), F32),
            pltpu.VMEM((16, 16, 128), F32),
            pltpu.VMEM((10, 16, 8, 128), F32),
            pltpu.VMEM((1, 128), F32),
            pltpu.VMEM((1, 128), F32),
            pltpu.VMEM((2, 128), F32),
            pltpu.VMEM((4, 128), F32),
            pltpu.VMEM((4, 1, 128), F32),
            pltpu.VMEM((4, 1, 128), F32),
            pltpu.VMEM((16, 1, 128), F32),
            pltpu.VMEM((16, 2, 128), F32),
            pltpu.VMEM((16, 4, 128), F32),
            pltpu.VMEM((4, 1, 128), F32),
            pltpu.VMEM((4, 1, 128), F32),
            dma((5,)),
            dma((5,)),
            dma((5,)),
            dma((3, 8)),
            dma((3, 8)),
            dma((3, 8)),
            dma((3, 8)),
            dma((3, 8)),
            dma((3, 8)),
            dma((2, 2)),
            dma((4,)),
            dma((2, 2, 4)),
            dma((4, 4)),
            dma((3, 4)),
            dma((4, 4)),
            dma((4, 16)),
            dma((4, 16)),
            dma((4, 4)),
            dma((2, 9)),
            pltpu.SemaphoreType.REGULAR,
        ],
        compiler_params=pltpu.CompilerParams(
            collective_id=0, has_side_effects=True, vmem_limit_bytes=58 * 2**20
        ),
    )(activations, kv_cotangents)
    return out.reshape(40, kv_cotangents.shape[1], kv_cotangents.shape[2])


def solution(mesh):
    return jax.shard_map(
        body,
        mesh=mesh,
        in_specs=(P("dp", None), P("dp", "tensor", None)),
        out_specs=P("dp", "tensor", None),
        check_vma=False,
    )
```

```python
import functools

import jax
import jax.numpy as jnp
from jax import lax
from jax.experimental import pallas as pl
from jax.experimental.pallas import tpu as pltpu
from jax.sharding import PartitionSpec as P

MESH = pl.DeviceIdType.MESH
F32 = jnp.float32
BF16 = jnp.bfloat16
EPS = 1e-6
POWER = 9
TOP = 2.0**13
HALF = 2560
TILE = 640
BLOCK = 80
COLS = 1024
PART = 512


def coords(dp):
    return dp // 32, (dp // 8) % 4, (dp // 2) % 4, dp % 2


def rank(y, z, x, c):
    return ((y * 4 + z) * 4 + x) * 2 + c


def encode(v):
    v2 = v * v
    v4 = v2 * v2
    return (v4 * v4 * v).astype(BF16)


def decode(code):
    y = code.astype(F32)
    size = jnp.exp2(jnp.log2(jnp.abs(y)) * (1.0 / POWER))
    return jnp.where(y < 0, -size, size)


def iotas(rows):
    shape = (rows, 128)
    return (
        lax.broadcasted_iota(jnp.int32, shape, 0),
        lax.broadcasted_iota(jnp.int32, shape, 1),
    )


def partner_rows(gram, bit):
    rows = gram.shape[0]
    if bit == 8:
        return jnp.concatenate([gram[8:16], gram[0:8]], axis=0)
    parts = []
    for first in range(0, rows, 8):
        part = gram[first : first + 8]
        row = lax.broadcasted_iota(jnp.int32, part.shape, 0)
        parts.append(
            jnp.where((row & bit) == 0, pltpu.roll(part, 8 - bit, 0), pltpu.roll(part, bit, 0))
        )
    return parts[0] if len(parts) == 1 else jnp.concatenate(parts, axis=0)


def partner_lanes(gram, bit):
    lane = lax.broadcasted_iota(jnp.int32, gram.shape, 1)
    return jnp.where((lane & bit) == 0, pltpu.roll(gram, 128 - bit, 1), pltpu.roll(gram, bit, 1))


def solve(gram, count):
    rows = gram.shape[0]
    row, lane = iotas(rows)
    on_diag = row == lane
    weight = jnp.ones((rows, 1), F32)
    bit = 1
    while bit < count:
        paired = (row ^ bit) == lane
        kept = jnp.where(on_diag, gram, 0.0)
        crossed = jnp.where(paired, gram, 0.0)
        col = 1.0 - jnp.sum(crossed, axis=1, keepdims=True) / (
            2.0 * jnp.sum(kept, axis=1, keepdims=True) + EPS
        )
        across = 1.0 - jnp.sum(crossed, axis=0, keepdims=True) / (
            2.0 * jnp.sum(kept, axis=0, keepdims=True) + EPS
        )
        weight = weight * col
        gram = gram * col * across
        if bit * 2 < count:
            gram = gram + partner_rows(gram, bit)
            gram = gram + partner_lanes(gram, bit)
        bit *= 2
    return weight


def total(values):
    return jnp.sum(values, keepdims=True)


def wide(value, rows=16):
    return jnp.broadcast_to(value, (rows, 128))


def fold(values):
    rows, columns = values.shape
    parts = [
        values[r : r + 8, l : l + 128] for r in range(0, rows, 8) for l in range(0, columns, 128)
    ]
    while len(parts) > 1:
        odd = parts[len(parts) & ~1 :]
        parts = [p + q for p, q in zip(parts[0::2], parts[1::2])] + odd
    return parts[0]


def pair_weights(low_sq, up_sq, cross):
    return 1.0 - cross / (2.0 * low_sq + EPS), 1.0 - cross / (2.0 * up_sq + EPS)


def solve4(gram):
    c0, c1 = pair_weights(gram[0, 0], gram[1, 1], gram[0, 1])
    c2, c3 = pair_weights(gram[2, 2], gram[3, 3], gram[2, 3])
    low_sq = c0 * c0 * gram[0, 0] + 2.0 * c0 * c1 * gram[0, 1] + c1 * c1 * gram[1, 1]
    up_sq = c2 * c2 * gram[2, 2] + 2.0 * c2 * c3 * gram[2, 3] + c3 * c3 * gram[3, 3]
    cross = c0 * (c2 * gram[0, 2] + c3 * gram[0, 3]) + c1 * (c2 * gram[1, 2] + c3 * gram[1, 3])
    low, up = pair_weights(low_sq, up_sq, cross)
    weight = [c0 * low, c1 * low, c2 * up, c3 * up]
    bound = sum(weight[i] * weight[i] * gram[i, i] for i in range(4)) * 4.0 + 1e-36
    return weight, bound


def kernel(
    a_hbm, k_hbm, o_ref,
    a_own, a_oth, k_raw, k_own, k_oth, grads, recv_g, msg_g, slots_g, enc_x, recv_x, dec_x, enc_q, recv_q, recv_r, dec_q, sums_q,
    enc_y, recv_y, recv_z, enc_yq, recv_yq, dec_z,
    rows_s, sums_z, msg0, msg1, msg2, msg3, msg_q, slots0, slots1, slots2, slots3, slots_q, slots_w,
    load_sem, tok_send, tok_recv, x_send, x_recv, zq_send, zq_recv, xr_send, xr_recv,
    yq_send, yq_recv, y_send, y_recv, z_send, z_recv, r_send, r_recv, q_sems, g_sems, ready,
):
    me = lax.axis_index("dp")
    t = lax.axis_index("tensor")
    y, z, x, c = coords(me)
    lane1 = lax.broadcasted_iota(jnp.int32, (1, 128), 1)

    def group16(k):
        return rank(y, z, (x + k // 4) % 4, (c + (k // 2) % 2) % 2), (t + k % 2) % 2

    def plane16(k):
        return rank((y + k // 4) % 4, (z + k % 4) % 4, x, c), t

    def a_cols(core, i):
        return pl.ds(pl.multiple_of(core * HALF + i * TILE, 128), TILE)

    load_k = pltpu.make_async_copy(k_hbm, k_raw, load_sem.at[4])
    load_k.start()

    def load_a(i):
        return pltpu.make_async_copy(a_hbm.at[:, a_cols(c, i)], a_own.at[i], load_sem.at[i])

    def start_load(i, _):
        load_a(i).start()
        return _

    lax.fori_loop(0, 4, start_load, 0)

    barrier = pltpu.get_barrier_semaphore()
    other = (rank(y, z, x, 1 - c), t)

    def greet_group(k, _):
        pl.semaphore_signal(
            barrier,
            inc=1,
            device_id=(rank(y, z, (x + k // 2) % 4, 0), (t + k % 2) % 2),
            device_id_type=MESH,
        )
        return _

    def greet_plane(k, _):
        pl.semaphore_signal(
            barrier,
            inc=1,
            device_id=(rank((y + k // 4) % 4, (z + k % 4) % 4, x, 0), t),
            device_id_type=MESH,
        )
        return _

    @pl.when(c == 0)
    def open_pair():
        pl.semaphore_signal(barrier, inc=1, device_id=other, device_id_type=MESH)

    @pl.when(c == 1)
    def answer_pair():
        pl.semaphore_wait(barrier, 1)
        pl.semaphore_signal(ready, inc=1, device_id=other, device_id_type=MESH)

    @pl.when(c == 0)
    def greet_chips():
        pl.semaphore_wait(ready, 1)

    give_k = pltpu.make_async_remote_copy(
        k_own, k_oth, tok_send.at[4], tok_recv.at[4], device_id=other, device_id_type=MESH
    )

    def give_a(i):
        return pltpu.make_async_remote_copy(
            a_hbm.at[:, a_cols(1 - c, i)],
            a_oth.at[i],
            tok_send.at[i],
            tok_recv.at[i],
            device_id=other,
            device_id_type=MESH,
        )

    give_a(0).start()

    @pl.when(c == 0)
    def greet_all():
        lax.fori_loop(1, 8, greet_group, 0)
        lax.fori_loop(1, 16, greet_plane, 0)

    load_k.wait()

    def pack_k(n, _):
        r = pl.ds(pl.multiple_of(n * 32, 32), 32)
        k_own[r] = pltpu.einshape("thc->t(hc)", k_raw[r])
        return _

    lax.fori_loop(0, k_raw.shape[0] // 32, pack_k, 0)
    give_k.start()

    def start_give(i, _):
        give_a(i).start()
        return _

    lax.fori_loop(1, 4, start_give, 0)

    def gradient(a_ref, k_ref):
        return lax.dot_general(
            a_ref[...], k_ref[...], (((0,), (0,)), ((), ())), preferred_element_type=F32
        ).astype(BF16)

    def own_tile(i, own_sq):
        load_a(i).wait()
        tile = gradient(a_own.at[i], k_own)
        grads[0, pl.ds(i * 8, 8)] = tile.reshape(8, BLOCK, COLS)
        tile = tile.astype(F32)
        return own_sq + fold(tile * tile)

    zero = jnp.zeros((8, 128), F32)
    own_sq = lax.fori_loop(0, 4, own_tile, zero)

    @pl.when(c == 0)
    def all_greeted():
        pl.semaphore_wait(barrier, 22)
        pl.semaphore_signal(ready, inc=1, device_id=other, device_id_type=MESH)

    @pl.when(c == 1)
    def told():
        pl.semaphore_wait(ready, 1)

    def along_x(d):
        return rank(y, z, (x + d) % 4, c), t

    def raw_copy(which, d):
        return pltpu.make_async_remote_copy(
            grads.at[which, (x + d) % 4, :, pl.ds(0, PART)],
            recv_g.at[which, d - 1],
            g_sems.at[0, which * 3 + d - 1],
            g_sems.at[1, which * 3 + d - 1],
            device_id=along_x(d),
            device_id_type=MESH,
        )

    for d in (2, 1, 3):
        raw_copy(0, d).start()
    give_k.wait_recv()

    def other_tile(i, sums):
        cross, oth_sq = sums
        give_a(i).wait_recv()
        tile = gradient(a_oth.at[i], k_oth)
        grads[1, pl.ds(i * 8, 8)] = tile.reshape(8, BLOCK, COLS)
        tile = tile.astype(F32)
        own = grads[0, pl.ds(i * 8, 8)].astype(F32).reshape(TILE, COLS)
        return cross + fold(own * tile), oth_sq + fold(tile * tile)

    sums = other_tile(0, (zero, zero))
    for d in (2, 1, 3):
        raw_copy(1, d).start()
    cross, oth_sq = lax.fori_loop(1, 4, other_tile, sums)

    own_sq, oth_sq, cross = total(own_sq), total(oth_sq), total(cross)
    lower_sq = jnp.where(c == 0, own_sq, oth_sq)
    upper_sq = jnp.where(c == 0, oth_sq, own_sq)

    def spot(lane, value):
        return jnp.where(lane1 == lane, value, 0.0)

    def pick(table, lane):
        return total(jnp.where(lane1 == lane, table, 0.0))

    def exchange(stage, msg, slots, first, last, target):
        def go(k, _):
            pltpu.make_async_remote_copy(
                msg,
                slots.at[k],
                r_send.at[stage, k],
                r_recv.at[stage, k],
                device_id=target(k),
                device_id_type=MESH,
            ).start()
            return _

        def arrive(k, table):
            pltpu.make_async_copy(slots.at[k], slots.at[k], r_recv.at[stage, k]).wait()
            return table + slots[k]

        lax.fori_loop(first, last, go, 0)
        return lax.fori_loop(first, last, arrive, msg[...])

    def finish_exchange(stage, slots, first, last):
        def done(k, _):
            pltpu.make_async_copy(slots.at[k], slots.at[k], r_send.at[stage, k]).wait()
            return _

        lax.fori_loop(first, last, done, 0)

    msg0[...] = spot(0, lower_sq) + spot(1, upper_sq) + spot(2, cross)
    table = exchange(0, msg0, slots0, 1, 4, group16)
    lower_sq, upper_sq, cross = pick(table, 0), pick(table, 1), pick(table, 2)
    w_low, w_up = pair_weights(lower_sq, upper_sq, cross)
    bound = 2.0 * (w_low * w_low * lower_sq + w_up * w_up * upper_sq) + 1e-36
    scale = TOP * lax.rsqrt(bound)
    inverse1 = 1.0 / scale
    w_own = scale * jnp.where(c == 0, w_low, w_up)
    w_oth = scale * jnp.where(c == 0, w_up, w_low)
    msg_g[...] = spot(0, w_own) + spot(1, w_oth)

    def pair_copy(d):
        return pltpu.make_async_remote_copy(
            msg_g,
            slots_g.at[d],
            g_sems.at[0, 5 + d],
            g_sems.at[1, 5 + d],
            device_id=along_x(d),
            device_id_type=MESH,
        )

    for d in (2, 1, 3):
        pair_copy(d).start()
    w_own, w_oth = wide(w_own), wide(w_oth)

    def pair_of(block, r, l):
        own = grads[0, block, r : r + 16, l : l + 128].astype(F32)
        oth = grads[1, block, r : r + 16, l : l + 128].astype(F32)
        return w_own * own + w_oth * oth

    def along_z(d):
        return rank(y, (z + d) % 4, x, c), t

    def x_copy(d, b):
        return pltpu.make_async_remote_copy(
            enc_x.at[d - 1, b],
            recv_x.at[d - 1, b],
            x_send.at[d - 1, b],
            x_recv.at[d - 1, b],
            device_id=along_x(d),
            device_id_type=MESH,
        )

    def zq_copy(dz, yy, dx):
        return pltpu.make_async_remote_copy(
            enc_q.at[dz - 1, yy, dx],
            recv_q.at[dz, yy, dx],
            zq_send.at[dz - 1, yy * 4 + dx],
            zq_recv.at[dz - 1, yy * 4 + dx],
            device_id=along_z(dz),
            device_id_type=MESH,
        )

    def xr_copy(dx, dz, yy):
        return pltpu.make_async_remote_copy(
            recv_q.at[dz, yy, dx],
            recv_r.at[dx - 1, dz, yy],
            xr_send.at[dx - 1, dz * 2 + yy],
            xr_recv.at[dx - 1, dz * 2 + yy],
            device_id=along_x(dx),
            device_id_type=MESH,
        )

    def x_send_block(b):
        for d in (2, 1, 3):
            block = b * 4 + (x + d) % 4
            for r in range(0, BLOCK, 16):
                for l in range(0, PART, 128):
                    enc_x[d - 1, b, r : r + 16, l : l + 128] = encode(pair_of(block, r, l))
            x_copy(d, b).start()

    def q_send_block(yy, dx):
        for dz in (2, 1, 3, 0):
            block = yy * 16 + ((z + dz) % 4) * 4 + (x + dx) % 4
            for r in range(0, BLOCK, 16):
                for l in range(0, COLS - PART, 128):
                    code = encode(pair_of(block, r, PART + l))
                    if dz:
                        enc_q[dz - 1, yy, dx, r : r + 16, l : l + 128] = code
                    else:
                        recv_q[0, yy, dx, r : r + 16, l : l + 128] = code
            if dz:
                zq_copy(dz, yy, dx).start()

    def send_far(m, _):
        x_send_block(1 + m)
        q_send_block(m, 2)
        return _

    def send_near(k, _):
        x_send_block(3 + k)
        q_send_block(k // 2, 1 + 2 * (k % 2))
        return _

    def send_own(m, _):
        q_send_block(m, 0)
        return _

    lax.fori_loop(0, 2, send_far, 0)
    lax.fori_loop(0, 4, send_near, 0)
    x_send_block(7)
    lax.fori_loop(0, 2, send_own, 0)

    def x_own_block(b, _):
        for r in range(0, BLOCK, 16):
            for l in range(0, PART, 128):
                dec_x[x, b, r : r + 16, l : l + 128] = pair_of(b * 4 + x, r, l)
        return _

    lax.fori_loop(0, 8, x_own_block, 0)
    pairs4 = [(i, j) for i in range(4) for j in range(i, 4)]

    def x_products(b, sums):
        sums = list(sums)
        for r in range(0, BLOCK, 8):
            for l in range(0, PART, 128):
                v = [dec_x[i, b, r : r + 8, l : l + 128] for i in range(4)]
                for n, (i, j) in enumerate(pairs4):
                    sums[n] = sums[n] + v[i] * v[j]
        return tuple(sums)

    def x_recv_raw(sums):
        for d in (1, 3, 2):
            raw_copy(0, d).wait_recv()
            raw_copy(1, d).wait_recv()
            pair_copy(d).wait_recv()
            w_first, w_second = wide(pick(slots_g[d], 0)), wide(pick(slots_g[d], 1))
            for r in range(0, BLOCK, 16):
                for l in range(0, PART, 128):
                    first = recv_g[0, d - 1, r : r + 16, l : l + 128].astype(F32)
                    second = recv_g[1, d - 1, r : r + 16, l : l + 128].astype(F32)
                    dec_x[(x + 4 - d) % 4, 0, r : r + 16, l : l + 128] = (
                        w_first * first + w_second * second
                    )
        return x_products(0, sums)

    def x_recv_block(b, sums):
        for d in (1, 3, 2):
            x_copy(d, b).wait_recv()
            source = (x + 4 - d) % 4
            for r in range(0, BLOCK, 16):
                for l in range(0, PART, 256):
                    dec_x[source, b, r : r + 16, l : l + 256] = decode(
                        recv_x[d - 1, b, r : r + 16, l : l + 256]
                    )
        return x_products(b, sums)

    def relay(yy, dx):
        for dz in (0, 1, 3, 2):
            if dz:
                zq_copy(dz, yy, dx).wait_recv()
            xr_copy(dx, dz, yy).start()

    def relay_far(m, _):
        relay(m, 2)
        return _

    def relay_near(k, _):
        relay(k // 2, 1 + 2 * (k % 2))
        return _

    sums = lax.fori_loop(1, 4, x_recv_block, x_recv_raw((zero,) * 10))
    lax.fori_loop(0, 2, relay_far, 0)
    sums = lax.fori_loop(4, 8, x_recv_block, sums)
    lax.fori_loop(0, 4, relay_near, 0)

    def q_decode(dx, yy):
        def one(dz, _):
            if dx:
                xr_copy(dx, dz, yy).wait_recv()
                source = recv_r.at[dx - 1, dz, yy]
            else:
                source = recv_q.at[dz, yy, 0]
            for r in range(0, BLOCK, 16):
                for l in range(0, COLS - PART, 256):
                    dec_q[dz, (x + 4 - dx) % 4, yy, r : r + 16, l : l + 256] = decode(
                        source[r : r + 16, l : l + 256]
                    )
            return _

        lax.fori_loop(0, 4, one, 0)

    def q_own(yy):
        for dz in (1, 2, 3):
            zq_copy(dz, yy, 0).wait_recv()
        q_decode(0, yy)

    def q_gram(yy, first, last):
        def one(dz, _):
            sums = [zero if yy == 0 else sums_q[dz, n] for n in range(10)]
            for r in range(0, BLOCK, 8):
                for l in range(0, COLS - PART, 128):
                    v = [dec_q[dz, i, yy, r : r + 8, l : l + 128] for i in range(4)]
                    for n, (i, j) in enumerate(pairs4):
                        sums[n] = sums[n] + v[i] * v[j]
            for n in range(10):
                sums_q[dz, n] = sums[n]
            return _

        lax.fori_loop(first, last, one, 0)

    q_decode(2, 0)
    q_decode(2, 1)
    q_decode(1, 0)
    q_decode(3, 0)
    q_own(0)
    q_gram(0, 0, 4)
    q_decode(1, 1)
    q_decode(3, 1)
    q_own(1)
    q_gram(1, 1, 4)

    def q_copy(dz):
        return pltpu.make_async_remote_copy(
            msg_q.at[dz],
            slots_q.at[dz],
            q_sems.at[0, dz],
            q_sems.at[1, dz],
            device_id=along_z(4 - dz),
            device_id_type=MESH,
        )

    def tile_of(sums):
        return sum((spot(n, total(s)) for n, s in enumerate(sums[1:], 1)), spot(0, total(sums[0])))

    for dz in (2, 1, 3):
        msg_q[dz] = tile_of([sums_q[dz, n] for n in range(10)])
        q_copy(dz).start()
    q_gram(1, 0, 1)
    table = spot(16 + x, 0.25 * inverse1)
    table = table + tile_of([s + sums_q[0, n] for n, s in enumerate(sums)])
    for dz in (1, 3, 2):
        q_copy(dz).wait_recv()
        table = table + slots_q[dz]
    msg1[...] = table
    table = exchange(1, msg1, slots1, 1, 16, group16)
    inv = [pick(table, 16 + i) for i in range(4)]
    weight, bound = solve4(
        {(i, j): pick(table, n) * inv[i] * inv[j] for n, (i, j) in enumerate(pairs4)}
    )
    scale = TOP * lax.rsqrt(bound)
    inverse3 = 1.0 / scale
    w_own_z = [weight[i] * inv[i] * scale for i in range(4)]

    def w_copy(dz):
        return pltpu.make_async_remote_copy(
            msg_q.at[0],
            slots_w.at[dz],
            q_sems.at[2, dz],
            q_sems.at[3, dz],
            device_id=along_z(dz),
            device_id_type=MESH,
        )

    msg_q[0] = (spot(0, w_own_z[0]) + spot(1, w_own_z[1])) + (
        spot(2, w_own_z[2]) + spot(3, w_own_z[3])
    )
    for dz in (2, 1, 3):
        w_copy(dz).start()
    w_x = [wide(w_own_z[i], 40) for i in range(4)]

    def y_stays(yy, half):
        py = 2 * c + yy
        return (py == y) & (half == c)

    def y_copy(yy, half, zt):
        return pltpu.make_async_remote_copy(
            enc_y.at[yy, half, zt],
            recv_y.at[y, zt],
            y_send.at[yy, half, zt],
            y_recv.at[y, zt],
            device_id=(rank(2 * c + yy, z, x, half), t),
            device_id_type=MESH,
        )

    def combined(weights, block, half, l, width):
        parts = []
        for first in (l, width + l):
            rows, at = slice(40 * half, 40 * half + 40), slice(first, first + 128)
            v = [block(i, rows, at) for i in range(4)]
            parts.append(
                (weights[0] * v[0] + weights[1] * v[1]) + (weights[2] * v[2] + weights[3] * v[3])
            )
        return encode(jnp.concatenate(parts, axis=0))

    def y_send_block(n, _):
        zt = (z + 1 + n // 2) % 4
        yy = n % 2
        b = yy * 4 + zt
        for half in range(2):
            for l in range(0, PART // 2, 128):
                enc_y[yy, half, zt, :, l : l + 128] = combined(
                    w_x, lambda i, r, at: dec_x[i, b, r, at], half, l, PART // 2
                )
            here = y_stays(yy, half)

            @pl.when(here)
            def keep():
                pltpu.make_async_copy(
                    enc_y.at[yy, half, zt], recv_y.at[y, zt], y_recv.at[y, zt]
                ).start()

            @pl.when(jnp.logical_not(here))
            def push():
                y_copy(yy, half, zt).start()

        return _

    lax.fori_loop(0, 8, y_send_block, 0)

    def z_copy(d, sy):
        zt = (z + d) % 4
        return pltpu.make_async_remote_copy(
            recv_y.at[sy, zt],
            recv_z.at[z, sy],
            z_send.at[d - 1, sy],
            z_recv.at[z, sy],
            device_id=(rank(y, zt, x, c), t),
            device_id_type=MESH,
        )

    def y_arrival(sy, zt):
        pltpu.make_async_copy(recv_y.at[sy, zt], recv_y.at[sy, zt], y_recv.at[sy, zt]).wait()

    def z_relay(n, _):
        d = 1 + n // 4
        sy = n % 4
        y_arrival(sy, (z + d) % 4)
        z_copy(d, sy).start()
        return _

    lax.fori_loop(0, 12, z_relay, 0)

    def yq_copy(yy, half):
        return pltpu.make_async_remote_copy(
            enc_yq.at[yy, half],
            recv_yq.at[y],
            yq_send.at[yy, half],
            yq_recv.at[y],
            device_id=(rank(2 * c + yy, z, x, half), t),
            device_id_type=MESH,
        )

    w_by_z = []
    for dz in range(4):
        if dz:
            w_copy(dz).wait_recv()
            w_by_z.append([wide(pick(slots_w[dz], i), 40) for i in range(4)])
        else:
            w_by_z.append(w_x)

    def yq_send_block(yy, _):
        for half in range(2):
            for dz in range(4):
                for l in range(0, (COLS - PART) // 2, 128):
                    enc_yq[yy, half, (z + 4 - dz) % 4, :, l : l + 128] = combined(
                        w_by_z[dz],
                        lambda i, r, at: dec_q[dz, i, yy, r, at],
                        half,
                        l,
                        (COLS - PART) // 2,
                    )
            here = y_stays(yy, half)

            @pl.when(here)
            def keep():
                pltpu.make_async_copy(enc_yq.at[yy, half], recv_yq.at[y], yq_recv.at[y]).start()

            @pl.when(jnp.logical_not(here))
            def push():
                yq_copy(yy, half).start()

        return _

    lax.fori_loop(0, 2, yq_send_block, 0)

    def own_z(sy, _):
        y_arrival(sy, z)
        for r in range(0, BLOCK, 16):
            dec_z[sy * 4 + z, r : r + 16, 0 : PART // 2] = decode(recv_y[sy, z, r : r + 16, :])
        return _

    lax.fori_loop(0, 4, own_z, 0)

    def yq_arrival(n, _):
        sy = (y + n) % 4
        pltpu.make_async_copy(recv_yq.at[sy], recv_yq.at[sy], yq_recv.at[sy]).wait()
        for sz in range(4):
            for r in range(0, BLOCK, 16):
                dec_z[sy * 4 + sz, r : r + 16, PART // 2 :] = decode(recv_yq[sy, sz, r : r + 16, :])
        return _

    lax.fori_loop(0, 4, yq_arrival, 0)

    def group_pairs(a, b):
        return [(i, j) for i in range(4) for j in range(4) if a != b or i <= j]

    def products(a, b, first, last, sums):
        def one(n, sums):
            r = pl.ds(pl.multiple_of(n * 8, 8), 8)
            sums = list(sums)
            for l in range(first, last, 128):
                v = [dec_z[i * 4 + (z + 4 - a) % 4, r, l : l + 128] for i in range(4)]
                w = v if a == b else [dec_z[i * 4 + (z + 4 - b) % 4, r, l : l + 128] for i in range(4)]
                for m, (i, j) in enumerate(group_pairs(a, b)):
                    sums[m] = sums[m] + v[i] * w[j]
            return tuple(sums)

        return lax.fori_loop(0, 10, one, tuple(sums), unroll=5)

    def finish_rows(a, b, sums):
        for (i, j), total_ij in zip(group_pairs(a, b), sums):
            line = jnp.sum(total_ij, axis=0, keepdims=True)
            first, second = i * 4 + (z + 4 - a) % 4, j * 4 + (z + 4 - b) % 4
            rows_s[first, pl.ds(second, 1), :] = line
            rows_s[second, pl.ds(first, 1), :] = line

    blocks = [(a, b) for a in range(4) for b in range(a + 1)]
    for n, (a, b) in enumerate(blocks):
        sums = products(a, b, PART // 2, COLS // 2, [zero] * len(group_pairs(a, b)))
        for m, value in enumerate(sums):
            sums_z[n, m] = value

    def z_arrival(source, sy):
        pltpu.make_async_copy(
            recv_z.at[source, sy], recv_z.at[source, sy], z_recv.at[source, sy]
        ).wait()
        for r in range(0, BLOCK, 16):
            dec_z[sy * 4 + source, r : r + 16, 0 : PART // 2] = decode(
                recv_z[source, sy, r : r + 16, :]
            )

    for a in range(4):
        if a:

            def arrive_z(sy, _):
                z_arrival((z + 4 - a) % 4, sy)
                return _

            lax.fori_loop(0, 4, arrive_z, 0)
        for b in range(a + 1):
            n = blocks.index((a, b))
            before = [sums_z[n, m] for m in range(len(group_pairs(a, b)))]
            finish_rows(a, b, products(a, b, 0, PART // 2, before))
    row16, lane16 = iotas(16)
    gram = jnp.zeros((16, 128), F32)
    for i in range(16):
        gram = gram + jnp.where(lane16 == i, jnp.sum(rows_s[i], axis=1, keepdims=True), 0.0)

    def flat(part):
        line = jnp.where(row16[0:8] == 0, part, 0.0)
        for i in range(1, 8):
            line = line + jnp.where(row16[0:8] == i, pltpu.roll(part, 16 * i, 1), 0.0)
        return jnp.sum(line, axis=0, keepdims=True)

    def square(line):
        full = wide(line, 8)
        part = jnp.where(row16[0:8] == 0, full, 0.0)
        for i in range(1, 8):
            part = part + jnp.where(row16[0:8] == i, pltpu.roll(full, 128 - 16 * i, 1), 0.0)
        return part

    msg2[0:1] = flat(gram[0:8])
    msg2[1:2] = flat(gram[8:16])
    partial = exchange(2, msg2, slots2, 1, 16, group16)
    msg3[0:2] = partial
    msg3[2:4] = wide(spot(4 * y + z, inverse3), 2)
    table = exchange(3, msg3, slots3, 1, 16, plane16)
    inv_row = table[2:3]
    inv_col = jnp.sum(jnp.where(row16 == lane16, inv_row, 0.0), axis=1, keepdims=True)
    gram = jnp.concatenate([square(table[0:1]), square(table[1:2])], axis=0)
    gram = jnp.where(lane16 < 16, gram, 0.0) * inv_row * inv_col
    weight = solve(gram, 16) * inv_col
    w_z = [wide(weight[i : i + 1], 8) for i in range(16)]
    for first, width, at in ((0, PART // 2, 0), (PART, (COLS - PART) // 2, PART // 2)):
        for h in range(2):
            for r in range(0, 40, 8):
                for l in range(0, width, 128):
                    rows, lanes = slice(40 * h + r, 40 * h + r + 8), slice(at + l, at + l + 128)
                    terms = [w_z[i] * dec_z[i, rows, lanes] for i in range(16)]
                    while len(terms) > 1:
                        terms = [p + q for p, q in zip(terms[0::2], terms[1::2])]
                    column = first + h * width + l
                    o_ref[r : r + 8, column : column + 128] = terms[0]

    give_k.wait_send()

    def given(i, _):
        give_a(i).wait_send()
        return _

    lax.fori_loop(0, 4, given, 0)

    def x_done(b, _):
        for d in (1, 2, 3):
            x_copy(d, b).wait_send()
        return _

    lax.fori_loop(1, 8, x_done, 0)
    for d in (1, 2, 3):
        raw_copy(0, d).wait_send()
        raw_copy(1, d).wait_send()
        pair_copy(d).wait_send()

    def zq_done(n, _):
        for dz in (1, 2, 3):
            zq_copy(dz, n // 4, n % 4).wait_send()
        return _

    lax.fori_loop(0, 8, zq_done, 0)

    def xr_done(n, _):
        for dx in (1, 2, 3):
            xr_copy(dx, n // 2, n % 2).wait_send()
        return _

    lax.fori_loop(0, 8, xr_done, 0)
    for dz in (1, 2, 3):
        q_copy(dz).wait_send()
        w_copy(dz).wait_send()

    def yq_done(yy, _):
        for half in range(2):

            @pl.when(jnp.logical_not(y_stays(yy, half)))
            def settle_q():
                yq_copy(yy, half).wait_send()

        return _

    lax.fori_loop(0, 2, yq_done, 0)

    def y_done(n, _):
        for half in range(2):

            @pl.when(jnp.logical_not(y_stays(n % 2, half)))
            def settle():
                y_copy(n % 2, half, n // 2).wait_send()

        return _

    lax.fori_loop(0, 8, y_done, 0)

    def z_done(n, _):
        z_copy(1 + n // 4, n % 4).wait_send()
        return _

    lax.fori_loop(0, 12, z_done, 0)
    finish_exchange(0, slots0, 1, 4)
    finish_exchange(1, slots1, 1, 16)
    finish_exchange(2, slots2, 1, 16)
    finish_exchange(3, slots3, 1, 16)


def body(activations, kv_cotangents):
    tokens = activations.shape[0]
    dma = pltpu.SemaphoreType.DMA
    rest = COLS - PART
    out = pl.pallas_call(
        kernel,
        out_shape=jax.ShapeDtypeStruct((40, COLS), F32),
        in_specs=[pl.BlockSpec(memory_space=pl.ANY)] * 2,
        out_specs=pl.BlockSpec(memory_space=pltpu.VMEM),
        scratch_shapes=[
            pltpu.VMEM((4, tokens, TILE), BF16),
            pltpu.VMEM((4, tokens, TILE), BF16),
            pltpu.VMEM(kv_cotangents.shape, BF16),
            pltpu.VMEM((tokens, COLS), BF16),
            pltpu.VMEM((tokens, COLS), BF16),
            pltpu.VMEM((2, 32, BLOCK, COLS), BF16),
            pltpu.VMEM((2, 3, BLOCK, PART), BF16),
            pltpu.VMEM((1, 128), F32),
            pltpu.VMEM((4, 1, 128), F32),
            pltpu.VMEM((3, 8, BLOCK, PART), BF16),
            pltpu.VMEM((3, 8, BLOCK, PART), BF16),
            pltpu.VMEM((4, 8, BLOCK, PART), F32),
            pltpu.VMEM((3, 2, 4, BLOCK, rest), BF16),
            pltpu.VMEM((4, 2, 4, BLOCK, rest), BF16),
            pltpu.VMEM((3, 4, 2, BLOCK, rest), BF16),
            pltpu.VMEM((4, 4, 2, BLOCK, rest), F32),
            pltpu.VMEM((4, 10, 8, 128), F32),
            pltpu.VMEM((2, 2, 4, BLOCK, PART // 2), BF16),
            pltpu.VMEM((4, 4, BLOCK, PART // 2), BF16),
            pltpu.VMEM((4, 4, BLOCK, PART // 2), BF16),
            pltpu.VMEM((2, 2, 4, BLOCK, rest // 2), BF16),
            pltpu.VMEM((4, 4, BLOCK, rest // 2), BF16),
            pltpu.VMEM((16, BLOCK, COLS // 2), F32),
            pltpu.VMEM((16, 16, 128), F32),
            pltpu.VMEM((10, 16, 8, 128), F32),
            pltpu.VMEM((1, 128), F32),
            pltpu.VMEM((1, 128), F32),
            pltpu.VMEM((2, 128), F32),
            pltpu.VMEM((4, 128), F32),
            pltpu.VMEM((4, 1, 128), F32),
            pltpu.VMEM((4, 1, 128), F32),
            pltpu.VMEM((16, 1, 128), F32),
            pltpu.VMEM((16, 2, 128), F32),
            pltpu.VMEM((16, 4, 128), F32),
            pltpu.VMEM((4, 1, 128), F32),
            pltpu.VMEM((4, 1, 128), F32),
            dma((5,)),
            dma((5,)),
            dma((5,)),
            dma((3, 8)),
            dma((3, 8)),
            dma((3, 8)),
            dma((3, 8)),
            dma((3, 8)),
            dma((3, 8)),
            dma((2, 2)),
            dma((4,)),
            dma((2, 2, 4)),
            dma((4, 4)),
            dma((3, 4)),
            dma((4, 4)),
            dma((4, 16)),
            dma((4, 16)),
            dma((4, 4)),
            dma((2, 9)),
            pltpu.SemaphoreType.REGULAR,
        ],
        compiler_params=pltpu.CompilerParams(
            collective_id=0, has_side_effects=True, vmem_limit_bytes=58 * 2**20
        ),
    )(activations, kv_cotangents)
    return out.reshape(40, kv_cotangents.shape[1], kv_cotangents.shape[2])


def solution(mesh):
    return jax.shard_map(
        body,
        mesh=mesh,
        in_specs=(P("dp", None), P("dp", "tensor", None)),
        out_specs=P("dp", "tensor", None),
        check_vma=False,
    )
```
